32 devices in a mesh: section: 4 (over y, x), sp: 8 (over z, core).
Axes of the slice: x: 2, y: 2, z: 4, core: 2. Of those that a mesh axis runs over, the one named last changes fastest.
Arguments:
- images: bfloat16 [32, 32, 32, 128], P('section', 'sp'), may hold values from -6 to 6
- labels: int32 [32, 1], P('section'), may hold values from 0 to 9
- chain_steps: int32 [32, 1], P(('section', 'sp')), may hold values from 20 to 60
- conv_weights: float32 [589824], P(('section', 'sp')), may hold values from -0.1875 to 0.1875
- class_affine: float32 [10240], P(('section', 'sp')), may hold values from -1.2 to 1.6, as said below
- power_vectors: float32 [4, 128], replicated, may hold values from -6 to 6
- cotangent: bfloat16 [32, 16, 16, 128], P(('section', 'sp')), may hold values from -6 to 6
Outputs:
- energy_features: float32 [32, 16, 16, 128], P(('section', 'sp'))
- input_grad: float32 [32, 32, 32, 128], P('section', 'sp')
- weight_grad: float32 [589824], P(('section', 'sp'))
- affine_grad: float32 [10240], P(('section', 'sp'))
The draws below stay inside these ranges and needn't reach their ends.
Inputs may be any that keep to these rules, and one draw needn't show every extreme that they name: `class_affine`: the first 5120 entries are gains, the rest biases.
All inputs are finite; a program needn't handle non-finite values.
Results may differ from the reference program's by a relative error of at most 0.0059.
Values may be sent and summed in bfloat16 or wider, within the bound.
A program may use at most 128 MiB of HBM per device.

```python
import jax
import jax.numpy as jnp
from jax import lax

CHANNELS = 128
CLASSES = 10
SIDE = 32
LANGEVIN_T = 40
ACROSS = 1
MBATCH = 32
HALF = 16


def draw_class_affine(key, part):
    key = jax.random.fold_in(key, 7)
    total = 8 * CLASSES * CHANNELS
    first, second = jax.random.split(key)
    position = jnp.arange(total)
    is_gain = position < 4 * CLASSES * CHANNELS
    gains = 1.0 + jax.random.uniform(first, (total,), jnp.float32, -0.5, 0.5)
    biases = jnp.clip(0.3 * jax.random.normal(second, (total,), jnp.float32), -1.2, 1.2)
    return jnp.where(is_gain, gains, biases).astype(jnp.float32)


def touch_ends(values, stream_key, low, top_value):
    index_at = [jax.random.randint(jax.random.fold_in(stream_key, axis), (), 0, length) for axis, length in enumerate(values.shape)]
    main_axis = values.shape.index(max(values.shape))
    next_to = index_at[:main_axis] + [(index_at[main_axis] + 1) % values.shape[main_axis]] + index_at[main_axis + 1:]
    return values.at[tuple(index_at)].set(low).at[tuple(next_to)].set(top_value)


def levels(stream_key, extent, pieces, low, largest):
    gain, own = 1.0, jax.random.fold_in(stream_key, 6)
    for dim, shards_of in pieces:
        heights = jnp.exp(jax.random.uniform(jax.random.fold_in(own, dim), (shards_of,), jnp.float32, low / len(pieces), largest / len(pieces)))
        gain = gain * jnp.repeat(heights, extent[dim] // shards_of).reshape([-1 if axis == dim else 1 for axis in range(len(extent))])
    return gain


def bell_draw(stream_key, shape, deviation, limit, cuts=(), kind=jnp.bfloat16):
    values = deviation * jax.random.normal(stream_key, shape, jnp.float32)
    if cuts:
        values = values * levels(stream_key, shape, cuts, -0.22, 0.18)
    return jnp.clip(values, -limit, limit).astype(kind)


def setup_inputs(seed: int = 0) -> dict:
    splits = jax.random.split(jax.random.key(seed), 8)
    images = bell_draw(splits[0], (MBATCH, ACROSS * SIDE, SIDE, CHANNELS), 1.0, 6.0, ((0, 4), (1, 8)))
    labels = touch_ends(jax.random.randint(splits[1], (MBATCH, ACROSS), 0, CLASSES), jax.random.fold_in(splits[1], 1), 0, CLASSES - 1).astype(jnp.int32)
    chain_steps = touch_ends(jax.random.randint(splits[2], (MBATCH, ACROSS), 20, 61), jax.random.fold_in(splits[2], 1), 20, 60).astype(jnp.int32)
    conv_weights = bell_draw(splits[3], (36 * CHANNELS * CHANNELS,), (9 * CHANNELS) ** -0.5, 0.1875, ((0, 32),), jnp.float32)
    class_affine = draw_class_affine(jax.random.fold_in(splits[7], 71), 0)
    power_vectors = bell_draw(splits[5], (4, CHANNELS), 1.0, 6.0, (), jnp.float32)
    cotangent = bell_draw(splits[6], (MBATCH, ACROSS * HALF, HALF, CHANNELS), 1.0, 6.0, ((0, 32),))
    return dict(images=images, labels=labels, chain_steps=chain_steps, conv_weights=conv_weights, class_affine=class_affine, power_vectors=power_vectors, cotangent=cotangent)


@jax.custom_vjp
def low(v):
    return lax.optimization_barrier(v.astype(jnp.bfloat16)).astype(jnp.float32)

@jax.custom_vjp
def low_back(v):
    return v

def low_keep(v):
    return (low(v), None)

def low_pass(kept, grad):
    return (grad,)

def back_keep(v):
    return (v, None)

def back_low(kept, grad):
    return (low(grad),)
low.defvjp(low_keep, low_pass)
low_back.defvjp(back_keep, back_low)

def leaky(value):
    return 0.2 * value + 0.8 * jax.nn.softplus(value)

def spectral(matrix, vector):
    forward = jnp.dot(matrix, vector, precision=lax.Precision.HIGHEST)
    unit = forward / jnp.sqrt(jnp.sum(forward * forward) + 1e-06)
    backward = jnp.dot(unit, matrix, precision=lax.Precision.HIGHEST)
    return jnp.sqrt(jnp.sum(backward * backward) + 1e-06)

def convolve(pictures, kernel):
    return lax.conv_general_dilated(pictures, kernel, (1, 1), 'SAME', dimension_numbers=('NHWC', 'HWIO', 'NHWC'), precision=lax.Precision.HIGHEST)

def branch(pictures, kernels, sigmas, gains, biases, first):
    value = pictures
    for index in (first, first + 1):
        raw = low_back(convolve(value, kernels[index]))
        value = leaky(raw / sigmas[index] * gains[index][:, None, None, :] + biases[index][:, None, None, :])
        if index == first:
            value = low(value)
    return pictures + value

def forward(pictures, weights, affine, vectors, onehot, active):
    kernels = low(weights).reshape(4, 3, 3, CHANNELS, CHANNELS)
    table = low(affine).reshape(2, 4, CLASSES, CHANNELS)
    picked = jnp.einsum('nk,wjkc->wjnc', onehot, table, precision=lax.Precision.HIGHEST)
    matrices = kernels.reshape(4, 9 * CHANNELS, CHANNELS)
    sigmas = [spectral(matrices[j], vectors[j]) for j in range(4)]
    first_out = branch(pictures, kernels, sigmas, picked[0], picked[1], 0)
    second_out = branch(low_back(low(first_out)), kernels, sigmas, picked[0], picked[1], 2)
    pooled = lax.optimization_barrier(jnp.mean(second_out.reshape(-1, HALF, 2, HALF, 2, CHANNELS), axis=(2, 4)))
    return pooled * active[:, None, None, None]

def reference(images, labels, chain_steps, conv_weights, class_affine, power_vectors, cotangent):
    inputs = images.astype(jnp.float32).reshape(MBATCH, ACROSS, SIDE, SIDE, CHANNELS)
    cot_blocks = cotangent.astype(jnp.float32).reshape(MBATCH, ACROSS, HALF, HALF, CHANNELS)
    classes = jnp.arange(CLASSES, dtype=jnp.int32)

    def step(carry, item):
        block, tags, counts, cot_block = item
        onehot = (tags[:, None] == classes[None, :]).astype(jnp.float32)
        active = (counts > LANGEVIN_T).astype(jnp.float32)

        def local(pictures, weights, affine):
            return forward(pictures, weights, affine, power_vectors, onehot, active)
        result, pullback = jax.vjp(local, block, conv_weights, class_affine)
        grad_x, grad_w, grad_a = pullback(cot_block)
        return ((carry[0] + grad_w, carry[1] + grad_a), (result, grad_x))
    start = (jnp.zeros_like(conv_weights), jnp.zeros_like(class_affine))
    (weight_grad, affine_grad), (results, grads_x) = lax.scan(step, start, (inputs, labels, chain_steps, cot_blocks))
    energy_features = results.reshape(MBATCH, ACROSS * HALF, HALF, CHANNELS)
    input_grad = grads_x.reshape(MBATCH, ACROSS * SIDE, SIDE, CHANNELS)
    return (energy_features, input_grad, weight_grad, affine_grad)
```

```python
from functools import partial

import jax
import jax.numpy as jnp
from jax import lax
from jax.experimental import pallas as pl
from jax.experimental.pallas import tpu as pltpu
from jax.sharding import PartitionSpec as P

LANGEVIN_T = 40


HIGHEST = lax.Precision.HIGHEST


def extended_2(block, sides, width):
    for axis, dim in sides:
        count = lax.axis_size(axis)
        forward = [(i, i + 1) for i in range(count - 1)]
        backward = [(target, source) for source, target in forward]
        low = lax.ppermute(
            lax.slice_in_dim(block, block.shape[dim] - width, None, axis=dim), axis, forward
        )
        high = lax.ppermute(lax.slice_in_dim(block, 0, width, axis=dim), axis, backward)
        block = jnp.concatenate([low, block, high], axis=dim)
    return block


def leaky(value):
    return 0.2 * value + 0.8 * jax.nn.softplus(value)


def leaky_slope(value):
    return 0.2 + 0.8 * jax.nn.sigmoid(value)


def spectral(matrix, vector):
    forward = jnp.dot(matrix, vector, precision=HIGHEST)
    unit = forward / jnp.sqrt(jnp.sum(forward * forward) + 1e-06)
    backward = jnp.dot(unit, matrix, precision=HIGHEST)
    return jnp.sqrt(jnp.sum(backward * backward) + 1e-06)


def taps(padded, kernel):
    return lax.conv_general_dilated(
        padded,
        kernel,
        (1, 1),
        "VALID",
        dimension_numbers=("NHWC", "HWIO", "NHWC"),
        preferred_element_type=jnp.float32,
    )


def kernel_grad(padded, grad):
    result = lax.conv_general_dilated(
        padded,
        grad,
        (1, 1),
        "VALID",
        dimension_numbers=("CHWN", "IHWO", "NHWC"),
        preferred_element_type=jnp.float32,
    )
    return jnp.transpose(result, (1, 2, 0, 3))


def flipped(kernel):
    return jnp.transpose(jnp.flip(kernel, (0, 1)), (0, 1, 3, 2))


def trim_rims(extended, band, side):
    start = lax.axis_index("sp") * band
    keep_top = jnp.where(start % side == 0, 0.0, 1.0).astype(extended.dtype)
    keep_bottom = jnp.where((start + band) % side == 0, 0.0, 1.0).astype(extended.dtype)
    merged = jnp.concatenate(
        [extended[:, :1] * keep_top, extended[:, 1:-1], extended[:, -1:] * keep_bottom], axis=1
    )
    return jnp.pad(merged, ((0, 0), (0, 0), (1, 1), (0, 0)))


def rows_forward(values, band, side):
    extended = extended_2(values, (("sp", 1),), 1)
    return trim_rims(extended, band, side)


def rows_backward(values, band, side):
    extended = extended_2(values, (("sp", 1),), 1)
    return trim_rims(extended, band, side)


def pad_whole(values):
    return jnp.pad(values, ((0, 0), (1, 1), (1, 1), (0, 0)))


def affine_terms(upstream, raw, value, scale, gain, sigma):
    pre = upstream * leaky_slope(value)
    grad_raw = (pre * scale[:, None, None, :]).astype(jnp.bfloat16)
    grad_gain = jnp.sum(pre * raw, axis=(1, 2)) / sigma
    grad_bias = jnp.sum(pre, axis=(1, 2))
    grad_sigma = -jnp.sum(grad_gain * gain) / sigma
    return (grad_raw, grad_gain, grad_bias, grad_sigma)


def general_body(images, labels, chain_steps, conv_weights, class_affine, power_vectors, cotangent):
    channels = images.shape[3]
    band = images.shape[1]
    side = images.shape[2]
    half = side // 2
    across = labels.shape[1]
    groups = chain_steps.shape[0]
    gathered_w, gathered_a = (
        lax.all_gather(conv_weights.astype(jnp.bfloat16), ("section", "sp"), axis=0, tiled=True),
        lax.all_gather(class_affine.astype(jnp.bfloat16), ("section", "sp"), axis=0, tiled=True),
    )
    kernels = gathered_w.reshape(4, 3, 3, channels, channels)
    table = gathered_a.astype(jnp.float32).reshape(2, 4, -1, channels)
    count = table.shape[2]
    matrices = kernels.astype(jnp.float32).reshape(4, 9 * channels, channels)
    sigmas = [spectral(matrices[j], power_vectors[j]) for j in range(4)]
    kinds = jnp.arange(count)
    start = lax.axis_index("sp") * groups
    tags_second = lax.dynamic_slice_in_dim(labels, start, groups, 0).reshape(-1)
    onehot_second = (tags_second[:, None] == kinds[None, :]).astype(jnp.float32)
    active = (chain_steps.reshape(-1) > LANGEVIN_T).astype(jnp.float32)
    column = lax.axis_index("sp") * band // side
    picks = jnp.arange(across) == column
    tags_first = jnp.sum(jnp.where(picks[None, :], labels, 0), axis=1)
    onehot_first = (tags_first[:, None] == kinds[None, :]).astype(jnp.float32)
    pad_forward = partial(rows_forward, band=band, side=side)
    pad_backward = partial(rows_backward, band=band, side=side)
    gains_first = jnp.einsum("nk,jkc->jnc", onehot_first, table[0], precision=HIGHEST)
    biases_first = jnp.einsum("nk,jkc->jnc", onehot_first, table[1], precision=HIGHEST)
    gains_second = jnp.einsum("nk,jkc->jnc", onehot_second, table[0], precision=HIGHEST)
    biases_second = jnp.einsum("nk,jkc->jnc", onehot_second, table[1], precision=HIGHEST)
    scales = [
        gains_first[0] / sigmas[0],
        gains_first[1] / sigmas[1],
        gains_second[2] / sigmas[2],
        gains_second[3] / sigmas[3],
    ]
    input_pad = pad_forward(images)
    raw_zero = taps(input_pad, kernels[0])
    pre_zero = raw_zero * scales[0][:, None, None, :] + biases_first[0][:, None, None, :]
    hidden_zero = leaky(pre_zero).astype(jnp.bfloat16)
    hidden_pad = pad_forward(hidden_zero)
    raw_one = taps(hidden_pad, kernels[1])
    pre_one = raw_one * scales[1][:, None, None, :] + biases_first[1][:, None, None, :]
    first_out = images.astype(jnp.float32) + leaky(pre_one)
    moved = lax.all_to_all(
        first_out.astype(jnp.bfloat16), "sp", split_axis=0, concat_axis=1, tiled=True
    )
    whole = moved.reshape(groups * across, side, side, channels)
    whole_pad = pad_whole(whole)
    raw_two = taps(whole_pad, kernels[2])
    pre_two = raw_two * scales[2][:, None, None, :] + biases_second[2][:, None, None, :]
    hidden_two = leaky(pre_two).astype(jnp.bfloat16)
    hidden_two_pad = pad_whole(hidden_two)
    raw_three = taps(hidden_two_pad, kernels[3])
    pre_three = raw_three * scales[3][:, None, None, :] + biases_second[3][:, None, None, :]
    second_out = whole.astype(jnp.float32) + leaky(pre_three)
    pooled = (
        jnp.mean(second_out.reshape(-1, half, 2, half, 2, channels), axis=(2, 4))
        * active[:, None, None, None]
    )
    energy = pooled.reshape(groups, across * half, half, channels)
    upstream = (
        cotangent.astype(jnp.float32).reshape(-1, half, half, channels)
        * (0.25 * active)[:, None, None, None]
    )
    images_n = upstream.shape[0]
    grad_out = jnp.broadcast_to(
        upstream[:, :, None, :, None, :], (images_n, half, 2, half, 2, channels)
    ).reshape(images_n, side, side, channels)
    dz_three, dg_three, db_three, dsig_three = affine_terms(
        grad_out, raw_three, pre_three, scales[3], gains_second[3], sigmas[3]
    )
    kg_three = kernel_grad(hidden_two_pad, dz_three)
    grad_hidden = taps(pad_whole(dz_three), flipped(kernels[3]))
    dz_two, dg_two, db_two, dsig_two = affine_terms(
        grad_hidden, raw_two, pre_two, scales[2], gains_second[2], sigmas[2]
    )
    kg_two = kernel_grad(whole_pad, dz_two)
    grad_whole = grad_out + taps(pad_whole(dz_two), flipped(kernels[2]))
    back_rows = grad_whole.astype(jnp.bfloat16).reshape(groups, across * side, side, channels)
    returned = lax.all_to_all(back_rows, "sp", split_axis=1, concat_axis=0, tiled=True)
    grad_first = returned.astype(jnp.float32)
    dz_one, dg_one, db_one, dsig_one = affine_terms(
        grad_first, raw_one, pre_one, scales[1], gains_first[1], sigmas[1]
    )
    kg_one = kernel_grad(hidden_pad, dz_one)
    grad_hidden_first = taps(pad_backward(dz_one), flipped(kernels[1]))
    dz_zero, dg_zero, db_zero, dsig_zero = affine_terms(
        grad_hidden_first, raw_zero, pre_zero, scales[0], gains_first[0], sigmas[0]
    )
    kg_zero = kernel_grad(input_pad, dz_zero)
    local_grad = grad_first + taps(pad_backward(dz_zero), flipped(kernels[0]))
    conv_grads = [kg_zero, kg_one, kg_two, kg_three]
    sigma_grads = [dsig_zero, dsig_one, dsig_two, dsig_three]
    pieces = []
    for index in range(4):
        unused, pullback = jax.vjp(partial(spectral, vector=power_vectors[index]), matrices[index])
        pieces.append(
            conv_grads[index].reshape(9 * channels, channels) + pullback(sigma_grads[index])[0]
        )
    weight_total = jnp.stack(pieces).reshape(-1)
    gain_rows = [
        jnp.einsum("nk,nc->kc", onehot_first, dg_zero, precision=HIGHEST),
        jnp.einsum("nk,nc->kc", onehot_first, dg_one, precision=HIGHEST),
        jnp.einsum("nk,nc->kc", onehot_second, dg_two, precision=HIGHEST),
        jnp.einsum("nk,nc->kc", onehot_second, dg_three, precision=HIGHEST),
    ]
    bias_rows = [
        jnp.einsum("nk,nc->kc", onehot_first, db_zero, precision=HIGHEST),
        jnp.einsum("nk,nc->kc", onehot_first, db_one, precision=HIGHEST),
        jnp.einsum("nk,nc->kc", onehot_second, db_two, precision=HIGHEST),
        jnp.einsum("nk,nc->kc", onehot_second, db_three, precision=HIGHEST),
    ]
    affine_total = jnp.stack([jnp.stack(gain_rows), jnp.stack(bias_rows)]).reshape(-1)
    weight_grad, affine_grad = (
        lax.psum_scatter(weight_total, ("section", "sp"), scatter_dimension=0, tiled=True),
        lax.psum_scatter(affine_total, ("section", "sp"), scatter_dimension=0, tiled=True),
    )
    return (energy, local_grad, weight_grad, affine_grad)

F32 = jnp.float32
BF16 = jnp.bfloat16
MESH = pl.DeviceIdType.MESH
NN = (((1,), (0,)), ((), ()))
NT = (((1,), (1,)), ((), ()))
TN = (((0,), (0,)), ((), ()))
KERNELS = 4
TILE = 16


def dot(left, right, dims, precision=None):
    return lax.dot_general(left, right, dims, precision=precision, preferred_element_type=F32)


def twice(row):
    return jnp.concatenate([row, row], 1)


def beside(value, side):
    rows = value.shape[0]
    column = lax.broadcasted_iota(jnp.int32, (rows, 1), 0) % side
    left = jnp.where(column == 0, 0.0, pltpu.roll(value, 1, 0))
    right = jnp.where(column == side - 1, 0.0, pltpu.roll(value, rows - 1, 0))
    return (left, value, right)


def put_patches(ref, pair, value, side, ch):
    count = value.shape[0] // side
    rows = slice(pair + 1, pair + 1 + count)
    for b, part in enumerate(beside(value, side)):
        part = part.astype(BF16)
        for e in range(2):
            half = part[:, e * ch : (e + 1) * ch].reshape(count, side, ch)
            ref[rows, e, :, b * ch : (b + 1) * ch] = half


def patch_rows(ref, count):
    side, width = ref.shape[2], ref.shape[3]
    parts = [ref[0:count, 1], ref[1 : count + 1, 0], ref[1 : count + 1, 1], ref[2 : count + 2, 0]]
    return jnp.concatenate(parts, -1).reshape(count * side, 4 * width)


def pair_weights(kernel):
    rows = kernel.shape[0] // 3
    zero = jnp.zeros((rows, kernel.shape[1]), kernel.dtype)
    a, b, c = (kernel[i * rows : (i + 1) * rows] for i in range(3))
    pairs = ((a, zero), (b, a), (c, b), (zero, c))
    return jnp.concatenate([jnp.concatenate(pair, 1) for pair in pairs], 0)


def pair_weights_back(kernel):
    ch = kernel.shape[1]
    zero = jnp.zeros((ch, ch), kernel.dtype)
    blocks = []
    for e in range(2):
        row = []
        for r in range(4):
            for b in range(3):
                a = 2 - (r - e)
                tap = (a * 3 + 2 - b) * ch
                row.append(kernel[tap : tap + ch] if 0 <= a <= 2 else zero)
        blocks.append(jnp.concatenate(row, 1))
    return jnp.concatenate(blocks, 0)


def leaky_terms(value):
    small = jnp.exp(-jnp.abs(value))
    result = 0.2 * value + 0.8 * (jnp.maximum(value, 0.0) + jnp.log(1.0 + small))
    return result, 0.6 + 0.4 * jnp.tanh(0.5 * value)


def halves(pairs, ch):
    wide = jnp.concatenate([pairs[:, 0], pairs[:, 1]], -1)
    return wide.reshape(-1, 2 * ch)


def three(row):
    high = row.astype(BF16).astype(F32)
    middle = (row - high).astype(BF16).astype(F32)
    return (high, middle, row - high - middle)


def whole_kernel(
    nsec, nz, count, active_above,
    images, labels, steps, weights, affine, vectors, cotangent,
    energy, returned, weight_out, table_out,
    pieces, xin, patches, grads, raws, slopes, up_rows, pool_rows, rows_ref,
    dk, first, summed, second, total, third, back, tiles, tables, tables_in,
    piece_in, piece_z, piece_s, piece_c, image_out, image_in, local,
    one_out, one_in, two_out, two_in, three_out, three_in, back_out, back_in,
    tile_out, tile_in, table_out_sem, table_in_sem,
):
    nsp = 2 * nz
    side, ch = images.shape[2], images.shape[3]
    band = images.shape[1]
    half = side // 2
    rows = weights.shape[0]
    s = lax.axis_index("section")
    p = lax.axis_index("sp")
    z = p // 2
    c = p % 2

    def sec(d):
        return jnp.bitwise_xor(s, d)

    def zed(d):
        return jnp.bitwise_xor(z, d)

    def remote(src, dst, out_sem, in_sem, where):
        return pltpu.make_async_remote_copy(
            src_ref=src, dst_ref=dst, send_sem=out_sem, recv_sem=in_sem,
            device_id=where, device_id_type=MESH,
        )

    sibling = (s, p + 1 - 2 * c)

    def at_section(d):
        return (sec(d), p)

    def at_z(d):
        return (s, 2 * zed(d) + c)

    def at_sp(d):
        return (s, jnp.bitwise_xor(p, d))

    barrier = pltpu.get_barrier_semaphore()
    for d in range(1, nsec):
        pl.semaphore_signal(barrier, inc=1, device_id=at_section(d), device_id_type=MESH)
    for d in range(1, nsp):
        pl.semaphore_signal(barrier, inc=1, device_id=at_sp(d), device_id_type=MESH)

    own_image = pltpu.make_async_copy(images.at[p], xin.at[p], local.at[0])
    own_image.start()

    mine = weights[...].astype(BF16)
    pieces[s, z, c, 0:rows] = mine
    matrix = mine.astype(F32)
    vector = vectors[pl.ds(s, 1)]
    proj = jnp.sum(matrix * vector, axis=1, keepdims=True)
    crossed = jnp.sum(proj * matrix, axis=0, keepdims=True)
    norm = jnp.broadcast_to(jnp.sum(proj * proj, axis=0, keepdims=True), (1, ch))
    flat = affine[...].astype(BF16).astype(F32)
    hollow = jnp.zeros((1, ch // 2), F32)
    even = [flat[:, 0:ch], flat[:, ch : 2 * ch], jnp.concatenate([flat[:, 2 * ch :], hollow], 1)]
    odd = [
        jnp.concatenate([hollow, flat[:, 0 : ch // 2]], 1),
        flat[:, ch // 2 : 3 * ch // 2],
        flat[:, 3 * ch // 2 :],
    ]
    is_odd = jnp.full((1, ch), c, jnp.int32) == 1
    lines = [jnp.where(is_odd, b, a) for a, b in zip(even, odd)] + [*three(crossed), *three(norm)]
    tile = jnp.zeros((TILE, ch), F32)
    line = lax.broadcasted_iota(jnp.int32, (TILE, ch), 0)
    for index, value in enumerate(lines):
        tile = jnp.where(line == index, value, tile)
    pieces[s, z, c, rows : rows + TILE] = tile.astype(BF16)

    patches[:, 0:1] = jnp.zeros_like(patches[:, 0:1])
    patches[:, half + 1 :] = jnp.zeros_like(patches[:, half + 1 :])
    grads[0:1] = jnp.zeros_like(grads[0:1])
    grads[half + 1 :] = jnp.zeros_like(grads[half + 1 :])

    pl.semaphore_wait(barrier, nsec - 1 + nsp - 1)

    def piece_copy(a, b, e, out_sem, where):
        ref = pieces.at[a, b, e]
        return remote(ref, ref, out_sem, piece_in.at[a, b, e], where)

    sends = []

    def send(copy):
        copy.start()
        sends.append(copy)

    for d in range(1, nz):
        send(piece_copy(s, z, c, piece_z.at[d - 1], at_z(d)))
    for d in range(1, nsec):
        send(piece_copy(s, z, c, piece_s.at[0, d - 1], at_section(d)))
    send(piece_copy(s, z, c, piece_c.at[0, 0], sibling))
    for d in range(1, nsp):
        q = jnp.bitwise_xor(p, d)
        send(remote(images.at[q], xin.at[p], image_out.at[d - 1], image_in.at[p], at_sp(d)))

    own_image.wait()
    active = jnp.where(steps[...] > active_above, 1.0, 0.0)
    pulled = cotangent[...].astype(F32).reshape(half * half, ch) * (0.25 * active)
    up_rows[pl.ds(0, half * half, stride=2), :] = pulled
    up_rows[pl.ds(1, half * half, stride=2), :] = pulled

    for d in range(1, nz):
        piece_copy(s, zed(d), c, piece_z.at[d - 1], sibling).wait_recv()
        for e in range(1, nsec):
            send(piece_copy(s, zed(d), c, piece_s.at[d, e - 1], at_section(e)))
        send(piece_copy(s, zed(d), c, piece_c.at[0, d], sibling))

    per = band // 2
    for d in range(1, nsp):
        q = jnp.bitwise_xor(p, d)
        remote(images.at[q], xin.at[q], image_out.at[d - 1], image_in.at[q], sibling).wait_recv()
    for q in range(nsp):
        block = xin[q].astype(F32).reshape(per, 2, side, ch)
        put_patches(patches.at[0], q * per, halves(block, ch), side, ch)

    for d in range(1, nsec):
        for e in range(nz):
            piece_copy(sec(d), zed(e), c, piece_c.at[d, e], sibling).wait_recv()
            send(piece_copy(sec(d), zed(e), c, piece_c.at[d, e], sibling))
    for a in range(nsec):
        for b in range(nz):
            piece_copy(a, b, 1 - c, piece_c.at[a, b], sibling).wait_recv()

    label = labels[pl.ds(p, 1)]
    width = nsec * nsp * TILE
    column = lax.broadcasted_iota(jnp.int32, (TILE, width), 1)
    picked = lax.broadcasted_iota(jnp.int32, (TILE, width), 0)
    device = jnp.right_shift(column, 4)
    entry = jnp.bitwise_and(column, TILE - 1)
    wanted = picked * count + label
    at_row = jnp.right_shift(device * 5, 1) + entry
    section = jnp.right_shift(column, (nsp * TILE).bit_length() - 1)
    chosen = (picked < 8) & (entry < 3) & (at_row == wanted)
    chosen |= (picked >= 8) & (picked < 12) & (section == picked - 8) & (entry >= 3) & (entry < 6)
    chosen |= (picked >= 12) & (section == picked - 12) & (entry >= 6) & (entry < 9)
    everything = pieces[:, :, :, rows : rows + TILE].reshape(width, ch)
    rows_ref[...] = dot(jnp.where(chosen, 1.0, 0.0).astype(BF16), everything, NN)
    gains, biases = rows_ref[0:4], rows_ref[4:8]
    lengths = jnp.sqrt(rows_ref[12:16] + 1e-06)
    units = rows_ref[8:12] / lengths
    sigmas = jnp.sqrt(jnp.sum(units * units, axis=1, keepdims=True) + 1e-06)
    scales = gains / sigmas

    def kernel_of(j):
        parts = [pieces[j, b, e, 0:rows] for b in range(nz) for e in range(2)]
        return jnp.concatenate(parts, 0)

    chunks = 8
    step = half // chunks
    spans = [(i * step, pl.ds(i * step * side, step * side)) for i in range(chunks)]

    for j in range(KERNELS):
        raws[j] = dot(patch_rows(patches.at[j], half), pair_weights(kernel_of(j)), NN)
        scale, bias = twice(scales[j : j + 1]), twice(biases[j : j + 1])
        for pair, span in spans:
            value, slope = leaky_terms(raws[j, span] * scale + bias)
            slopes[j, span] = slope
            if j % 2 == 1:
                source = patches[j - 1, pair + 1 : pair + 1 + step, :, :, ch : 2 * ch]
                value = halves(source.astype(F32), ch) + value
            if j < KERNELS - 1:
                put_patches(patches.at[j + 1], pair, value, side, ch)
            else:
                pool_rows[span] = value[:, :ch] + value[:, ch:]
    pooled = pool_rows[pl.ds(0, half * half, stride=2), :] + pool_rows[pl.ds(1, half * half, stride=2), :]
    energy[...] = (pooled * (0.25 * active)).reshape(half, half, ch)

    def first_sum(j):
        remote(dk.at[j, :, 1 - c], first.at[j], one_out.at[j], one_in.at[j], sibling).wait_recv()
        summed[j] = (dk[j, :, c].astype(F32) + first[j].astype(F32)).astype(BF16)
        for d in range(1, nz):
            send(remote(summed.at[j, zed(d)], second.at[j, d - 1], two_out.at[j, d - 1], two_in.at[j, d - 1], at_z(d)))

    def second_sum(j):
        value = summed[j, z].astype(F32)
        for d in range(1, nz):
            remote(summed.at[j, zed(d)], second.at[j, d - 1], two_out.at[j, d - 1], two_in.at[j, d - 1], at_z(d)).wait_recv()
            value += second[j, d - 1].astype(F32)
        total[j] = value.astype(BF16)

        @pl.when(s != j)
        def _():
            third_copy(j).start()

    def third_copy(j):
        d = jnp.maximum(jnp.bitwise_xor(s, j) - 1, 0)
        return remote(total.at[j], third.at[d], three_out.at[j], three_in.at[d], (j, p))

    lines = []
    for j in reversed(range(KERNELS)):
        scale = twice(scales[j : j + 1])
        gain_sum = jnp.zeros((1, 2 * ch), F32)
        bias_sum = jnp.zeros((1, 2 * ch), F32)
        for pair, span in spans:
            upstream = twice(up_rows[span]) if j == KERNELS - 1 else slopes[j + 1, span]
            pre = upstream * slopes[j, span]
            gain_sum += jnp.sum(pre * raws[j, span], axis=0, keepdims=True)
            bias_sum += jnp.sum(pre, axis=0, keepdims=True)
            put_patches(grads, pair, pre * scale, side, ch)
        sigma = sigmas[j : j + 1]
        gain_row = (gain_sum[:, :ch] + gain_sum[:, ch:]) / sigma
        lines.append((j, gain_row))
        lines.append((4 + j, bias_sum[:, :ch] + bias_sum[:, ch:]))
        lines.append((8 + j, -gain_row * gains[j : j + 1] / sigma))
        inputs = patches[j, 1 : half + 1].reshape(2 * half * side, 3 * ch)
        centre = grads[...].reshape(2 * half + 4, side, 3 * ch)[:, :, ch : 2 * ch]
        shifted = [centre[3 - a : 3 - a + 2 * half] for a in range(3)]
        shifted = jnp.concatenate(shifted, -1).reshape(2 * half * side, 3 * ch)
        grad = dot(inputs, shifted, TN)
        grad = jnp.concatenate([grad[:, a * ch : (a + 1) * ch] for a in range(3)], 0).astype(BF16)
        for b in range(nz):
            for e in range(2):
                at = (2 * b + e) * rows
                dk[j, b, e] = grad[at : at + rows]
        send(remote(dk.at[j, :, 1 - c], first.at[j], one_out.at[j], one_in.at[j], sibling))
        down = dot(patch_rows(grads, half), pair_weights_back(kernel_of(j)), NT)
        if j == 2:
            down = (down + twice(up_rows[...])).astype(BF16).astype(F32)
            raws[2] = down
        if j > 0:
            slopes[j] = down
        else:
            down = (down + raws[2]).astype(BF16)
            for q in range(nsp):
                for e in range(2):
                    part = down[q * per * side : (q + 1) * per * side, e * ch : (e + 1) * ch]
                    back[q, :, e] = part.reshape(per, side, ch)
        if j > 0:
            first_sum(j)

    own_back = pltpu.make_async_copy(back.at[p], returned.at[p], local.at[1])
    own_back.start()
    for d in range(1, nsp):
        q = jnp.bitwise_xor(p, d)
        send(remote(back.at[q], returned.at[p], back_out.at[d - 1], back_in.at[p], at_sp(d)))
    first_sum(0)

    tile = jnp.zeros((TILE, ch), F32)
    for index, value in lines:
        tile = jnp.where(line == index, value, tile)
    tiles[p] = tile
    for d in range(1, nsp):
        send(remote(tiles.at[p], tiles.at[p], tile_out.at[d - 1], tile_in.at[p], at_sp(d)))
    for j in (3, 2, 1):
        second_sum(j)
    for d in range(1, nsp):
        q = jnp.bitwise_xor(p, d)
        remote(tiles.at[q], tiles.at[q], tile_out.at[d - 1], tile_in.at[q], sibling).wait_recv()
    spread = nsp * TILE
    column = lax.broadcasted_iota(jnp.int32, (24, spread), 1)
    row = lax.broadcasted_iota(jnp.int32, (24, spread), 0)
    entry = jnp.bitwise_and(column, TILE - 1)
    owner = jnp.right_shift(column, 4)
    tag = jnp.zeros((24, spread), jnp.int32)
    for q in range(nsp):
        tag = jnp.where(owner == q, labels[q : q + 1], tag)
    gathered = tiles[...].reshape(spread, ch)
    upper = row >= count
    kind = row - jnp.where(upper, count, 0)
    for blk in range(nsec):
        slot = 2 * blk + jnp.where(upper, 1, 0)
        chosen = (row < 2 * count) & (entry == slot) & (tag == kind)
        chosen |= (row >= 2 * count) & (entry == 8 + row - 2 * count)
        tables[blk] = dot(jnp.where(chosen, 1.0, 0.0), gathered, NN, HIGHEST)
    for d in range(1, nsec):
        send(remote(tables.at[sec(d)], tables_in.at[d - 1], table_out_sem.at[d - 1], table_in_sem.at[d - 1], at_section(d)))
    second_sum(0)
    table = tables[s]
    for d in range(1, nsec):
        remote(tables.at[sec(d)], tables_in.at[d - 1], table_out_sem.at[d - 1], table_in_sem.at[d - 1], at_section(d)).wait_recv()
        table += tables_in[d - 1]
    table_out[...] = table

    mine = pieces[s, z, c, 0:rows].astype(F32)
    proj = jnp.sum(mine * vector, axis=1, keepdims=True)
    q_row = rows_ref[pl.ds(8 + s, 1)]
    length = jnp.sqrt(rows_ref[pl.ds(12 + s, 1)][:, 0:1] + 1e-06)
    unit = q_row / length
    sigma = jnp.sqrt(jnp.sum(unit * unit, axis=1, keepdims=True) + 1e-06)
    along = unit / sigma
    reach = jnp.sum(mine * along, axis=1, keepdims=True)
    crossing = jnp.sum(q_row * along, axis=1, keepdims=True)
    slope = (reach - proj * (crossing / (length * length))) / length
    dsigma = table_out[pl.ds(2 * count + s, 1)]
    dsigma = jnp.sum(dsigma, axis=1, keepdims=True)
    value = total[s].astype(F32) + dsigma * ((proj / length) * along + slope * vector)
    for d in range(1, nsec):
        remote(total.at[0], third.at[d - 1], three_out.at[0], three_in.at[d - 1], sibling).wait_recv()
        value += third[d - 1].astype(F32)
    weight_out[...] = value

    for d in range(1, nsp):
        q = jnp.bitwise_xor(p, d)
        remote(back.at[q], returned.at[q], back_out.at[d - 1], back_in.at[q], sibling).wait_recv()
    own_back.wait()
    for copy in sends:
        copy.wait_send()
    for j in range(KERNELS):

        @pl.when(s != j)
        def _():
            third_copy(j).wait_send()


def whole_body(images, labels, chain_steps, conv_weights, class_affine, power_vectors, cotangent):
    nsec, nsp = lax.axis_size("section"), lax.axis_size("sp")
    nz = nsp // 2
    own, band, side, ch = images.shape
    half = side // 2
    rows = conv_weights.shape[0] // ch
    count = class_affine.shape[0] * nsec * nsp // (2 * KERNELS * ch)
    vmem = pl.BlockSpec(memory_space=pltpu.VMEM)
    anywhere = pl.BlockSpec(memory_space=pl.ANY)
    pixels = half * side
    dma = pltpu.SemaphoreType.DMA
    energy, returned, weight_grad, table = pl.pallas_call(
        partial(whole_kernel, nsec, nz, count, LANGEVIN_T),
        out_shape=[
            jax.ShapeDtypeStruct((half, half, ch), F32),
            jax.ShapeDtypeStruct((own, band // 2, 2, side, ch), BF16),
            jax.ShapeDtypeStruct((rows, ch), F32),
            jax.ShapeDtypeStruct((24, ch), F32),
        ],
        in_specs=[anywhere, vmem, vmem, vmem, vmem, vmem, vmem],
        out_specs=[vmem, anywhere, vmem, vmem],
        scratch_shapes=[
            pltpu.VMEM((nsec, nz, 2, rows + TILE, ch), BF16),
            pltpu.VMEM((nsp, band, side, ch), BF16),
            pltpu.VMEM((KERNELS, half + 2, 2, side, 3 * ch), BF16),
            pltpu.VMEM((half + 2, 2, side, 3 * ch), BF16),
            pltpu.VMEM((KERNELS, pixels, 2 * ch), F32),
            pltpu.VMEM((KERNELS, pixels, 2 * ch), F32),
            pltpu.VMEM((pixels, ch), F32),
            pltpu.VMEM((pixels, ch), F32),
            pltpu.VMEM((TILE, ch), F32),
            pltpu.VMEM((KERNELS, nz, 2, rows, ch), BF16),
            pltpu.VMEM((KERNELS, nz, rows, ch), BF16),
            pltpu.VMEM((KERNELS, nz, rows, ch), BF16),
            pltpu.VMEM((KERNELS, nz - 1, rows, ch), BF16),
            pltpu.VMEM((KERNELS, rows, ch), BF16),
            pltpu.VMEM((nsec - 1, rows, ch), BF16),
            pltpu.VMEM((nsp, band // 2, 2, side, ch), BF16),
            pltpu.VMEM((nsp, TILE, ch), F32),
            pltpu.VMEM((nsec, 24, ch), F32),
            pltpu.VMEM((nsec - 1, 24, ch), F32),
            dma((nsec, nz, 2)),
            dma((nz - 1,)),
            dma((nz, nsec - 1)),
            dma((nsec, nz)),
            dma((nsp - 1,)),
            dma((nsp,)),
            dma((2,)),
            dma((KERNELS,)),
            dma((KERNELS,)),
            dma((KERNELS, nz - 1)),
            dma((KERNELS, nz - 1)),
            dma((KERNELS,)),
            dma((nsec - 1,)),
            dma((nsp - 1,)),
            dma((nsp,)),
            dma((nsp - 1,)),
            dma((nsp,)),
            dma((nsec - 1,)),
            dma((nsec - 1,)),
        ],
        compiler_params=pltpu.CompilerParams(
            collective_id=0, has_side_effects=True, vmem_limit_bytes=56 * 2**20
        ),
    )(
        images,
        labels,
        chain_steps,
        conv_weights.reshape(rows, ch),
        class_affine.reshape(1, -1),
        power_vectors,
        cotangent.reshape(half, half, ch),
    )
    share = class_affine.shape[0]
    affine_grad = lax.dynamic_slice_in_dim(
        table[: 2 * count].reshape(-1), lax.axis_index("sp") * share, share, 0
    )
    return (
        energy[None],
        returned.reshape(own, band, side, ch).astype(F32),
        weight_grad.reshape(-1),
        affine_grad,
    )


def body(images, labels, chain_steps, conv_weights, class_affine, power_vectors, cotangent):
    nsec, nsp = lax.axis_size("section"), lax.axis_size("sp")
    channels = images.shape[3]
    rows = conv_weights.shape[0] // channels
    fits = (
        nsec == KERNELS
        and nsp % 2 == 0
        and nsp & (nsp - 1) == 0
        and images.shape[0] == nsp
        and images.shape[1] * nsp == images.shape[2]
        and images.shape[1] % 2 == 0
        and chain_steps.shape == (1, 1)
        and rows % 16 == 0
        and class_affine.shape[0] * 2 == 5 * channels
    )
    chosen = whole_body if fits else general_body
    return chosen(
        images, labels, chain_steps, conv_weights, class_affine, power_vectors, cotangent
    )


def solution(mesh):
    in_specs = (
        P("section", "sp", None, None),
        P("section", None),
        P(("section", "sp"), None),
        P(("section", "sp")),
        P(("section", "sp")),
        P(),
        P(("section", "sp"), None, None, None),
    )
    out_specs = (
        P(("section", "sp"), None, None, None),
        P("section", "sp", None, None),
        P(("section", "sp")),
        P(("section", "sp")),
    )
    return jax.shard_map(body, mesh=mesh, in_specs=in_specs, out_specs=out_specs, check_vma=False)
```

```python
from functools import partial

import jax
import jax.numpy as jnp
from jax import lax
from jax.experimental import pallas as pl
from jax.experimental.pallas import tpu as pltpu
from jax.sharding import PartitionSpec as P

LANGEVIN_T = 40


HIGHEST = lax.Precision.HIGHEST


def extended_2(block, sides, width):
    for axis, dim in sides:
        count = lax.axis_size(axis)
        forward = [(i, i + 1) for i in range(count - 1)]
        backward = [(target, source) for source, target in forward]
        low = lax.ppermute(
            lax.slice_in_dim(block, block.shape[dim] - width, None, axis=dim), axis, forward
        )
        high = lax.ppermute(lax.slice_in_dim(block, 0, width, axis=dim), axis, backward)
        block = jnp.concatenate([low, block, high], axis=dim)
    return block


def leaky(value):
    return 0.2 * value + 0.8 * jax.nn.softplus(value)


def leaky_slope(value):
    return 0.2 + 0.8 * jax.nn.sigmoid(value)


def spectral(matrix, vector):
    forward = jnp.dot(matrix, vector, precision=HIGHEST)
    unit = forward / jnp.sqrt(jnp.sum(forward * forward) + 1e-06)
    backward = jnp.dot(unit, matrix, precision=HIGHEST)
    return jnp.sqrt(jnp.sum(backward * backward) + 1e-06)


def taps(padded, kernel):
    return lax.conv_general_dilated(
        padded,
        kernel,
        (1, 1),
        "VALID",
        dimension_numbers=("NHWC", "HWIO", "NHWC"),
        preferred_element_type=jnp.float32,
    )


def kernel_grad(padded, grad):
    result = lax.conv_general_dilated(
        padded,
        grad,
        (1, 1),
        "VALID",
        dimension_numbers=("CHWN", "IHWO", "NHWC"),
        preferred_element_type=jnp.float32,
    )
    return jnp.transpose(result, (1, 2, 0, 3))


def flipped(kernel):
    return jnp.transpose(jnp.flip(kernel, (0, 1)), (0, 1, 3, 2))


def trim_rims(extended, band, side):
    start = lax.axis_index("sp") * band
    keep_top = jnp.where(start % side == 0, 0.0, 1.0).astype(extended.dtype)
    keep_bottom = jnp.where((start + band) % side == 0, 0.0, 1.0).astype(extended.dtype)
    merged = jnp.concatenate(
        [extended[:, :1] * keep_top, extended[:, 1:-1], extended[:, -1:] * keep_bottom], axis=1
    )
    return jnp.pad(merged, ((0, 0), (0, 0), (1, 1), (0, 0)))


def rows_forward(values, band, side):
    extended = extended_2(values, (("sp", 1),), 1)
    return trim_rims(extended, band, side)


def rows_backward(values, band, side):
    extended = extended_2(values, (("sp", 1),), 1)
    return trim_rims(extended, band, side)


def pad_whole(values):
    return jnp.pad(values, ((0, 0), (1, 1), (1, 1), (0, 0)))


def affine_terms(upstream, raw, value, scale, gain, sigma):
    pre = upstream * leaky_slope(value)
    grad_raw = (pre * scale[:, None, None, :]).astype(jnp.bfloat16)
    grad_gain = jnp.sum(pre * raw, axis=(1, 2)) / sigma
    grad_bias = jnp.sum(pre, axis=(1, 2))
    grad_sigma = -jnp.sum(grad_gain * gain) / sigma
    return (grad_raw, grad_gain, grad_bias, grad_sigma)


def general_body(images, labels, chain_steps, conv_weights, class_affine, power_vectors, cotangent):
    channels = images.shape[3]
    band = images.shape[1]
    side = images.shape[2]
    half = side // 2
    across = labels.shape[1]
    groups = chain_steps.shape[0]
    gathered_w, gathered_a = (
        lax.all_gather(conv_weights.astype(jnp.bfloat16), ("section", "sp"), axis=0, tiled=True),
        lax.all_gather(class_affine.astype(jnp.bfloat16), ("section", "sp"), axis=0, tiled=True),
    )
    kernels = gathered_w.reshape(4, 3, 3, channels, channels)
    table = gathered_a.astype(jnp.float32).reshape(2, 4, -1, channels)
    count = table.shape[2]
    matrices = kernels.astype(jnp.float32).reshape(4, 9 * channels, channels)
    sigmas = [spectral(matrices[j], power_vectors[j]) for j in range(4)]
    kinds = jnp.arange(count)
    start = lax.axis_index("sp") * groups
    tags_second = lax.dynamic_slice_in_dim(labels, start, groups, 0).reshape(-1)
    onehot_second = (tags_second[:, None] == kinds[None, :]).astype(jnp.float32)
    active = (chain_steps.reshape(-1) > LANGEVIN_T).astype(jnp.float32)
    column = lax.axis_index("sp") * band // side
    picks = jnp.arange(across) == column
    tags_first = jnp.sum(jnp.where(picks[None, :], labels, 0), axis=1)
    onehot_first = (tags_first[:, None] == kinds[None, :]).astype(jnp.float32)
    pad_forward = partial(rows_forward, band=band, side=side)
    pad_backward = partial(rows_backward, band=band, side=side)
    gains_first = jnp.einsum("nk,jkc->jnc", onehot_first, table[0], precision=HIGHEST)
    biases_first = jnp.einsum("nk,jkc->jnc", onehot_first, table[1], precision=HIGHEST)
    gains_second = jnp.einsum("nk,jkc->jnc", onehot_second, table[0], precision=HIGHEST)
    biases_second = jnp.einsum("nk,jkc->jnc", onehot_second, table[1], precision=HIGHEST)
    scales = [
        gains_first[0] / sigmas[0],
        gains_first[1] / sigmas[1],
        gains_second[2] / sigmas[2],
        gains_second[3] / sigmas[3],
    ]
    input_pad = pad_forward(images)
    raw_zero = taps(input_pad, kernels[0])
    pre_zero = raw_zero * scales[0][:, None, None, :] + biases_first[0][:, None, None, :]
    hidden_zero = leaky(pre_zero).astype(jnp.bfloat16)
    hidden_pad = pad_forward(hidden_zero)
    raw_one = taps(hidden_pad, kernels[1])
    pre_one = raw_one * scales[1][:, None, None, :] + biases_first[1][:, None, None, :]
    first_out = images.astype(jnp.float32) + leaky(pre_one)
    moved = lax.all_to_all(
        first_out.astype(jnp.bfloat16), "sp", split_axis=0, concat_axis=1, tiled=True
    )
    whole = moved.reshape(groups * across, side, side, channels)
    whole_pad = pad_whole(whole)
    raw_two = taps(whole_pad, kernels[2])
    pre_two = raw_two * scales[2][:, None, None, :] + biases_second[2][:, None, None, :]
    hidden_two = leaky(pre_two).astype(jnp.bfloat16)
    hidden_two_pad = pad_whole(hidden_two)
    raw_three = taps(hidden_two_pad, kernels[3])
    pre_three = raw_three * scales[3][:, None, None, :] + biases_second[3][:, None, None, :]
    second_out = whole.astype(jnp.float32) + leaky(pre_three)
    pooled = (
        jnp.mean(second_out.reshape(-1, half, 2, half, 2, channels), axis=(2, 4))
        * active[:, None, None, None]
    )
    energy = pooled.reshape(groups, across * half, half, channels)
    upstream = (
        cotangent.astype(jnp.float32).reshape(-1, half, half, channels)
        * (0.25 * active)[:, None, None, None]
    )
    images_n = upstream.shape[0]
    grad_out = jnp.broadcast_to(
        upstream[:, :, None, :, None, :], (images_n, half, 2, half, 2, channels)
    ).reshape(images_n, side, side, channels)
    dz_three, dg_three, db_three, dsig_three = affine_terms(
        grad_out, raw_three, pre_three, scales[3], gains_second[3], sigmas[3]
    )
    kg_three = kernel_grad(hidden_two_pad, dz_three)
    grad_hidden = taps(pad_whole(dz_three), flipped(kernels[3]))
    dz_two, dg_two, db_two, dsig_two = affine_terms(
        grad_hidden, raw_two, pre_two, scales[2], gains_second[2], sigmas[2]
    )
    kg_two = kernel_grad(whole_pad, dz_two)
    grad_whole = grad_out + taps(pad_whole(dz_two), flipped(kernels[2]))
    back_rows = grad_whole.astype(jnp.bfloat16).reshape(groups, across * side, side, channels)
    returned = lax.all_to_all(back_rows, "sp", split_axis=1, concat_axis=0, tiled=True)
    grad_first = returned.astype(jnp.float32)
    dz_one, dg_one, db_one, dsig_one = affine_terms(
        grad_first, raw_one, pre_one, scales[1], gains_first[1], sigmas[1]
    )
    kg_one = kernel_grad(hidden_pad, dz_one)
    grad_hidden_first = taps(pad_backward(dz_one), flipped(kernels[1]))
    dz_zero, dg_zero, db_zero, dsig_zero = affine_terms(
        grad_hidden_first, raw_zero, pre_zero, scales[0], gains_first[0], sigmas[0]
    )
    kg_zero = kernel_grad(input_pad, dz_zero)
    local_grad = grad_first + taps(pad_backward(dz_zero), flipped(kernels[0]))
    conv_grads = [kg_zero, kg_one, kg_two, kg_three]
    sigma_grads = [dsig_zero, dsig_one, dsig_two, dsig_three]
    pieces = []
    for index in range(4):
        unused, pullback = jax.vjp(partial(spectral, vector=power_vectors[index]), matrices[index])
        pieces.append(
            conv_grads[index].reshape(9 * channels, channels) + pullback(sigma_grads[index])[0]
        )
    weight_total = jnp.stack(pieces).reshape(-1)
    gain_rows = [
        jnp.einsum("nk,nc->kc", onehot_first, dg_zero, precision=HIGHEST),
        jnp.einsum("nk,nc->kc", onehot_first, dg_one, precision=HIGHEST),
        jnp.einsum("nk,nc->kc", onehot_second, dg_two, precision=HIGHEST),
        jnp.einsum("nk,nc->kc", onehot_second, dg_three, precision=HIGHEST),
    ]
    bias_rows = [
        jnp.einsum("nk,nc->kc", onehot_first, db_zero, precision=HIGHEST),
        jnp.einsum("nk,nc->kc", onehot_first, db_one, precision=HIGHEST),
        jnp.einsum("nk,nc->kc", onehot_second, db_two, precision=HIGHEST),
        jnp.einsum("nk,nc->kc", onehot_second, db_three, precision=HIGHEST),
    ]
    affine_total = jnp.stack([jnp.stack(gain_rows), jnp.stack(bias_rows)]).reshape(-1)
    weight_grad, affine_grad = (
        lax.psum_scatter(weight_total, ("section", "sp"), scatter_dimension=0, tiled=True),
        lax.psum_scatter(affine_total, ("section", "sp"), scatter_dimension=0, tiled=True),
    )
    return (energy, local_grad, weight_grad, affine_grad)

F32 = jnp.float32
BF16 = jnp.bfloat16
MESH = pl.DeviceIdType.MESH
NN = (((1,), (0,)), ((), ()))
NT = (((1,), (1,)), ((), ()))
TN = (((0,), (0,)), ((), ()))
KERNELS = 4
MODES = ("z", "s", "s", "s")
TILE = 16


def dot(left, right, dims, precision=None):
    return lax.dot_general(left, right, dims, precision=precision, preferred_element_type=F32)


def twice(row):
    return jnp.concatenate([row, row], 1)


def beside(value, side):
    rows = value.shape[0]
    column = lax.broadcasted_iota(jnp.int32, (rows, 1), 0) % side
    left = jnp.where(column == 0, 0.0, pltpu.roll(value, 1, 0))
    right = jnp.where(column == side - 1, 0.0, pltpu.roll(value, rows - 1, 0))
    return (left, value, right)


def put_patches(ref, pair, value, side, ch):
    count = value.shape[0] // side
    rows = slice(pair + 1, pair + 1 + count)
    for b, part in enumerate(beside(value, side)):
        part = part.astype(BF16)
        for e in range(2):
            half = part[:, e * ch : (e + 1) * ch].reshape(count, side, ch)
            ref[rows, e, :, b * ch : (b + 1) * ch] = half


def patch_rows(ref, count):
    side, width = ref.shape[2], ref.shape[3]
    parts = [ref[0:count, 1], ref[1 : count + 1, 0], ref[1 : count + 1, 1], ref[2 : count + 2, 0]]
    return jnp.concatenate(parts, -1).reshape(count * side, 4 * width)


def pair_weights(kernel):
    rows = kernel.shape[0] // 3
    zero = jnp.zeros((rows, kernel.shape[1]), kernel.dtype)
    a, b, c = (kernel[i * rows : (i + 1) * rows] for i in range(3))
    pairs = ((a, zero), (b, a), (c, b), (zero, c))
    return jnp.concatenate([jnp.concatenate(pair, 1) for pair in pairs], 0)


def pair_weights_back(kernel):
    ch = kernel.shape[1]
    zero = jnp.zeros((ch, ch), kernel.dtype)
    blocks = []
    for e in range(2):
        row = []
        for r in range(4):
            for b in range(3):
                a = 2 - (r - e)
                tap = (a * 3 + 2 - b) * ch
                row.append(kernel[tap : tap + ch] if 0 <= a <= 2 else zero)
        blocks.append(jnp.concatenate(row, 1))
    return jnp.concatenate(blocks, 0)


def leaky_terms(value):
    small = jnp.exp(-jnp.abs(value))
    result = 0.2 * value + 0.8 * (jnp.maximum(value, 0.0) + jnp.log(1.0 + small))
    return result, 0.6 + 0.4 * jnp.tanh(0.5 * value)


def halves(pairs, ch):
    wide = jnp.concatenate([pairs[:, 0], pairs[:, 1]], -1)
    return wide.reshape(-1, 2 * ch)


def three(row):
    high = row.astype(BF16).astype(F32)
    middle = (row - high).astype(BF16).astype(F32)
    return (high, middle, row - high - middle)


def whole_kernel(
    nsec, nz, count, active_above, modes,
    images, labels_in, steps_in, weights_in, affine_in, vectors_in, cotangent_in,
    energy, returned, weight_out, table_out,
    labels, steps, weights, affine, vectors, cotangent,
    pieces, lines_all, xin, patches, grads, raws, slopes, up_rows, pool_rows, rows_ref,
    dk, first, summed, second, total, third, wide, joined, last, back, tiles, tables, tables_in,
    local, piece_in, piece_z, piece_s, piece_c, line_out, line_in, image_out, image_in,
    one_out, one_in, two_out, two_in, three_out, three_in, wide_out, wide_in, last_out, last_in,
    back_out, back_in, tile_out, tile_in, table_out_sem, table_in_sem,
):
    nsp = 2 * nz
    side, ch = images.shape[2], images.shape[3]
    band = images.shape[1]
    half = side // 2
    rows = weights.shape[0]
    s = lax.axis_index("section")
    p = lax.axis_index("sp")
    z = p // 2
    c = p % 2

    def sec(d):
        return jnp.bitwise_xor(s, d)

    def zed(d):
        return jnp.bitwise_xor(z, d)

    def remote(src, dst, out_sem, in_sem, where):
        return pltpu.make_async_remote_copy(
            src_ref=src, dst_ref=dst, send_sem=out_sem, recv_sem=in_sem,
            device_id=where, device_id_type=MESH,
        )

    sibling = (s, p + 1 - 2 * c)

    def at_section(d):
        return (sec(d), p)

    def at_z(d):
        return (s, 2 * zed(d) + c)

    def at_sp(d):
        return (s, jnp.bitwise_xor(p, d))

    barrier = pltpu.get_barrier_semaphore()
    for d in range(1, nsec):
        pl.semaphore_signal(barrier, inc=1, device_id=at_section(d), device_id_type=MESH)
    for d in range(1, nsp):
        pl.semaphore_signal(barrier, inc=1, device_id=at_sp(d), device_id_type=MESH)

    arrivals = [
        pltpu.make_async_copy(src, dst, local.at[i])
        for i, (src, dst) in enumerate((
            (weights_in, weights), (vectors_in, vectors), (affine_in, affine), (labels_in, labels),
            (steps_in, steps), (cotangent_in, cotangent), (images.at[p], xin.at[p]),
        ))
    ]
    for copy in arrivals:
        copy.start()

    patches[:, 0:1] = jnp.zeros_like(patches[:, 0:1])
    patches[:, half + 1 :] = jnp.zeros_like(patches[:, half + 1 :])
    grads[0:1] = jnp.zeros_like(grads[0:1])
    grads[half + 1 :] = jnp.zeros_like(grads[half + 1 :])

    for copy in arrivals[:3]:
        copy.wait()
    mine = weights[...].astype(BF16)
    pieces[s, z, c] = mine
    matrix = mine.astype(F32)
    vector = vectors[pl.ds(s, 1)]
    proj = jnp.sum(matrix * vector, axis=1, keepdims=True)
    crossed = jnp.sum(proj * matrix, axis=0, keepdims=True)
    norm = jnp.broadcast_to(jnp.sum(proj * proj, axis=0, keepdims=True), (1, ch))
    cuts = ((0, ch), (ch, ch), (2 * ch, ch // 2))
    flat = jnp.concatenate([affine[pl.ds(at, n)].reshape(1, n) for at, n in cuts], 1)
    flat = flat.astype(BF16).astype(F32)
    hollow = jnp.zeros((1, ch // 2), F32)
    even = [flat[:, 0:ch], flat[:, ch : 2 * ch], jnp.concatenate([flat[:, 2 * ch :], hollow], 1)]
    odd = [
        jnp.concatenate([hollow, flat[:, 0 : ch // 2]], 1),
        flat[:, ch // 2 : 3 * ch // 2],
        flat[:, 3 * ch // 2 :],
    ]
    is_odd = jnp.full((1, ch), c, jnp.int32) == 1
    lines = [jnp.where(is_odd, b, a) for a, b in zip(even, odd)] + [*three(crossed), *three(norm)]
    tile = jnp.zeros((TILE, ch), F32)
    line = lax.broadcasted_iota(jnp.int32, (TILE, ch), 0)
    for index, value in enumerate(lines):
        tile = jnp.where(line == index, value, tile)
    lines_all[s, z, c] = tile.astype(BF16)

    pl.semaphore_wait(barrier, nsec - 1 + nsp - 1)

    def piece_copy(a, b, e, out_sem, where):
        ref = pieces.at[a, b, e]
        return remote(ref, ref, out_sem, piece_in.at[a, b, e], where)

    def line_copy(ref, index, where):
        return remote(ref, ref, line_out.at[index], line_in.at[index], where)

    sends = []

    def send(copy):
        copy.start()
        sends.append(copy)

    for d in range(1, nsec):
        send(line_copy(lines_all.at[s, z, c], d - 1, at_section(d)))
    for d in range(1, nz):
        send(piece_copy(s, z, c, piece_z.at[d - 1], at_z(d)))
    for d in range(1, nsec):
        send(piece_copy(s, z, c, piece_s.at[0, d - 1], at_section(d)))
    for d in range(1, nsp):
        q = jnp.bitwise_xor(p, d)
        send(remote(images.at[q], xin.at[p], image_out.at[d - 1], image_in.at[p], at_sp(d)))
    send(piece_copy(s, z, c, piece_c.at[0, 0], sibling))

    for copy in arrivals[3:]:
        copy.wait()
    active = jnp.where(steps[...] > active_above, 1.0, 0.0)
    pulled = cotangent[...].astype(F32).reshape(half * half, ch) * (0.25 * active)
    up_rows[pl.ds(0, half * half, stride=2), :] = pulled
    up_rows[pl.ds(1, half * half, stride=2), :] = pulled

    for d in range(1, nsec):
        line_copy(lines_all.at[sec(d), z, c], d - 1, sibling).wait_recv()
    for d in range(1, nz):
        send(line_copy(lines_all.at[:, z, c], nsec - 2 + d, at_z(d)))
    for d in range(1, nz):
        piece_copy(s, zed(d), c, piece_z.at[d - 1], sibling).wait_recv()
        for e in range(1, nsec):
            send(piece_copy(s, zed(d), c, piece_s.at[d, e - 1], at_section(e)))
        send(piece_copy(s, zed(d), c, piece_c.at[0, d], sibling))
    for d in range(1, nz):
        line_copy(lines_all.at[:, zed(d), c], nsec - 2 + d, sibling).wait_recv()
    lines_last = nsec + nz - 2
    send(line_copy(lines_all.at[:, :, c], lines_last, sibling))

    def pass_on(e):
        for d in range(1, nsec):
            piece_copy(sec(d), zed(e), c, piece_c.at[d, e], sibling).wait_recv()
            send(piece_copy(sec(d), zed(e), c, piece_c.at[d, e], sibling))

    pass_on(0)
    per = band // 2
    for d in range(nsp):
        q = jnp.bitwise_xor(p, d)
        if d:
            remote(images.at[q], xin.at[q], image_out.at[d - 1], image_in.at[q], sibling).wait_recv()
    for q in range(nsp):
        block = xin[q].astype(F32).reshape(per, 2, side, ch)
        put_patches(patches.at[0], q * per, halves(block, ch), side, ch)
    for e in range(1, nz):
        pass_on(e)
    line_copy(lines_all.at[:, :, 1 - c], lines_last, sibling).wait_recv()

    tags = labels[...]
    at = lax.broadcasted_iota(jnp.int32, tags.shape, 1)
    label = jnp.sum(jnp.where(at == p, tags, 0).astype(F32), axis=1, keepdims=True).astype(jnp.int32)
    width = nsec * nsp * TILE
    column = lax.broadcasted_iota(jnp.int32, (TILE, width), 1)
    picked = lax.broadcasted_iota(jnp.int32, (TILE, width), 0)
    device = jnp.right_shift(column, 4)
    entry = jnp.bitwise_and(column, TILE - 1)
    wanted = picked * count + label
    at_row = jnp.right_shift(device * 5, 1) + entry
    section = jnp.right_shift(column, (nsp * TILE).bit_length() - 1)
    chosen = (picked < 8) & (entry < 3) & (at_row == wanted)
    chosen |= (picked >= 8) & (picked < 12) & (section == picked - 8) & (entry >= 3) & (entry < 6)
    chosen |= (picked >= 12) & (section == picked - 12) & (entry >= 6) & (entry < 9)
    everything = lines_all[...].reshape(width, ch)
    rows_ref[...] = dot(jnp.where(chosen, 1.0, 0.0).astype(BF16), everything, NN)
    gains, biases = rows_ref[0:4], rows_ref[4:8]
    lengths = jnp.sqrt(rows_ref[12:16] + 1e-06)
    units = rows_ref[8:12] / lengths
    sigmas = jnp.sqrt(jnp.sum(units * units, axis=1, keepdims=True) + 1e-06)
    scales = gains / sigmas

    def kernel_of(j):
        parts = [pieces[j, b, e] for b in range(nz) for e in range(2)]
        return jnp.concatenate(parts, 0)

    chunks = 8
    step = half // chunks
    spans = [(i * step, pl.ds(i * step * side, step * side)) for i in range(chunks)]

    for j in range(KERNELS):
        for b in range(nz):
            piece_copy(j, b, 1 - c, piece_c.at[0, 0], sibling).wait_recv()
        raws[j] = dot(patch_rows(patches.at[j], half), pair_weights(kernel_of(j)), NN)
        scale, bias = twice(scales[j : j + 1]), twice(biases[j : j + 1])
        for pair, span in spans:
            value, slope = leaky_terms(raws[j, span] * scale + bias)
            slopes[j, span] = slope
            if j % 2 == 1:
                source = patches[j - 1, pair + 1 : pair + 1 + step, :, :, ch : 2 * ch]
                value = halves(source.astype(F32), ch) + value
            if j < KERNELS - 1:
                put_patches(patches.at[j + 1], pair, value, side, ch)
            else:
                pool_rows[span] = value[:, :ch] + value[:, ch:]
    pooled = pool_rows[pl.ds(0, half * half, stride=2), :] + pool_rows[pl.ds(1, half * half, stride=2), :]
    energy[...] = (pooled * (0.25 * active)).reshape(half, half, ch)

    def first_copy(j):
        return remote(dk.at[j, :, 1 - c], first.at[j], one_out.at[j], one_in.at[j], sibling)

    def second_copy(j, d):
        return remote(
            summed.at[j, zed(d)], second.at[j, d - 1], two_out.at[j, d - 1], two_in.at[j, d - 1], at_z(d)
        )

    def third_copy(j):
        d = jnp.maximum(jnp.bitwise_xor(s, j) - 1, 0)
        return remote(total.at[j], third.at[d], three_out.at[j], three_in.at[d], (j, p))

    def wide_copy(j):
        d = jnp.maximum(jnp.bitwise_xor(s, j) - 1, 0)
        return remote(summed.at[j], wide.at[d], wide_out.at[j], wide_in.at[d], (j, p))

    def last_copy(d):
        return remote(joined.at[zed(d)], last.at[d - 1], last_out.at[d - 1], last_in.at[d - 1], at_z(d))

    def first_sum(j):
        first_copy(j).wait_recv()
        summed[j] = (dk[j, :, c].astype(F32) + first[j].astype(F32)).astype(BF16)
        if modes[j] == "z":
            for d in range(1, nz):
                send(second_copy(j, d))
        else:
            pl.when(s != j)(lambda: wide_copy(j).start())

    def second_sum(j):
        value = summed[j, z].astype(F32)
        for d in range(1, nz):
            second_copy(j, d).wait_recv()
            value += second[j, d - 1].astype(F32)
        total[j] = value.astype(BF16)
        pl.when(s != j)(lambda: third_copy(j).start())

    by_z = [j for j in range(KERNELS) if modes[j] == "z"]
    by_section = [j for j in range(KERNELS) if modes[j] != "z"]

    def is_one_of(kernels):
        found = s < 0
        for j in kernels:
            found = jnp.logical_or(found, s == j)
        return found

    lines = []
    for j in reversed(range(KERNELS)):
        scale = twice(scales[j : j + 1])
        gain_sum = jnp.zeros((1, 2 * ch), F32)
        bias_sum = jnp.zeros((1, 2 * ch), F32)
        for pair, span in spans:
            upstream = twice(up_rows[span]) if j == KERNELS - 1 else slopes[j + 1, span]
            pre = upstream * slopes[j, span]
            gain_sum += jnp.sum(pre * raws[j, span], axis=0, keepdims=True)
            bias_sum += jnp.sum(pre, axis=0, keepdims=True)
            put_patches(grads, pair, pre * scale, side, ch)
        sigma = sigmas[j : j + 1]
        gain_row = (gain_sum[:, :ch] + gain_sum[:, ch:]) / sigma
        lines.append((j, gain_row))
        lines.append((4 + j, bias_sum[:, :ch] + bias_sum[:, ch:]))
        lines.append((8 + j, -gain_row * gains[j : j + 1] / sigma))
        if j == 0:
            tile = jnp.zeros((TILE, ch), F32)
            for index, value in lines:
                tile = jnp.where(line == index, value, tile)
            tiles[p] = tile
            for d in range(1, nsp):
                send(remote(tiles.at[p], tiles.at[p], tile_out.at[d - 1], tile_in.at[p], at_sp(d)))
        inputs = patches[j, 1 : half + 1].reshape(2 * half * side, 3 * ch)
        centre = grads[...].reshape(2 * half + 4, side, 3 * ch)[:, :, ch : 2 * ch]
        shifted = [centre[3 - a : 3 - a + 2 * half] for a in range(3)]
        shifted = jnp.concatenate(shifted, -1).reshape(2 * half * side, 3 * ch)
        grad = dot(inputs, shifted, TN)
        grad = jnp.concatenate([grad[:, a * ch : (a + 1) * ch] for a in range(3)], 0).astype(BF16)
        for b in range(nz):
            for e in range(2):
                at = (2 * b + e) * rows
                dk[j, b, e] = grad[at : at + rows]
        send(first_copy(j))
        down = dot(patch_rows(grads, half), pair_weights_back(kernel_of(j)), NT)
        if j == 2:
            down = (down + twice(up_rows[...])).astype(BF16).astype(F32)
            raws[2] = down
        if j > 0:
            slopes[j] = down
        else:
            down = (down + raws[2]).astype(BF16)
            for q in range(nsp):
                for e in range(2):
                    part = down[q * per * side : (q + 1) * per * side, e * ch : (e + 1) * ch]
                    back[q, :, e] = part.reshape(per, side, ch)
        first_sum(j)

    own_back = pltpu.make_async_copy(back.at[p], returned.at[p], local.at[7])
    own_back.start()
    for d in range(1, nsp):
        q = jnp.bitwise_xor(p, d)
        send(remote(back.at[q], returned.at[p], back_out.at[d - 1], back_in.at[p], at_sp(d)))

    for d in range(1, nsp):
        q = jnp.bitwise_xor(p, d)
        remote(tiles.at[q], tiles.at[q], tile_out.at[d - 1], tile_in.at[q], sibling).wait_recv()
    spread = nsp * TILE
    column = lax.broadcasted_iota(jnp.int32, (24, spread), 1)
    row = lax.broadcasted_iota(jnp.int32, (24, spread), 0)
    entry = jnp.bitwise_and(column, TILE - 1)
    owner = jnp.right_shift(column, 4)
    tag = jnp.zeros((24, spread), jnp.int32)
    for q in range(nsp):
        tag = jnp.where(owner == q, tags[:, q : q + 1], tag)
    gathered = tiles[...].reshape(spread, ch)
    upper = row >= count
    kind = row - jnp.where(upper, count, 0)
    for blk in range(nsec):
        slot = 2 * blk + jnp.where(upper, 1, 0)
        chosen = (row < 2 * count) & (entry == slot) & (tag == kind)
        chosen |= (row >= 2 * count) & (entry == 8 + row - 2 * count)
        tables[blk] = dot(jnp.where(chosen, 1.0, 0.0), gathered, NN, HIGHEST)
    for d in range(1, nsec):
        send(remote(tables.at[sec(d)], tables_in.at[d - 1], table_out_sem.at[d - 1], table_in_sem.at[d - 1], at_section(d)))
    for j in reversed(by_z):
        second_sum(j)

    @pl.when(is_one_of(by_section))
    def _():
        value = summed[s].astype(F32)
        for d in range(1, nsec):
            remote(summed.at[0], wide.at[d - 1], wide_out.at[0], wide_in.at[d - 1], sibling).wait_recv()
            value += wide[d - 1].astype(F32)
        joined[...] = value.astype(BF16)
        for d in range(1, nz):
            last_copy(d).start()

    table = tables[s]
    for d in range(1, nsec):
        remote(tables.at[sec(d)], tables_in.at[d - 1], table_out_sem.at[d - 1], table_in_sem.at[d - 1], at_section(d)).wait_recv()
        table += tables_in[d - 1]
    table_out[...] = table

    mine = pieces[s, z, c].astype(F32)
    proj = jnp.sum(mine * vector, axis=1, keepdims=True)
    q_row = rows_ref[pl.ds(8 + s, 1)]
    length = jnp.sqrt(rows_ref[pl.ds(12 + s, 1)][:, 0:1] + 1e-06)
    unit = q_row / length
    sigma = jnp.sqrt(jnp.sum(unit * unit, axis=1, keepdims=True) + 1e-06)
    along = unit / sigma
    reach = jnp.sum(mine * along, axis=1, keepdims=True)
    crossing = jnp.sum(q_row * along, axis=1, keepdims=True)
    slope = (reach - proj * (crossing / (length * length))) / length
    dsigma = table_out[pl.ds(2 * count + s, 1)]
    dsigma = jnp.sum(dsigma, axis=1, keepdims=True)
    weight_out[...] = dsigma * ((proj / length) * along + slope * vector)

    @pl.when(is_one_of(by_z))
    def _():
        value = weight_out[...] + total[s].astype(F32)
        for d in range(1, nsec):
            remote(total.at[0], third.at[d - 1], three_out.at[0], three_in.at[d - 1], sibling).wait_recv()
            value += third[d - 1].astype(F32)
        weight_out[...] = value

    @pl.when(is_one_of(by_section))
    def _():
        value = weight_out[...] + joined[z].astype(F32)
        for d in range(1, nz):
            last_copy(d).wait_recv()
            value += last[d - 1].astype(F32)
        weight_out[...] = value
        for d in range(1, nz):
            last_copy(d).wait_send()

    for d in range(1, nsp):
        q = jnp.bitwise_xor(p, d)
        remote(back.at[q], returned.at[q], back_out.at[d - 1], back_in.at[q], sibling).wait_recv()
    own_back.wait()
    for copy in sends:
        copy.wait_send()
    for j in by_z:
        pl.when(s != j)(lambda j=j: third_copy(j).wait_send())
    for j in by_section:
        pl.when(s != j)(lambda j=j: wide_copy(j).wait_send())


def finish_kernel(count, energy_in, returned, weight_in, table, energy, grad, weight, affine, wide, sems):
    copies = [
        pltpu.make_async_copy(energy_in, energy, sems.at[0]),
        pltpu.make_async_copy(weight_in, weight, sems.at[1]),
    ]
    for copy in copies:
        copy.start()
    for i in range(returned.shape[0]):
        wide[i] = returned[i].astype(F32)
        copies.append(pltpu.make_async_copy(wide.at[i], grad.at[i], sems.at[2 + i]))
        copies[-1].start()
    ch = table.shape[1]
    p = lax.axis_index("sp")
    start = 5 * p // 2
    block = table[pl.ds(start, 3)]
    odd = jnp.full((1, ch), p % 2, jnp.int32) == 1
    middle = ch // 2
    swapped = [jnp.concatenate([block[i : i + 1, middle:], block[i : i + 1, :middle]], 1) for i in range(3)]
    low = lax.broadcasted_iota(jnp.int32, (1, ch), 1) < middle
    later = [jnp.where(low, swapped[i], swapped[i + 1]) for i in range(2)]
    affine[pl.ds(0, ch)] = jnp.where(odd, later[0], block[0:1]).reshape(ch)
    affine[pl.ds(ch, ch)] = jnp.where(odd, later[1], block[1:2]).reshape(ch)
    affine[pl.ds(2 * ch, middle)] = jnp.where(odd, swapped[2], block[2:3])[:, :middle].reshape(middle)
    for copy in copies:
        copy.wait()


def whole_body(images, labels, chain_steps, conv_weights, class_affine, power_vectors, cotangent):
    nsec, nsp = lax.axis_size("section"), lax.axis_size("sp")
    nz = nsp // 2
    own, band, side, ch = images.shape
    half = side // 2
    rows = conv_weights.shape[0] // ch
    share = class_affine.shape[0]
    count = share * nsec * nsp // (2 * KERNELS * ch)
    anywhere = pl.BlockSpec(memory_space=pl.ANY)
    vmem = pl.BlockSpec(memory_space=pltpu.VMEM)
    pixels = half * side
    dma = pltpu.SemaphoreType.DMA
    results = pl.pallas_call(
        partial(whole_kernel, nsec, nz, count, LANGEVIN_T, MODES),
        out_shape=[
            pltpu.VMEM((half, half, ch), F32),
            pltpu.VMEM((own, band // 2, 2, side, ch), BF16),
            pltpu.VMEM((rows, ch), F32),
            pltpu.VMEM((24, ch), F32),
        ],
        in_specs=[anywhere] * 7,
        out_specs=[vmem] * 4,
        scratch_shapes=[
            pltpu.VMEM(labels.shape[::-1], jnp.int32),
            pltpu.VMEM(chain_steps.shape, jnp.int32),
            pltpu.VMEM((rows, ch), F32),
            pltpu.VMEM((share,), F32),
            pltpu.VMEM(power_vectors.shape, F32),
            pltpu.VMEM((half, half, ch), BF16),
            pltpu.VMEM((nsec, nz, 2, rows, ch), BF16),
            pltpu.VMEM((nsec, nz, 2, TILE, ch), BF16),
            pltpu.VMEM((nsp, band, side, ch), BF16),
            pltpu.VMEM((KERNELS, half + 2, 2, side, 3 * ch), BF16),
            pltpu.VMEM((half + 2, 2, side, 3 * ch), BF16),
            pltpu.VMEM((KERNELS, pixels, 2 * ch), F32),
            pltpu.VMEM((KERNELS, pixels, 2 * ch), F32),
            pltpu.VMEM((pixels, ch), F32),
            pltpu.VMEM((pixels, ch), F32),
            pltpu.VMEM((TILE, ch), F32),
            pltpu.VMEM((KERNELS, nz, 2, rows, ch), BF16),
            pltpu.VMEM((KERNELS, nz, rows, ch), BF16),
            pltpu.VMEM((KERNELS, nz, rows, ch), BF16),
            pltpu.VMEM((KERNELS, nz - 1, rows, ch), BF16),
            pltpu.VMEM((KERNELS, rows, ch), BF16),
            pltpu.VMEM((nsec - 1, rows, ch), BF16),
            pltpu.VMEM((nsec - 1, nz, rows, ch), BF16),
            pltpu.VMEM((nz, rows, ch), BF16),
            pltpu.VMEM((nz - 1, rows, ch), BF16),
            pltpu.VMEM((nsp, band // 2, 2, side, ch), BF16),
            pltpu.VMEM((nsp, TILE, ch), F32),
            pltpu.VMEM((nsec, 24, ch), F32),
            pltpu.VMEM((nsec - 1, 24, ch), F32),
            dma((8,)),
            dma((nsec, nz, 2)),
            dma((nz - 1,)),
            dma((nz, nsec - 1)),
            dma((nsec, nz)),
            dma((nsec + nz - 1,)),
            dma((nsec + nz - 1,)),
            dma((nsp - 1,)),
            dma((nsp,)),
            dma((KERNELS,)),
            dma((KERNELS,)),
            dma((KERNELS, nz - 1)),
            dma((KERNELS, nz - 1)),
            dma((KERNELS,)),
            dma((nsec - 1,)),
            dma((KERNELS,)),
            dma((nsec - 1,)),
            dma((nz - 1,)),
            dma((nz - 1,)),
            dma((nsp - 1,)),
            dma((nsp,)),
            dma((nsp - 1,)),
            dma((nsp,)),
            dma((nsec - 1,)),
            dma((nsec - 1,)),
        ],
        compiler_params=pltpu.CompilerParams(
            collective_id=0, has_side_effects=True, vmem_limit_bytes=56 * 2**20
        ),
    )(
        images,
        labels.reshape(labels.shape[::-1]),
        chain_steps,
        conv_weights.reshape(rows, ch),
        class_affine,
        power_vectors,
        cotangent.reshape(half, half, ch),
    )
    energy, returned, weight_grad, affine_grad = pl.pallas_call(
        partial(finish_kernel, count),
        out_shape=[
            jax.ShapeDtypeStruct((half, half, ch), F32),
            jax.ShapeDtypeStruct((own, band // 2, 2, side, ch), F32),
            jax.ShapeDtypeStruct((rows, ch), F32),
            jax.ShapeDtypeStruct((share,), F32),
        ],
        in_specs=[vmem] * 4,
        out_specs=[anywhere] * 3 + [vmem],
        scratch_shapes=[pltpu.VMEM((own, band // 2, 2, side, ch), F32), dma((own + 2,))],
    )(*(pltpu.with_memory_space_constraint(r, pltpu.VMEM) for r in results))
    return (
        energy[None],
        returned.reshape(own, band, side, ch),
        weight_grad.reshape(-1),
        affine_grad,
    )


def body(images, labels, chain_steps, conv_weights, class_affine, power_vectors, cotangent):
    nsec, nsp = lax.axis_size("section"), lax.axis_size("sp")
    channels = images.shape[3]
    rows = conv_weights.shape[0] // channels
    fits = (
        nsec == KERNELS
        and nsp % 2 == 0
        and nsp & (nsp - 1) == 0
        and images.shape[0] == nsp
        and images.shape[1] * nsp == images.shape[2]
        and images.shape[1] % 2 == 0
        and chain_steps.shape == (1, 1)
        and rows % 16 == 0
        and class_affine.shape[0] * 2 == 5 * channels
    )
    chosen = whole_body if fits else general_body
    return chosen(
        images, labels, chain_steps, conv_weights, class_affine, power_vectors, cotangent
    )


def solution(mesh):
    in_specs = (
        P("section", "sp", None, None),
        P("section", None),
        P(("section", "sp"), None),
        P(("section", "sp")),
        P(("section", "sp")),
        P(),
        P(("section", "sp"), None, None, None),
    )
    out_specs = (
        P(("section", "sp"), None, None, None),
        P("section", "sp", None, None),
        P(("section", "sp")),
        P(("section", "sp")),
    )
    return jax.shard_map(body, mesh=mesh, in_specs=in_specs, out_specs=out_specs, check_vma=False)
```

```python
from functools import partial

import jax
import jax.numpy as jnp
from jax import lax
from jax.experimental import pallas as pl
from jax.experimental.pallas import tpu as pltpu
from jax.sharding import PartitionSpec as P

LANGEVIN_T = 40


HIGHEST = lax.Precision.HIGHEST


def extended_2(block, sides, width):
    for axis, dim in sides:
        count = lax.axis_size(axis)
        forward = [(i, i + 1) for i in range(count - 1)]
        backward = [(target, source) for source, target in forward]
        low = lax.ppermute(
            lax.slice_in_dim(block, block.shape[dim] - width, None, axis=dim), axis, forward
        )
        high = lax.ppermute(lax.slice_in_dim(block, 0, width, axis=dim), axis, backward)
        block = jnp.concatenate([low, block, high], axis=dim)
    return block


def leaky(value):
    return 0.2 * value + 0.8 * jax.nn.softplus(value)


def leaky_slope(value):
    return 0.2 + 0.8 * jax.nn.sigmoid(value)


def spectral(matrix, vector):
    forward = jnp.dot(matrix, vector, precision=HIGHEST)
    unit = forward / jnp.sqrt(jnp.sum(forward * forward) + 1e-06)
    backward = jnp.dot(unit, matrix, precision=HIGHEST)
    return jnp.sqrt(jnp.sum(backward * backward) + 1e-06)


def taps(padded, kernel):
    return lax.conv_general_dilated(
        padded,
        kernel,
        (1, 1),
        "VALID",
        dimension_numbers=("NHWC", "HWIO", "NHWC"),
        preferred_element_type=jnp.float32,
    )


def kernel_grad(padded, grad):
    result = lax.conv_general_dilated(
        padded,
        grad,
        (1, 1),
        "VALID",
        dimension_numbers=("CHWN", "IHWO", "NHWC"),
        preferred_element_type=jnp.float32,
    )
    return jnp.transpose(result, (1, 2, 0, 3))


def flipped(kernel):
    return jnp.transpose(jnp.flip(kernel, (0, 1)), (0, 1, 3, 2))


def trim_rims(extended, band, side):
    start = lax.axis_index("sp") * band
    keep_top = jnp.where(start % side == 0, 0.0, 1.0).astype(extended.dtype)
    keep_bottom = jnp.where((start + band) % side == 0, 0.0, 1.0).astype(extended.dtype)
    merged = jnp.concatenate(
        [extended[:, :1] * keep_top, extended[:, 1:-1], extended[:, -1:] * keep_bottom], axis=1
    )
    return jnp.pad(merged, ((0, 0), (0, 0), (1, 1), (0, 0)))


def rows_forward(values, band, side):
    extended = extended_2(values, (("sp", 1),), 1)
    return trim_rims(extended, band, side)


def rows_backward(values, band, side):
    extended = extended_2(values, (("sp", 1),), 1)
    return trim_rims(extended, band, side)


def pad_whole(values):
    return jnp.pad(values, ((0, 0), (1, 1), (1, 1), (0, 0)))


def affine_terms(upstream, raw, value, scale, gain, sigma):
    pre = upstream * leaky_slope(value)
    grad_raw = (pre * scale[:, None, None, :]).astype(jnp.bfloat16)
    grad_gain = jnp.sum(pre * raw, axis=(1, 2)) / sigma
    grad_bias = jnp.sum(pre, axis=(1, 2))
    grad_sigma = -jnp.sum(grad_gain * gain) / sigma
    return (grad_raw, grad_gain, grad_bias, grad_sigma)


def general_body(images, labels, chain_steps, conv_weights, class_affine, power_vectors, cotangent):
    channels = images.shape[3]
    band = images.shape[1]
    side = images.shape[2]
    half = side // 2
    across = labels.shape[1]
    groups = chain_steps.shape[0]
    gathered_w, gathered_a = (
        lax.all_gather(conv_weights.astype(jnp.bfloat16), ("section", "sp"), axis=0, tiled=True),
        lax.all_gather(class_affine.astype(jnp.bfloat16), ("section", "sp"), axis=0, tiled=True),
    )
    kernels = gathered_w.reshape(4, 3, 3, channels, channels)
    table = gathered_a.astype(jnp.float32).reshape(2, 4, -1, channels)
    count = table.shape[2]
    matrices = kernels.astype(jnp.float32).reshape(4, 9 * channels, channels)
    sigmas = [spectral(matrices[j], power_vectors[j]) for j in range(4)]
    kinds = jnp.arange(count)
    start = lax.axis_index("sp") * groups
    tags_second = lax.dynamic_slice_in_dim(labels, start, groups, 0).reshape(-1)
    onehot_second = (tags_second[:, None] == kinds[None, :]).astype(jnp.float32)
    active = (chain_steps.reshape(-1) > LANGEVIN_T).astype(jnp.float32)
    column = lax.axis_index("sp") * band // side
    picks = jnp.arange(across) == column
    tags_first = jnp.sum(jnp.where(picks[None, :], labels, 0), axis=1)
    onehot_first = (tags_first[:, None] == kinds[None, :]).astype(jnp.float32)
    pad_forward = partial(rows_forward, band=band, side=side)
    pad_backward = partial(rows_backward, band=band, side=side)
    gains_first = jnp.einsum("nk,jkc->jnc", onehot_first, table[0], precision=HIGHEST)
    biases_first = jnp.einsum("nk,jkc->jnc", onehot_first, table[1], precision=HIGHEST)
    gains_second = jnp.einsum("nk,jkc->jnc", onehot_second, table[0], precision=HIGHEST)
    biases_second = jnp.einsum("nk,jkc->jnc", onehot_second, table[1], precision=HIGHEST)
    scales = [
        gains_first[0] / sigmas[0],
        gains_first[1] / sigmas[1],
        gains_second[2] / sigmas[2],
        gains_second[3] / sigmas[3],
    ]
    input_pad = pad_forward(images)
    raw_zero = taps(input_pad, kernels[0])
    pre_zero = raw_zero * scales[0][:, None, None, :] + biases_first[0][:, None, None, :]
    hidden_zero = leaky(pre_zero).astype(jnp.bfloat16)
    hidden_pad = pad_forward(hidden_zero)
    raw_one = taps(hidden_pad, kernels[1])
    pre_one = raw_one * scales[1][:, None, None, :] + biases_first[1][:, None, None, :]
    first_out = images.astype(jnp.float32) + leaky(pre_one)
    moved = lax.all_to_all(
        first_out.astype(jnp.bfloat16), "sp", split_axis=0, concat_axis=1, tiled=True
    )
    whole = moved.reshape(groups * across, side, side, channels)
    whole_pad = pad_whole(whole)
    raw_two = taps(whole_pad, kernels[2])
    pre_two = raw_two * scales[2][:, None, None, :] + biases_second[2][:, None, None, :]
    hidden_two = leaky(pre_two).astype(jnp.bfloat16)
    hidden_two_pad = pad_whole(hidden_two)
    raw_three = taps(hidden_two_pad, kernels[3])
    pre_three = raw_three * scales[3][:, None, None, :] + biases_second[3][:, None, None, :]
    second_out = whole.astype(jnp.float32) + leaky(pre_three)
    pooled = (
        jnp.mean(second_out.reshape(-1, half, 2, half, 2, channels), axis=(2, 4))
        * active[:, None, None, None]
    )
    energy = pooled.reshape(groups, across * half, half, channels)
    upstream = (
        cotangent.astype(jnp.float32).reshape(-1, half, half, channels)
        * (0.25 * active)[:, None, None, None]
    )
    images_n = upstream.shape[0]
    grad_out = jnp.broadcast_to(
        upstream[:, :, None, :, None, :], (images_n, half, 2, half, 2, channels)
    ).reshape(images_n, side, side, channels)
    dz_three, dg_three, db_three, dsig_three = affine_terms(
        grad_out, raw_three, pre_three, scales[3], gains_second[3], sigmas[3]
    )
    kg_three = kernel_grad(hidden_two_pad, dz_three)
    grad_hidden = taps(pad_whole(dz_three), flipped(kernels[3]))
    dz_two, dg_two, db_two, dsig_two = affine_terms(
        grad_hidden, raw_two, pre_two, scales[2], gains_second[2], sigmas[2]
    )
    kg_two = kernel_grad(whole_pad, dz_two)
    grad_whole = grad_out + taps(pad_whole(dz_two), flipped(kernels[2]))
    back_rows = grad_whole.astype(jnp.bfloat16).reshape(groups, across * side, side, channels)
    returned = lax.all_to_all(back_rows, "sp", split_axis=1, concat_axis=0, tiled=True)
    grad_first = returned.astype(jnp.float32)
    dz_one, dg_one, db_one, dsig_one = affine_terms(
        grad_first, raw_one, pre_one, scales[1], gains_first[1], sigmas[1]
    )
    kg_one = kernel_grad(hidden_pad, dz_one)
    grad_hidden_first = taps(pad_backward(dz_one), flipped(kernels[1]))
    dz_zero, dg_zero, db_zero, dsig_zero = affine_terms(
        grad_hidden_first, raw_zero, pre_zero, scales[0], gains_first[0], sigmas[0]
    )
    kg_zero = kernel_grad(input_pad, dz_zero)
    local_grad = grad_first + taps(pad_backward(dz_zero), flipped(kernels[0]))
    conv_grads = [kg_zero, kg_one, kg_two, kg_three]
    sigma_grads = [dsig_zero, dsig_one, dsig_two, dsig_three]
    pieces = []
    for index in range(4):
        unused, pullback = jax.vjp(partial(spectral, vector=power_vectors[index]), matrices[index])
        pieces.append(
            conv_grads[index].reshape(9 * channels, channels) + pullback(sigma_grads[index])[0]
        )
    weight_total = jnp.stack(pieces).reshape(-1)
    gain_rows = [
        jnp.einsum("nk,nc->kc", onehot_first, dg_zero, precision=HIGHEST),
        jnp.einsum("nk,nc->kc", onehot_first, dg_one, precision=HIGHEST),
        jnp.einsum("nk,nc->kc", onehot_second, dg_two, precision=HIGHEST),
        jnp.einsum("nk,nc->kc", onehot_second, dg_three, precision=HIGHEST),
    ]
    bias_rows = [
        jnp.einsum("nk,nc->kc", onehot_first, db_zero, precision=HIGHEST),
        jnp.einsum("nk,nc->kc", onehot_first, db_one, precision=HIGHEST),
        jnp.einsum("nk,nc->kc", onehot_second, db_two, precision=HIGHEST),
        jnp.einsum("nk,nc->kc", onehot_second, db_three, precision=HIGHEST),
    ]
    affine_total = jnp.stack([jnp.stack(gain_rows), jnp.stack(bias_rows)]).reshape(-1)
    weight_grad, affine_grad = (
        lax.psum_scatter(weight_total, ("section", "sp"), scatter_dimension=0, tiled=True),
        lax.psum_scatter(affine_total, ("section", "sp"), scatter_dimension=0, tiled=True),
    )
    return (energy, local_grad, weight_grad, affine_grad)

F32 = jnp.float32
BF16 = jnp.bfloat16
MESH = pl.DeviceIdType.MESH
NN = (((1,), (0,)), ((), ()))
NT = (((1,), (1,)), ((), ()))
TN = (((0,), (0,)), ((), ()))
KERNELS = 4
MODES = ("z", "h", "h", "z")
TILE = 16


def dot(left, right, dims, precision=None):
    return lax.dot_general(left, right, dims, precision=precision, preferred_element_type=F32)


def twice(row):
    return jnp.concatenate([row, row], 1)


def beside(value, side):
    rows = value.shape[0]
    column = lax.broadcasted_iota(jnp.int32, (rows, 1), 0) % side
    left = jnp.where(column == 0, 0.0, pltpu.roll(value, 1, 0))
    right = jnp.where(column == side - 1, 0.0, pltpu.roll(value, rows - 1, 0))
    return (left, value, right)


def put_patches(ref, pair, value, side, ch):
    count = value.shape[0] // side
    rows = pl.ds(pair + 1, count)
    for b, part in enumerate(beside(value, side)):
        part = part.astype(BF16)
        for e in range(2):
            half = part[:, e * ch : (e + 1) * ch].reshape(count, side, ch)
            ref[rows, e, :, b * ch : (b + 1) * ch] = half


def patch_rows(ref, count):
    side, width = ref.shape[2], ref.shape[3]
    parts = [ref[0:count, 1], ref[1 : count + 1, 0], ref[1 : count + 1, 1], ref[2 : count + 2, 0]]
    return jnp.concatenate(parts, -1).reshape(count * side, 4 * width)


def pair_weights(kernel):
    rows = kernel.shape[0] // 3
    zero = jnp.zeros((rows, kernel.shape[1]), kernel.dtype)
    a, b, c = (kernel[i * rows : (i + 1) * rows] for i in range(3))
    pairs = ((a, zero), (b, a), (c, b), (zero, c))
    return jnp.concatenate([jnp.concatenate(pair, 1) for pair in pairs], 0)


def pair_weights_back(kernel):
    ch = kernel.shape[1]
    zero = jnp.zeros((ch, ch), kernel.dtype)
    blocks = []
    for e in range(2):
        row = []
        for r in range(4):
            for b in range(3):
                a = 2 - (r - e)
                tap = (a * 3 + 2 - b) * ch
                row.append(kernel[tap : tap + ch] if 0 <= a <= 2 else zero)
        blocks.append(jnp.concatenate(row, 1))
    return jnp.concatenate(blocks, 0)


def leaky_terms(value):
    small = jnp.exp(-jnp.abs(value))
    result = 0.2 * value + 0.8 * (jnp.maximum(value, 0.0) + jnp.log(1.0 + small))
    return result, 0.6 + 0.4 * jnp.tanh(0.5 * value)


def halves(pairs, ch):
    wide = jnp.concatenate([pairs[:, 0], pairs[:, 1]], -1)
    return wide.reshape(-1, 2 * ch)


def three(row):
    high = row.astype(BF16).astype(F32)
    middle = (row - high).astype(BF16).astype(F32)
    return (high, middle, row - high - middle)


def whole_kernel(
    nsec, nz, count, active_above, modes,
    images, labels_in, steps_in, weights_in, affine_in, vectors_in, cotangent_in,
    energy, returned, weight_out, table_out,
    labels, steps, weights, affine, vectors, cotangent,
    pieces, lines_all, xin, patches, grads, raws, slopes, up_rows, pool_rows, rows_ref,
    dk, first, summed, second, total, third, near, paired, wide, joined, last, back, tiles, tables, tables_in,
    local, piece_in, piece_z, piece_s, piece_c, piece_k, line_out, line_in, image_out, image_in,
    one_out, one_in, two_out, two_in, three_out, three_in, near_out, near_in, wide_out, wide_in, last_sems,
    back_out, back_in, tile_out, tile_in, table_out_sem, table_in_sem,
):
    nsp = 2 * nz
    side, ch = images.shape[2], images.shape[3]
    band = images.shape[1]
    half = side // 2
    rows = weights.shape[0]
    s = lax.axis_index("section")
    p = lax.axis_index("sp")
    z = p // 2
    c = p % 2

    def sec(d):
        return jnp.bitwise_xor(s, d)

    def zed(d):
        return jnp.bitwise_xor(z, d)

    def remote(src, dst, out_sem, in_sem, where):
        return pltpu.make_async_remote_copy(
            src_ref=src, dst_ref=dst, send_sem=out_sem, recv_sem=in_sem,
            device_id=where, device_id_type=MESH,
        )

    sibling = (s, p + 1 - 2 * c)

    def at_section(d):
        return (sec(d), p)

    def at_z(d):
        return (s, 2 * zed(d) + c)

    def at_sp(d):
        return (s, jnp.bitwise_xor(p, d))

    barrier = pltpu.get_barrier_semaphore()
    for d in range(1, nsec):
        pl.semaphore_signal(barrier, inc=1, device_id=at_section(d), device_id_type=MESH)
    for d in range(1, nsp):
        pl.semaphore_signal(barrier, inc=1, device_id=at_sp(d), device_id_type=MESH)

    arrivals = [
        pltpu.make_async_copy(src, dst, local.at[i])
        for i, (src, dst) in enumerate((
            (weights_in, weights), (vectors_in, vectors), (affine_in, affine), (labels_in, labels),
            (steps_in, steps), (cotangent_in, cotangent), (images.at[p], xin.at[p]),
        ))
    ]
    for copy in arrivals:
        copy.start()

    patches[:, 0:1] = jnp.zeros_like(patches[:, 0:1])
    patches[:, half + 1 :] = jnp.zeros_like(patches[:, half + 1 :])
    grads[0:1] = jnp.zeros_like(grads[0:1])
    grads[half + 1 :] = jnp.zeros_like(grads[half + 1 :])

    for copy in arrivals[:3]:
        copy.wait()
    mine = weights[...].astype(BF16)
    pieces[s, z, c] = mine
    matrix = mine.astype(F32)
    vector = vectors[pl.ds(s, 1)]
    proj = jnp.sum(matrix * vector, axis=1, keepdims=True)
    crossed = jnp.sum(proj * matrix, axis=0, keepdims=True)
    norm = jnp.broadcast_to(jnp.sum(proj * proj, axis=0, keepdims=True), (1, ch))
    cuts = ((0, ch), (ch, ch), (2 * ch, ch // 2))
    flat = jnp.concatenate([affine[pl.ds(at, n)].reshape(1, n) for at, n in cuts], 1)
    flat = flat.astype(BF16).astype(F32)
    hollow = jnp.zeros((1, ch // 2), F32)
    even = [flat[:, 0:ch], flat[:, ch : 2 * ch], jnp.concatenate([flat[:, 2 * ch :], hollow], 1)]
    odd = [
        jnp.concatenate([hollow, flat[:, 0 : ch // 2]], 1),
        flat[:, ch // 2 : 3 * ch // 2],
        flat[:, 3 * ch // 2 :],
    ]
    is_odd = jnp.full((1, ch), c, jnp.int32) == 1
    lines = [jnp.where(is_odd, b, a) for a, b in zip(even, odd)] + [*three(crossed), *three(norm)]
    tile = jnp.zeros((TILE, ch), F32)
    line = lax.broadcasted_iota(jnp.int32, (TILE, ch), 0)
    for index, value in enumerate(lines):
        tile = jnp.where(line == index, value, tile)
    lines_all[s, z, c] = tile.astype(BF16)

    pl.semaphore_wait(barrier, nsec - 1 + nsp - 1)

    def piece_copy(a, b, e, out_sem, where):
        ref = pieces.at[a, b, e]
        return remote(ref, ref, out_sem, piece_in.at[a, b, e], where)

    def line_copy(ref, index, where):
        return remote(ref, ref, line_out.at[index], line_in.at[index], where)

    sends = []

    def send(copy):
        copy.start()
        sends.append(copy)

    for d in range(1, nsec):
        send(line_copy(lines_all.at[s, z, c], d - 1, at_section(d)))
    for d in range(1, nz):
        send(piece_copy(s, z, c, piece_z.at[d - 1], at_z(d)))
    for d in range(1, nsec):
        send(piece_copy(s, z, c, piece_s.at[0, d - 1], at_section(d)))
    send(piece_copy(s, z, c, piece_c.at[0], sibling))

    for copy in arrivals[3:]:
        copy.wait()
    active = jnp.where(steps[...] > active_above, 1.0, 0.0)
    pulled = cotangent[...].astype(F32).reshape(half * half, ch) * (0.25 * active)
    up_rows[pl.ds(0, half * half, stride=2), :] = pulled
    up_rows[pl.ds(1, half * half, stride=2), :] = pulled

    for d in range(1, nsec):
        line_copy(lines_all.at[sec(d), z, c], d - 1, sibling).wait_recv()
    for d in range(1, nz):
        send(line_copy(lines_all.at[:, z, c], nsec - 2 + d, at_z(d)))
    for d in range(1, nsp):
        q = jnp.bitwise_xor(p, d)
        send(remote(images.at[q], xin.at[p], image_out.at[d - 1], image_in.at[p], at_sp(d)))
    for d in range(1, nz):
        piece_copy(s, zed(d), c, piece_z.at[d - 1], sibling).wait_recv()
        for e in range(1, nsec):
            send(piece_copy(s, zed(d), c, piece_s.at[d, e - 1], at_section(e)))
        send(piece_copy(s, zed(d), c, piece_c.at[d], sibling))
    for d in range(1, nz):
        line_copy(lines_all.at[:, zed(d), c], nsec - 2 + d, sibling).wait_recv()
    lines_last = nsec + nz - 2
    send(line_copy(lines_all.at[:, :, c], lines_last, sibling))

    def pass_on(e):
        for d in range(1, nsec):
            copy = piece_copy(sec(d), zed(e), c, piece_k.at[d, e], sibling)
            copy.wait_recv()
            send(copy)

    per = band // 2

    def take_image(d):
        q = jnp.bitwise_xor(p, d)
        if d:
            remote(images.at[q], xin.at[q], image_out.at[d - 1], image_in.at[q], sibling).wait_recv()
        block = xin[q].astype(F32).reshape(per, 2, side, ch)
        put_patches(patches.at[0], q * per, halves(block, ch), side, ch)

    for e in range(nz):
        pass_on(e)
        take_image(2 * e)
        take_image(2 * e + 1)
    line_copy(lines_all.at[:, :, 1 - c], lines_last, sibling).wait_recv()

    tags = labels[...]
    at = lax.broadcasted_iota(jnp.int32, tags.shape, 1)
    label = jnp.sum(jnp.where(at == p, tags, 0).astype(F32), axis=1, keepdims=True).astype(jnp.int32)
    width = nsec * nsp * TILE
    column = lax.broadcasted_iota(jnp.int32, (TILE, width), 1)
    picked = lax.broadcasted_iota(jnp.int32, (TILE, width), 0)
    device = jnp.right_shift(column, 4)
    entry = jnp.bitwise_and(column, TILE - 1)
    wanted = picked * count + label
    at_row = jnp.right_shift(device * 5, 1) + entry
    section = jnp.right_shift(column, (nsp * TILE).bit_length() - 1)
    chosen = (picked < 8) & (entry < 3) & (at_row == wanted)
    chosen |= (picked >= 8) & (picked < 12) & (section == picked - 8) & (entry >= 3) & (entry < 6)
    chosen |= (picked >= 12) & (section == picked - 12) & (entry >= 6) & (entry < 9)
    everything = lines_all[...].reshape(width, ch)
    rows_ref[...] = dot(jnp.where(chosen, 1.0, 0.0).astype(BF16), everything, NN)
    gains, biases = rows_ref[0:4], rows_ref[4:8]
    lengths = jnp.sqrt(rows_ref[12:16] + 1e-06)
    units = rows_ref[8:12] / lengths
    sigmas = jnp.sqrt(jnp.sum(units * units, axis=1, keepdims=True) + 1e-06)
    scales = gains / sigmas

    def kernel_of(j):
        parts = [pieces[j, b, e] for b in range(nz) for e in range(2)]
        return jnp.concatenate(parts, 0)

    chunks = 8
    step = half // chunks
    spans = [(i * step, pl.ds(i * step * side, step * side)) for i in range(chunks)]

    for j in range(KERNELS):
        for b in range(nz):
            piece_copy(j, b, 1 - c, piece_c.at[0], sibling).wait_recv()
        raws[j] = dot(patch_rows(patches.at[j], half), pair_weights(kernel_of(j)), NN)
        scale, bias = twice(scales[j : j + 1]), twice(biases[j : j + 1])
        for pair, span in spans:
            value, slope = leaky_terms(raws[j, span] * scale + bias)
            slopes[j, span] = slope
            if j % 2 == 1:
                source = patches[j - 1, pair + 1 : pair + 1 + step, :, :, ch : 2 * ch]
                value = halves(source.astype(F32), ch) + value
            if j < KERNELS - 1:
                put_patches(patches.at[j + 1], pair, value, side, ch)
            else:
                pool_rows[span] = value[:, :ch] + value[:, ch:]
    pooled = pool_rows[pl.ds(0, half * half, stride=2), :] + pool_rows[pl.ds(1, half * half, stride=2), :]
    energy[...] = (pooled * (0.25 * active)).reshape(half, half, ch)

    def first_copy(j):
        return remote(dk.at[j, :, 1 - c], first.at[j], one_out.at[j], one_in.at[j], sibling)

    def second_copy(j, d):
        return remote(
            summed.at[j, zed(d)], second.at[j, d - 1], two_out.at[j, d - 1], two_in.at[j, d - 1], at_z(d)
        )

    def third_copy(j):
        d = jnp.maximum(jnp.bitwise_xor(s, j) - 1, 0)
        return remote(total.at[j], third.at[d], three_out.at[j], three_in.at[d], (j, p))

    def near_copy(j, k):
        return remote(
            summed.at[j, zed(3 - 2 * k)], near.at[j, k], near_out.at[j, k], near_in.at[j, k], at_z(1)
        )

    def wide_copy(j, k):
        d = jnp.maximum(jnp.bitwise_xor(s, j) - 1, 0)
        return remote(paired.at[j, k], wide.at[d, k], wide_out.at[j, k], wide_in.at[d, k], (j, p))

    def last_copy():
        return remote(joined, last, last_sems.at[0], last_sems.at[1], at_z(2))

    def first_sum(j):
        first_copy(j).wait_recv()
        summed[j] = (dk[j, :, c].astype(F32) + first[j].astype(F32)).astype(BF16)
        if modes[j] == "z":
            for d in reversed(range(1, nz)):
                send(second_copy(j, d))
        else:
            for k in range(2):
                send(near_copy(j, k))

    def near_sum(j):
        for k in range(2):
            near_copy(j, k).wait_recv()
            paired[j, k] = (summed[j, zed(2 - 2 * k)].astype(F32) + near[j, k].astype(F32)).astype(BF16)
            pl.when(s != j)(lambda: wide_copy(j, k).start())

    def wide_sum(k):
        value = paired[s, k].astype(F32)
        for d in range(1, nsec):
            remote(paired.at[0, k], wide.at[d - 1, k], wide_out.at[0, k], wide_in.at[d - 1, k], sibling).wait_recv()
            value += wide[d - 1, k].astype(F32)
        return value

    def second_sum(j):
        value = summed[j, z].astype(F32)
        for d in range(1, nz):
            second_copy(j, d).wait_recv()
            value += second[j, d - 1].astype(F32)
        total[j] = value.astype(BF16)
        pl.when(s != j)(lambda: third_copy(j).start())

    by_z = [j for j in range(KERNELS) if modes[j] == "z"]
    by_near = [j for j in range(KERNELS) if modes[j] != "z"]

    def is_one_of(kernels):
        found = s < 0
        for j in kernels:
            found = jnp.logical_or(found, s == j)
        return found

    lines = []
    for j in reversed(range(KERNELS)):
        scale = twice(scales[j : j + 1])
        gain_sum = jnp.zeros((1, 2 * ch), F32)
        bias_sum = jnp.zeros((1, 2 * ch), F32)
        for pair, span in spans:
            upstream = twice(up_rows[span]) if j == KERNELS - 1 else slopes[j + 1, span]
            pre = upstream * slopes[j, span]
            gain_sum += jnp.sum(pre * raws[j, span], axis=0, keepdims=True)
            bias_sum += jnp.sum(pre, axis=0, keepdims=True)
            put_patches(grads, pair, pre * scale, side, ch)
        sigma = sigmas[j : j + 1]
        gain_row = (gain_sum[:, :ch] + gain_sum[:, ch:]) / sigma
        lines.append((j, gain_row))
        lines.append((4 + j, bias_sum[:, :ch] + bias_sum[:, ch:]))
        lines.append((8 + j, -gain_row * gains[j : j + 1] / sigma))
        if j == 0:
            tile = jnp.zeros((TILE, ch), F32)
            for index, value in lines:
                tile = jnp.where(line == index, value, tile)
            tiles[p] = tile
            for d in range(1, nsp):
                send(remote(tiles.at[p], tiles.at[p], tile_out.at[d - 1], tile_in.at[p], at_sp(d)))
        if j < KERNELS - 1:
            first_sum(j + 1)
        inputs = patches[j, 1 : half + 1].reshape(2 * half * side, 3 * ch)
        centre = grads[...].reshape(2 * half + 4, side, 3 * ch)[:, :, ch : 2 * ch]
        shifted = [centre[3 - a : 3 - a + 2 * half] for a in range(3)]
        shifted = jnp.concatenate(shifted, -1).reshape(2 * half * side, 3 * ch)
        grad = dot(inputs, shifted, TN)
        grad = jnp.concatenate([grad[:, a * ch : (a + 1) * ch] for a in range(3)], 0).astype(BF16)
        for b in range(nz):
            for e in range(2):
                at = (2 * b + e) * rows
                dk[j, b, e] = grad[at : at + rows]
        send(first_copy(j))
        down = dot(patch_rows(grads, half), pair_weights_back(kernel_of(j)), NT)
        if j == 2:
            down = (down + twice(up_rows[...])).astype(BF16).astype(F32)
            raws[2] = down
        if j > 0:
            slopes[j] = down
        else:
            down = (down + raws[2]).astype(BF16)
            for q in range(nsp):
                for e in range(2):
                    part = down[q * per * side : (q + 1) * per * side, e * ch : (e + 1) * ch]
                    back[q, :, e] = part.reshape(per, side, ch)
    first_sum(0)

    own_back = pltpu.make_async_copy(back.at[p], returned.at[p], local.at[7])
    own_back.start()
    for d in range(1, nsp):
        q = jnp.bitwise_xor(p, d)
        send(remote(back.at[q], returned.at[p], back_out.at[d - 1], back_in.at[p], at_sp(d)))

    for j in sorted(by_z)[1:]:
        second_sum(j)
    for j in reversed(by_near):
        near_sum(j)
    for d in range(1, nsp):
        q = jnp.bitwise_xor(p, d)
        remote(tiles.at[q], tiles.at[q], tile_out.at[d - 1], tile_in.at[q], sibling).wait_recv()
    spread = nsp * TILE
    column = lax.broadcasted_iota(jnp.int32, (24, spread), 1)
    row = lax.broadcasted_iota(jnp.int32, (24, spread), 0)
    entry = jnp.bitwise_and(column, TILE - 1)
    owner = jnp.right_shift(column, 4)
    tag = jnp.zeros((24, spread), jnp.int32)
    for q in range(nsp):
        tag = jnp.where(owner == q, tags[:, q : q + 1], tag)
    gathered = tiles[...].reshape(spread, ch)
    upper = row >= count
    kind = row - jnp.where(upper, count, 0)
    for blk in range(nsec):
        slot = 2 * blk + jnp.where(upper, 1, 0)
        chosen = (row < 2 * count) & (entry == slot) & (tag == kind)
        chosen |= (row >= 2 * count) & (entry == 8 + row - 2 * count)
        tables[blk] = dot(jnp.where(chosen, 1.0, 0.0), gathered, NN, HIGHEST)
    for d in range(1, nsec):
        send(remote(tables.at[sec(d)], tables_in.at[d - 1], table_out_sem.at[d - 1], table_in_sem.at[d - 1], at_section(d)))
    @pl.when(is_one_of(by_near))
    def _():
        joined[...] = wide_sum(0).astype(BF16)
        last_copy().start()

    second_sum(min(by_z))

    table = tables[s]
    for d in range(1, nsec):
        remote(tables.at[sec(d)], tables_in.at[d - 1], table_out_sem.at[d - 1], table_in_sem.at[d - 1], at_section(d)).wait_recv()
        table += tables_in[d - 1]
    table_out[...] = table

    mine = pieces[s, z, c].astype(F32)
    proj = jnp.sum(mine * vector, axis=1, keepdims=True)
    q_row = rows_ref[pl.ds(8 + s, 1)]
    length = jnp.sqrt(rows_ref[pl.ds(12 + s, 1)][:, 0:1] + 1e-06)
    unit = q_row / length
    sigma = jnp.sqrt(jnp.sum(unit * unit, axis=1, keepdims=True) + 1e-06)
    along = unit / sigma
    reach = jnp.sum(mine * along, axis=1, keepdims=True)
    crossing = jnp.sum(q_row * along, axis=1, keepdims=True)
    slope = (reach - proj * (crossing / (length * length))) / length
    dsigma = table_out[pl.ds(2 * count + s, 1)]
    dsigma = jnp.sum(dsigma, axis=1, keepdims=True)
    weight_out[...] = dsigma * ((proj / length) * along + slope * vector)

    @pl.when(is_one_of(by_z))
    def _():
        value = weight_out[...] + total[s].astype(F32)
        for d in range(1, nsec):
            remote(total.at[0], third.at[d - 1], three_out.at[0], three_in.at[d - 1], sibling).wait_recv()
            value += third[d - 1].astype(F32)
        weight_out[...] = value

    @pl.when(is_one_of(by_near))
    def _():
        value = weight_out[...] + wide_sum(1)
        last_copy().wait_recv()
        weight_out[...] = value + last[...].astype(F32)
        last_copy().wait_send()

    for d in range(1, nsp):
        q = jnp.bitwise_xor(p, d)
        remote(back.at[q], returned.at[q], back_out.at[d - 1], back_in.at[q], sibling).wait_recv()
    own_back.wait()
    for copy in sends:
        copy.wait_send()
    for j in by_z:
        pl.when(s != j)(lambda j=j: third_copy(j).wait_send())
    for j in by_near:
        for k in range(2):
            pl.when(s != j)(lambda j=j, k=k: wide_copy(j, k).wait_send())


def finish_kernel(count, energy_in, returned, weight_in, table, energy, grad, weight, affine, wide, sems):
    copies = [
        pltpu.make_async_copy(energy_in, energy, sems.at[0]),
        pltpu.make_async_copy(weight_in, weight, sems.at[1]),
    ]
    for copy in copies:
        copy.start()
    for i in range(returned.shape[0]):
        wide[i] = returned[i].astype(F32)
        copies.append(pltpu.make_async_copy(wide.at[i], grad.at[i], sems.at[2 + i]))
        copies[-1].start()
    ch = table.shape[1]
    p = lax.axis_index("sp")
    start = 5 * p // 2
    block = table[pl.ds(start, 3)]
    odd = jnp.full((1, ch), p % 2, jnp.int32) == 1
    middle = ch // 2
    swapped = [jnp.concatenate([block[i : i + 1, middle:], block[i : i + 1, :middle]], 1) for i in range(3)]
    low = lax.broadcasted_iota(jnp.int32, (1, ch), 1) < middle
    later = [jnp.where(low, swapped[i], swapped[i + 1]) for i in range(2)]
    affine[pl.ds(0, ch)] = jnp.where(odd, later[0], block[0:1]).reshape(ch)
    affine[pl.ds(ch, ch)] = jnp.where(odd, later[1], block[1:2]).reshape(ch)
    affine[pl.ds(2 * ch, middle)] = jnp.where(odd, swapped[2], block[2:3])[:, :middle].reshape(middle)
    for copy in copies:
        copy.wait()


def whole_body(images, labels, chain_steps, conv_weights, class_affine, power_vectors, cotangent):
    nsec, nsp = lax.axis_size("section"), lax.axis_size("sp")
    nz = nsp // 2
    own, band, side, ch = images.shape
    half = side // 2
    rows = conv_weights.shape[0] // ch
    share = class_affine.shape[0]
    count = share * nsec * nsp // (2 * KERNELS * ch)
    anywhere = pl.BlockSpec(memory_space=pl.ANY)
    vmem = pl.BlockSpec(memory_space=pltpu.VMEM)
    pixels = half * side
    dma = pltpu.SemaphoreType.DMA
    results = pl.pallas_call(
        partial(whole_kernel, nsec, nz, count, LANGEVIN_T, MODES),
        out_shape=[
            pltpu.VMEM((half, half, ch), F32),
            pltpu.VMEM((own, band // 2, 2, side, ch), BF16),
            pltpu.VMEM((rows, ch), F32),
            pltpu.VMEM((24, ch), F32),
        ],
        in_specs=[anywhere] * 7,
        out_specs=[vmem] * 4,
        scratch_shapes=[
            pltpu.VMEM(labels.shape[::-1], jnp.int32),
            pltpu.VMEM(chain_steps.shape, jnp.int32),
            pltpu.VMEM((rows, ch), F32),
            pltpu.VMEM((share,), F32),
            pltpu.VMEM(power_vectors.shape, F32),
            pltpu.VMEM((half, half, ch), BF16),
            pltpu.VMEM((nsec, nz, 2, rows, ch), BF16),
            pltpu.VMEM((nsec, nz, 2, TILE, ch), BF16),
            pltpu.VMEM((nsp, band, side, ch), BF16),
            pltpu.VMEM((KERNELS, half + 2, 2, side, 3 * ch), BF16),
            pltpu.VMEM((half + 2, 2, side, 3 * ch), BF16),
            pltpu.VMEM((KERNELS, pixels, 2 * ch), F32),
            pltpu.VMEM((KERNELS, pixels, 2 * ch), F32),
            pltpu.VMEM((pixels, ch), F32),
            pltpu.VMEM((pixels, ch), F32),
            pltpu.VMEM((TILE, ch), F32),
            pltpu.VMEM((KERNELS, nz, 2, rows, ch), BF16),
            pltpu.VMEM((KERNELS, nz, rows, ch), BF16),
            pltpu.VMEM((KERNELS, nz, rows, ch), BF16),
            pltpu.VMEM((KERNELS, nz - 1, rows, ch), BF16),
            pltpu.VMEM((KERNELS, rows, ch), BF16),
            pltpu.VMEM((nsec - 1, rows, ch), BF16),
            pltpu.VMEM((KERNELS, 2, rows, ch), BF16),
            pltpu.VMEM((KERNELS, 2, rows, ch), BF16),
            pltpu.VMEM((nsec - 1, 2, rows, ch), BF16),
            pltpu.VMEM((rows, ch), BF16),
            pltpu.VMEM((rows, ch), BF16),
            pltpu.VMEM((nsp, band // 2, 2, side, ch), BF16),
            pltpu.VMEM((nsp, TILE, ch), F32),
            pltpu.VMEM((nsec, 24, ch), F32),
            pltpu.VMEM((nsec - 1, 24, ch), F32),
            dma((8,)),
            dma((nsec, nz, 2)),
            dma((nz - 1,)),
            dma((nz, nsec - 1)),
            dma((nz,)),
            dma((nsec, nz)),
            dma((nsec + nz - 1,)),
            dma((nsec + nz - 1,)),
            dma((nsp - 1,)),
            dma((nsp,)),
            dma((KERNELS,)),
            dma((KERNELS,)),
            dma((KERNELS, nz - 1)),
            dma((KERNELS, nz - 1)),
            dma((KERNELS,)),
            dma((nsec - 1,)),
            dma((KERNELS, 2)),
            dma((KERNELS, 2)),
            dma((KERNELS, 2)),
            dma((nsec - 1, 2)),
            dma((2,)),
            dma((nsp - 1,)),
            dma((nsp,)),
            dma((nsp - 1,)),
            dma((nsp,)),
            dma((nsec - 1,)),
            dma((nsec - 1,)),
        ],
        compiler_params=pltpu.CompilerParams(
            collective_id=0, has_side_effects=True, vmem_limit_bytes=56 * 2**20
        ),
    )(
        images,
        labels.reshape(labels.shape[::-1]),
        chain_steps,
        conv_weights.reshape(rows, ch),
        class_affine,
        power_vectors,
        cotangent.reshape(half, half, ch),
    )
    energy, returned, weight_grad, affine_grad = pl.pallas_call(
        partial(finish_kernel, count),
        out_shape=[
            jax.ShapeDtypeStruct((half, half, ch), F32),
            jax.ShapeDtypeStruct((own, band // 2, 2, side, ch), F32),
            jax.ShapeDtypeStruct((rows, ch), F32),
            jax.ShapeDtypeStruct((share,), F32),
        ],
        in_specs=[vmem] * 4,
        out_specs=[anywhere] * 3 + [vmem],
        scratch_shapes=[pltpu.VMEM((own, band // 2, 2, side, ch), F32), dma((own + 2,))],
    )(*(pltpu.with_memory_space_constraint(r, pltpu.VMEM) for r in results))
    return (
        energy[None],
        returned.reshape(own, band, side, ch),
        weight_grad.reshape(-1),
        affine_grad,
    )


def body(images, labels, chain_steps, conv_weights, class_affine, power_vectors, cotangent):
    nsec, nsp = lax.axis_size("section"), lax.axis_size("sp")
    channels = images.shape[3]
    rows = conv_weights.shape[0] // channels
    fits = (
        nsec == KERNELS
        and nsp == 8
        and images.shape[0] == nsp
        and images.shape[1] * nsp == images.shape[2]
        and images.shape[1] % 2 == 0
        and chain_steps.shape == (1, 1)
        and rows % 16 == 0
        and class_affine.shape[0] * 2 == 5 * channels
    )
    chosen = whole_body if fits else general_body
    return chosen(
        images, labels, chain_steps, conv_weights, class_affine, power_vectors, cotangent
    )


def solution(mesh):
    in_specs = (
        P("section", "sp", None, None),
        P("section", None),
        P(("section", "sp"), None),
        P(("section", "sp")),
        P(("section", "sp")),
        P(),
        P(("section", "sp"), None, None, None),
    )
    out_specs = (
        P(("section", "sp"), None, None, None),
        P("section", "sp", None, None),
        P(("section", "sp")),
        P(("section", "sp")),
    )
    return jax.shard_map(body, mesh=mesh, in_specs=in_specs, out_specs=out_specs, check_vma=False)
```

```python
from functools import partial

import jax
import jax.numpy as jnp
from jax import lax
from jax.experimental import pallas as pl
from jax.experimental.pallas import tpu as pltpu
from jax.sharding import PartitionSpec as P

LANGEVIN_T = 40


HIGHEST = lax.Precision.HIGHEST


def extended_2(block, sides, width):
    for axis, dim in sides:
        count = lax.axis_size(axis)
        forward = [(i, i + 1) for i in range(count - 1)]
        backward = [(target, source) for source, target in forward]
        low = lax.ppermute(
            lax.slice_in_dim(block, block.shape[dim] - width, None, axis=dim), axis, forward
        )
        high = lax.ppermute(lax.slice_in_dim(block, 0, width, axis=dim), axis, backward)
        block = jnp.concatenate([low, block, high], axis=dim)
    return block


def leaky(value):
    return 0.2 * value + 0.8 * jax.nn.softplus(value)


def leaky_slope(value):
    return 0.2 + 0.8 * jax.nn.sigmoid(value)


def spectral(matrix, vector):
    forward = jnp.dot(matrix, vector, precision=HIGHEST)
    unit = forward / jnp.sqrt(jnp.sum(forward * forward) + 1e-06)
    backward = jnp.dot(unit, matrix, precision=HIGHEST)
    return jnp.sqrt(jnp.sum(backward * backward) + 1e-06)


def taps(padded, kernel):
    return lax.conv_general_dilated(
        padded,
        kernel,
        (1, 1),
        "VALID",
        dimension_numbers=("NHWC", "HWIO", "NHWC"),
        preferred_element_type=jnp.float32,
    )


def kernel_grad(padded, grad):
    result = lax.conv_general_dilated(
        padded,
        grad,
        (1, 1),
        "VALID",
        dimension_numbers=("CHWN", "IHWO", "NHWC"),
        preferred_element_type=jnp.float32,
    )
    return jnp.transpose(result, (1, 2, 0, 3))


def flipped(kernel):
    return jnp.transpose(jnp.flip(kernel, (0, 1)), (0, 1, 3, 2))


def trim_rims(extended, band, side):
    start = lax.axis_index("sp") * band
    keep_top = jnp.where(start % side == 0, 0.0, 1.0).astype(extended.dtype)
    keep_bottom = jnp.where((start + band) % side == 0, 0.0, 1.0).astype(extended.dtype)
    merged = jnp.concatenate(
        [extended[:, :1] * keep_top, extended[:, 1:-1], extended[:, -1:] * keep_bottom], axis=1
    )
    return jnp.pad(merged, ((0, 0), (0, 0), (1, 1), (0, 0)))


def rows_forward(values, band, side):
    extended = extended_2(values, (("sp", 1),), 1)
    return trim_rims(extended, band, side)


def rows_backward(values, band, side):
    extended = extended_2(values, (("sp", 1),), 1)
    return trim_rims(extended, band, side)


def pad_whole(values):
    return jnp.pad(values, ((0, 0), (1, 1), (1, 1), (0, 0)))


def affine_terms(upstream, raw, value, scale, gain, sigma):
    pre = upstream * leaky_slope(value)
    grad_raw = (pre * scale[:, None, None, :]).astype(jnp.bfloat16)
    grad_gain = jnp.sum(pre * raw, axis=(1, 2)) / sigma
    grad_bias = jnp.sum(pre, axis=(1, 2))
    grad_sigma = -jnp.sum(grad_gain * gain) / sigma
    return (grad_raw, grad_gain, grad_bias, grad_sigma)


def general_body(images, labels, chain_steps, conv_weights, class_affine, power_vectors, cotangent):
    channels = images.shape[3]
    band = images.shape[1]
    side = images.shape[2]
    half = side // 2
    across = labels.shape[1]
    groups = chain_steps.shape[0]
    gathered_w, gathered_a = (
        lax.all_gather(conv_weights.astype(jnp.bfloat16), ("section", "sp"), axis=0, tiled=True),
        lax.all_gather(class_affine.astype(jnp.bfloat16), ("section", "sp"), axis=0, tiled=True),
    )
    kernels = gathered_w.reshape(4, 3, 3, channels, channels)
    table = gathered_a.astype(jnp.float32).reshape(2, 4, -1, channels)
    count = table.shape[2]
    matrices = kernels.astype(jnp.float32).reshape(4, 9 * channels, channels)
    sigmas = [spectral(matrices[j], power_vectors[j]) for j in range(4)]
    kinds = jnp.arange(count)
    start = lax.axis_index("sp") * groups
    tags_second = lax.dynamic_slice_in_dim(labels, start, groups, 0).reshape(-1)
    onehot_second = (tags_second[:, None] == kinds[None, :]).astype(jnp.float32)
    active = (chain_steps.reshape(-1) > LANGEVIN_T).astype(jnp.float32)
    column = lax.axis_index("sp") * band // side
    picks = jnp.arange(across) == column
    tags_first = jnp.sum(jnp.where(picks[None, :], labels, 0), axis=1)
    onehot_first = (tags_first[:, None] == kinds[None, :]).astype(jnp.float32)
    pad_forward = partial(rows_forward, band=band, side=side)
    pad_backward = partial(rows_backward, band=band, side=side)
    gains_first = jnp.einsum("nk,jkc->jnc", onehot_first, table[0], precision=HIGHEST)
    biases_first = jnp.einsum("nk,jkc->jnc", onehot_first, table[1], precision=HIGHEST)
    gains_second = jnp.einsum("nk,jkc->jnc", onehot_second, table[0], precision=HIGHEST)
    biases_second = jnp.einsum("nk,jkc->jnc", onehot_second, table[1], precision=HIGHEST)
    scales = [
        gains_first[0] / sigmas[0],
        gains_first[1] / sigmas[1],
        gains_second[2] / sigmas[2],
        gains_second[3] / sigmas[3],
    ]
    input_pad = pad_forward(images)
    raw_zero = taps(input_pad, kernels[0])
    pre_zero = raw_zero * scales[0][:, None, None, :] + biases_first[0][:, None, None, :]
    hidden_zero = leaky(pre_zero).astype(jnp.bfloat16)
    hidden_pad = pad_forward(hidden_zero)
    raw_one = taps(hidden_pad, kernels[1])
    pre_one = raw_one * scales[1][:, None, None, :] + biases_first[1][:, None, None, :]
    first_out = images.astype(jnp.float32) + leaky(pre_one)
    moved = lax.all_to_all(
        first_out.astype(jnp.bfloat16), "sp", split_axis=0, concat_axis=1, tiled=True
    )
    whole = moved.reshape(groups * across, side, side, channels)
    whole_pad = pad_whole(whole)
    raw_two = taps(whole_pad, kernels[2])
    pre_two = raw_two * scales[2][:, None, None, :] + biases_second[2][:, None, None, :]
    hidden_two = leaky(pre_two).astype(jnp.bfloat16)
    hidden_two_pad = pad_whole(hidden_two)
    raw_three = taps(hidden_two_pad, kernels[3])
    pre_three = raw_three * scales[3][:, None, None, :] + biases_second[3][:, None, None, :]
    second_out = whole.astype(jnp.float32) + leaky(pre_three)
    pooled = (
        jnp.mean(second_out.reshape(-1, half, 2, half, 2, channels), axis=(2, 4))
        * active[:, None, None, None]
    )
    energy = pooled.reshape(groups, across * half, half, channels)
    upstream = (
        cotangent.astype(jnp.float32).reshape(-1, half, half, channels)
        * (0.25 * active)[:, None, None, None]
    )
    images_n = upstream.shape[0]
    grad_out = jnp.broadcast_to(
        upstream[:, :, None, :, None, :], (images_n, half, 2, half, 2, channels)
    ).reshape(images_n, side, side, channels)
    dz_three, dg_three, db_three, dsig_three = affine_terms(
        grad_out, raw_three, pre_three, scales[3], gains_second[3], sigmas[3]
    )
    kg_three = kernel_grad(hidden_two_pad, dz_three)
    grad_hidden = taps(pad_whole(dz_three), flipped(kernels[3]))
    dz_two, dg_two, db_two, dsig_two = affine_terms(
        grad_hidden, raw_two, pre_two, scales[2], gains_second[2], sigmas[2]
    )
    kg_two = kernel_grad(whole_pad, dz_two)
    grad_whole = grad_out + taps(pad_whole(dz_two), flipped(kernels[2]))
    back_rows = grad_whole.astype(jnp.bfloat16).reshape(groups, across * side, side, channels)
    returned = lax.all_to_all(back_rows, "sp", split_axis=1, concat_axis=0, tiled=True)
    grad_first = returned.astype(jnp.float32)
    dz_one, dg_one, db_one, dsig_one = affine_terms(
        grad_first, raw_one, pre_one, scales[1], gains_first[1], sigmas[1]
    )
    kg_one = kernel_grad(hidden_pad, dz_one)
    grad_hidden_first = taps(pad_backward(dz_one), flipped(kernels[1]))
    dz_zero, dg_zero, db_zero, dsig_zero = affine_terms(
        grad_hidden_first, raw_zero, pre_zero, scales[0], gains_first[0], sigmas[0]
    )
    kg_zero = kernel_grad(input_pad, dz_zero)
    local_grad = grad_first + taps(pad_backward(dz_zero), flipped(kernels[0]))
    conv_grads = [kg_zero, kg_one, kg_two, kg_three]
    sigma_grads = [dsig_zero, dsig_one, dsig_two, dsig_three]
    pieces = []
    for index in range(4):
        unused, pullback = jax.vjp(partial(spectral, vector=power_vectors[index]), matrices[index])
        pieces.append(
            conv_grads[index].reshape(9 * channels, channels) + pullback(sigma_grads[index])[0]
        )
    weight_total = jnp.stack(pieces).reshape(-1)
    gain_rows = [
        jnp.einsum("nk,nc->kc", onehot_first, dg_zero, precision=HIGHEST),
        jnp.einsum("nk,nc->kc", onehot_first, dg_one, precision=HIGHEST),
        jnp.einsum("nk,nc->kc", onehot_second, dg_two, precision=HIGHEST),
        jnp.einsum("nk,nc->kc", onehot_second, dg_three, precision=HIGHEST),
    ]
    bias_rows = [
        jnp.einsum("nk,nc->kc", onehot_first, db_zero, precision=HIGHEST),
        jnp.einsum("nk,nc->kc", onehot_first, db_one, precision=HIGHEST),
        jnp.einsum("nk,nc->kc", onehot_second, db_two, precision=HIGHEST),
        jnp.einsum("nk,nc->kc", onehot_second, db_three, precision=HIGHEST),
    ]
    affine_total = jnp.stack([jnp.stack(gain_rows), jnp.stack(bias_rows)]).reshape(-1)
    weight_grad, affine_grad = (
        lax.psum_scatter(weight_total, ("section", "sp"), scatter_dimension=0, tiled=True),
        lax.psum_scatter(affine_total, ("section", "sp"), scatter_dimension=0, tiled=True),
    )
    return (energy, local_grad, weight_grad, affine_grad)

F32 = jnp.float32
BF16 = jnp.bfloat16
MESH = pl.DeviceIdType.MESH
NN = (((1,), (0,)), ((), ()))
NT = (((1,), (1,)), ((), ()))
TN = (((0,), (0,)), ((), ()))
KERNELS = 4
MODES = ("z", "h", "h", "h")
TILE = 16


def dot(left, right, dims, precision=None):
    return lax.dot_general(left, right, dims, precision=precision, preferred_element_type=F32)


def twice(row):
    return jnp.concatenate([row, row], 1)


def beside(value, side):
    rows = value.shape[0]
    column = lax.broadcasted_iota(jnp.int32, (rows, 1), 0) % side
    left = jnp.where(column == 0, 0.0, pltpu.roll(value, 1, 0))
    right = jnp.where(column == side - 1, 0.0, pltpu.roll(value, rows - 1, 0))
    return (left, value, right)


def put_patches(ref, pair, value, side, ch):
    count = value.shape[0] // side
    rows = pl.ds(pair + 1, count)
    for b, part in enumerate(beside(value, side)):
        part = part.astype(BF16)
        for e in range(2):
            half = part[:, e * ch : (e + 1) * ch].reshape(count, side, ch)
            ref[rows, e, :, b * ch : (b + 1) * ch] = half


def patch_rows(ref, at, count):
    side, width = ref.shape[2], ref.shape[3]
    end = at + count
    parts = [ref[at:end, 1], ref[at + 1 : end + 1, 0], ref[at + 1 : end + 1, 1], ref[at + 2 : end + 2, 0]]
    return jnp.concatenate(parts, -1).reshape(count * side, 4 * width)


def pair_weights(kernel):
    rows = kernel.shape[0] // 3
    zero = jnp.zeros((rows, kernel.shape[1]), kernel.dtype)
    a, b, c = (kernel[i * rows : (i + 1) * rows] for i in range(3))
    pairs = ((a, zero), (b, a), (c, b), (zero, c))
    return jnp.concatenate([jnp.concatenate(pair, 1) for pair in pairs], 0)


def pair_weights_back(kernel):
    ch = kernel.shape[1]
    zero = jnp.zeros((ch, ch), kernel.dtype)
    blocks = []
    for e in range(2):
        row = []
        for r in range(4):
            for b in range(3):
                a = 2 - (r - e)
                tap = (a * 3 + 2 - b) * ch
                row.append(kernel[tap : tap + ch] if 0 <= a <= 2 else zero)
        blocks.append(jnp.concatenate(row, 1))
    return jnp.concatenate(blocks, 0)


def leaky_terms(value):
    small = jnp.exp(-jnp.abs(value))
    result = 0.2 * value + 0.8 * (jnp.maximum(value, 0.0) + jnp.log(1.0 + small))
    return result, 0.6 + 0.4 * jnp.tanh(0.5 * value)


def halves(pairs, ch):
    wide = jnp.concatenate([pairs[:, 0], pairs[:, 1]], -1)
    return wide.reshape(-1, 2 * ch)


def three(row):
    high = row.astype(BF16).astype(F32)
    middle = (row - high).astype(BF16).astype(F32)
    return (high, middle, row - high - middle)


def whole_kernel(
    nsec, nz, count, active_above, modes,
    images, labels_in, steps_in, weights_in, affine_in, vectors_in, cotangent_in,
    energy, returned, weight_out, table_out,
    labels, steps, weights, affine, vectors, cotangent,
    pieces, lines_all, xin, patches, grads, back_weights, raws, slopes, up_rows, pool_rows, rows_ref,
    dk, first, summed, second, total, third, near, paired, wide, joined, last, back, tiles, tables, tables_in,
    local, piece_in, piece_z, piece_s, piece_c, piece_k, line_out, line_in, image_out, image_in,
    one_out, one_in, two_out, two_in, three_out, three_in, near_out, near_in, wide_out, wide_in, last_sems,
    back_out, back_in, tile_out, tile_in, table_out_sem, table_in_sem,
):
    nsp = 2 * nz
    side, ch = images.shape[2], images.shape[3]
    band = images.shape[1]
    half = side // 2
    rows = weights.shape[0]
    s = lax.axis_index("section")
    p = lax.axis_index("sp")
    z = p // 2
    c = p % 2

    def sec(d):
        return jnp.bitwise_xor(s, d)

    def zed(d):
        return jnp.bitwise_xor(z, d)

    def remote(src, dst, out_sem, in_sem, where):
        return pltpu.make_async_remote_copy(
            src_ref=src, dst_ref=dst, send_sem=out_sem, recv_sem=in_sem,
            device_id=where, device_id_type=MESH,
        )

    sibling = (s, p + 1 - 2 * c)

    def at_section(d):
        return (sec(d), p)

    def at_z(d):
        return (s, 2 * zed(d) + c)

    def at_sp(d):
        return (s, jnp.bitwise_xor(p, d))

    barrier = pltpu.get_barrier_semaphore()
    for d in range(1, nsec):
        pl.semaphore_signal(barrier, inc=1, device_id=at_section(d), device_id_type=MESH)
    for d in range(1, nsp):
        pl.semaphore_signal(barrier, inc=1, device_id=at_sp(d), device_id_type=MESH)

    arrivals = [
        pltpu.make_async_copy(src, dst, local.at[i])
        for i, (src, dst) in enumerate((
            (weights_in, weights), (vectors_in, vectors), (affine_in, affine), (labels_in, labels),
            (steps_in, steps), (cotangent_in, cotangent), (images.at[p], xin.at[p]),
        ))
    ]
    for copy in arrivals:
        copy.start()

    patches[:, 0:1] = jnp.zeros_like(patches[:, 0:1])
    patches[:, half + 1 :] = jnp.zeros_like(patches[:, half + 1 :])
    grads[:, 0:1] = jnp.zeros_like(grads[:, 0:1])
    grads[:, half + 1 :] = jnp.zeros_like(grads[:, half + 1 :])

    for copy in arrivals[:3]:
        copy.wait()
    mine = weights[...].astype(BF16)
    pieces[s, z, c] = mine
    matrix = mine.astype(F32)
    vector = vectors[pl.ds(s, 1)]
    proj = jnp.sum(matrix * vector, axis=1, keepdims=True)
    crossed = jnp.sum(proj * matrix, axis=0, keepdims=True)
    norm = jnp.broadcast_to(jnp.sum(proj * proj, axis=0, keepdims=True), (1, ch))
    cuts = ((0, ch), (ch, ch), (2 * ch, ch // 2))
    flat = jnp.concatenate([affine[pl.ds(at, n)].reshape(1, n) for at, n in cuts], 1)
    flat = flat.astype(BF16).astype(F32)
    hollow = jnp.zeros((1, ch // 2), F32)
    even = [flat[:, 0:ch], flat[:, ch : 2 * ch], jnp.concatenate([flat[:, 2 * ch :], hollow], 1)]
    odd = [
        jnp.concatenate([hollow, flat[:, 0 : ch // 2]], 1),
        flat[:, ch // 2 : 3 * ch // 2],
        flat[:, 3 * ch // 2 :],
    ]
    is_odd = jnp.full((1, ch), c, jnp.int32) == 1
    lines = [jnp.where(is_odd, b, a) for a, b in zip(even, odd)] + [*three(crossed), *three(norm)]
    tile = jnp.zeros((TILE, ch), F32)
    line = lax.broadcasted_iota(jnp.int32, (TILE, ch), 0)
    for index, value in enumerate(lines):
        tile = jnp.where(line == index, value, tile)
    lines_all[s, z, c] = tile.astype(BF16)

    pl.semaphore_wait(barrier, nsec - 1 + nsp - 1)

    def piece_copy(a, b, e, out_sem, where):
        ref = pieces.at[a, b, e]
        return remote(ref, ref, out_sem, piece_in.at[a, b, e], where)

    def line_copy(ref, index, where):
        return remote(ref, ref, line_out.at[index], line_in.at[index], where)

    sends = []

    def send(copy):
        copy.start()
        sends.append(copy)

    for d in range(1, nsec):
        send(line_copy(lines_all.at[s, z, c], d - 1, at_section(d)))
    for d in range(1, nz):
        send(piece_copy(s, z, c, piece_z.at[d - 1], at_z(d)))
    for d in range(1, nsec):
        send(piece_copy(s, z, c, piece_s.at[0, d - 1], at_section(d)))
    send(piece_copy(s, z, c, piece_c.at[0], sibling))

    for copy in arrivals[3:]:
        copy.wait()
    active = jnp.where(steps[...] > active_above, 1.0, 0.0)
    pulled = cotangent[...].astype(F32).reshape(half * half, ch) * (0.25 * active)
    up_rows[pl.ds(0, half * half, stride=2), :] = pulled
    up_rows[pl.ds(1, half * half, stride=2), :] = pulled

    for d in range(1, nsec):
        line_copy(lines_all.at[sec(d), z, c], d - 1, sibling).wait_recv()
    for d in range(1, nz):
        send(line_copy(lines_all.at[:, z, c], nsec - 2 + d, at_z(d)))
    for d in range(1, nsp):
        q = jnp.bitwise_xor(p, d)
        send(remote(images.at[q], xin.at[p], image_out.at[d - 1], image_in.at[p], at_sp(d)))
    for d in range(1, nz):
        piece_copy(s, zed(d), c, piece_z.at[d - 1], sibling).wait_recv()
        for e in range(1, nsec):
            send(piece_copy(s, zed(d), c, piece_s.at[d, e - 1], at_section(e)))
        send(piece_copy(s, zed(d), c, piece_c.at[d], sibling))
    for d in range(1, nz):
        line_copy(lines_all.at[:, zed(d), c], nsec - 2 + d, sibling).wait_recv()
    lines_last = nsec + nz - 2
    send(line_copy(lines_all.at[:, :, c], lines_last, sibling))

    def pass_on(e):
        for d in range(1, nsec):
            copy = piece_copy(sec(d), zed(e), c, piece_k.at[d, e], sibling)
            copy.wait_recv()
            send(copy)

    per = band // 2

    def take_image(d):
        q = jnp.bitwise_xor(p, d)
        if d:
            remote(images.at[q], xin.at[q], image_out.at[d - 1], image_in.at[q], sibling).wait_recv()
        block = xin[q].astype(F32).reshape(per, 2, side, ch)
        put_patches(patches.at[0], q * per, halves(block, ch), side, ch)

    for e in range(nz):
        pass_on(e)
        take_image(2 * e)
        take_image(2 * e + 1)
    line_copy(lines_all.at[:, :, 1 - c], lines_last, sibling).wait_recv()

    tags = labels[...]
    at = lax.broadcasted_iota(jnp.int32, tags.shape, 1)
    label = jnp.sum(jnp.where(at == p, tags, 0).astype(F32), axis=1, keepdims=True).astype(jnp.int32)
    width = nsec * nsp * TILE
    column = lax.broadcasted_iota(jnp.int32, (TILE, width), 1)
    picked = lax.broadcasted_iota(jnp.int32, (TILE, width), 0)
    device = jnp.right_shift(column, 4)
    entry = jnp.bitwise_and(column, TILE - 1)
    wanted = picked * count + label
    at_row = jnp.right_shift(device * 5, 1) + entry
    section = jnp.right_shift(column, (nsp * TILE).bit_length() - 1)
    chosen = (picked < 8) & (entry < 3) & (at_row == wanted)
    chosen |= (picked >= 8) & (picked < 12) & (section == picked - 8) & (entry >= 3) & (entry < 6)
    chosen |= (picked >= 12) & (section == picked - 12) & (entry >= 6) & (entry < 9)
    everything = lines_all[...].reshape(width, ch)
    rows_ref[...] = dot(jnp.where(chosen, 1.0, 0.0).astype(BF16), everything, NN)
    gains, biases = rows_ref[0:4], rows_ref[4:8]
    lengths = jnp.sqrt(rows_ref[12:16] + 1e-06)
    units = rows_ref[8:12] / lengths
    sigmas = jnp.sqrt(jnp.sum(units * units, axis=1, keepdims=True) + 1e-06)
    scales = gains / sigmas

    def kernel_of(j):
        parts = [pieces[j, b, e] for b in range(nz) for e in range(2)]
        return jnp.concatenate(parts, 0)

    chunks = 8
    step = half // chunks
    spans = [(i * step, pl.ds(i * step * side, step * side)) for i in range(chunks)]
    part = half // 4
    parts = [(i * part, pl.ds(i * part * side, part * side)) for i in range(4)]

    for j in range(KERNELS):
        for b in range(nz):
            piece_copy(j, b, 1 - c, piece_c.at[0], sibling).wait_recv()
        matrix = pair_weights(kernel_of(j))
        for pair, span in parts:
            raws[j, span] = dot(patch_rows(patches.at[j], pair, part), matrix, NN)
        back_weights[j] = pair_weights_back(kernel_of(j)).T
        scale, bias = twice(scales[j : j + 1]), twice(biases[j : j + 1])
        for pair, span in spans:
            value, slope = leaky_terms(raws[j, span] * scale + bias)
            slopes[j, span] = slope
            if j % 2 == 1:
                source = patches[j - 1, pair + 1 : pair + 1 + step, :, :, ch : 2 * ch]
                value = halves(source.astype(F32), ch) + value
            if j < KERNELS - 1:
                put_patches(patches.at[j + 1], pair, value, side, ch)
            else:
                pool_rows[span] = value[:, :ch] + value[:, ch:]
    pooled = pool_rows[pl.ds(0, half * half, stride=2), :] + pool_rows[pl.ds(1, half * half, stride=2), :]
    energy[...] = (pooled * (0.25 * active)).reshape(half, half, ch)

    def first_copy(j):
        return remote(dk.at[j, :, 1 - c], first.at[j], one_out.at[j], one_in.at[j], sibling)

    def second_copy(j, d):
        return remote(
            summed.at[j, zed(d)], second.at[j, d - 1], two_out.at[j, d - 1], two_in.at[j, d - 1], at_z(d)
        )

    def third_copy(j):
        d = jnp.maximum(jnp.bitwise_xor(s, j) - 1, 0)
        return remote(total.at[j], third.at[d], three_out.at[j], three_in.at[d], (j, p))

    def near_copy(j, k):
        return remote(
            summed.at[j, zed(3 - 2 * k)], near.at[j, k], near_out.at[j, k], near_in.at[j, k], at_z(1)
        )

    def wide_copy(j, k):
        d = jnp.maximum(jnp.bitwise_xor(s, j) - 1, 0)
        return remote(paired.at[j, k], wide.at[d, k], wide_out.at[j, k], wide_in.at[d, k], (j, p))

    def last_copy():
        return remote(joined, last, last_sems.at[0], last_sems.at[1], at_z(2))

    def first_sum(j):
        first_copy(j).wait_recv()
        summed[j] = (dk[j, :, c].astype(F32) + first[j].astype(F32)).astype(BF16)
        if modes[j] == "z":
            for d in reversed(range(1, nz)):
                send(second_copy(j, d))
        else:
            for k in range(2):
                send(near_copy(j, k))

    def near_sum(j):
        for k in range(2):
            near_copy(j, k).wait_recv()
            paired[j, k] = (summed[j, zed(2 - 2 * k)].astype(F32) + near[j, k].astype(F32)).astype(BF16)
            pl.when(s != j)(lambda: wide_copy(j, k).start())

    def wide_sum(k):
        value = paired[s, k].astype(F32)
        for d in range(1, nsec):
            remote(paired.at[0, k], wide.at[d - 1, k], wide_out.at[0, k], wide_in.at[d - 1, k], sibling).wait_recv()
            value += wide[d - 1, k].astype(F32)
        return value

    def second_sum(j):
        value = summed[j, z].astype(F32)
        for d in range(1, nz):
            second_copy(j, d).wait_recv()
            value += second[j, d - 1].astype(F32)
        total[j] = value.astype(BF16)
        pl.when(s != j)(lambda: third_copy(j).start())

    by_z = [j for j in range(KERNELS) if modes[j] == "z"]
    by_near = [j for j in range(KERNELS) if modes[j] != "z"]

    def is_one_of(kernels):
        found = s < 0
        for j in kernels:
            found = jnp.logical_or(found, s == j)
        return found

    lines = []

    def tile_copy(q, k, d, where):
        return remote(tiles.at[q, k], tiles.at[q, k], tile_out.at[k, d - 1], tile_in.at[k, q], where)

    def pixel_step(j):
        scale = twice(scales[j : j + 1])
        gain_sum = jnp.zeros((1, 2 * ch), F32)
        bias_sum = jnp.zeros((1, 2 * ch), F32)
        for pair, span in spans:
            upstream = twice(up_rows[span]) if j == KERNELS - 1 else slopes[j + 1, span]
            pre = upstream * slopes[j, span]
            gain_sum += jnp.sum(pre * raws[j, span], axis=0, keepdims=True)
            bias_sum += jnp.sum(pre, axis=0, keepdims=True)
            put_patches(grads.at[j % 2], pair, pre * scale, side, ch)
        sigma = sigmas[j : j + 1]
        gain_row = (gain_sum[:, :ch] + gain_sum[:, ch:]) / sigma
        lines.append(gain_row)
        lines.append(bias_sum[:, :ch] + bias_sum[:, ch:])
        lines.append(-gain_row * gains[j : j + 1] / sigma)

    def weight_step(j):
        inputs = patches[j, 1 : half + 1].reshape(2 * half * side, 3 * ch)
        centre = grads[j % 2].reshape(2 * half + 4, side, 3 * ch)[:, :, ch : 2 * ch]
        shifted = [centre[3 - a : 3 - a + 2 * half] for a in range(3)]
        shifted = jnp.concatenate(shifted, -1).reshape(2 * half * side, 3 * ch)
        grad = dot(inputs, shifted, TN)
        grad = jnp.concatenate([grad[:, a * ch : (a + 1) * ch] for a in range(3)], 0).astype(BF16)
        for b in range(nz):
            for e in range(2):
                at = (2 * b + e) * rows
                dk[j, b, e] = grad[at : at + rows]

    def input_step(j):
        for pair, span in parts:
            down = dot(patch_rows(grads.at[j % 2], pair, part), back_weights[j], NN)
            if j == 2:
                down = (down + twice(up_rows[span])).astype(BF16).astype(F32)
                raws[2, span] = down
            if j > 0:
                slopes[j, span] = down
            else:
                down = (down + raws[2, span]).astype(BF16)
                for i in range(part // per):
                    for e in range(2):
                        block = down[i * per * side : (i + 1) * per * side, e * ch : (e + 1) * ch]
                        back[pair // per + i, :, e] = block.reshape(per, side, ch)

    for j in reversed(range(KERNELS)):
        pixel_step(j)
        if j % 2 == 0:
            tile = jnp.zeros((8, ch), F32)
            for index, value in enumerate(lines):
                tile = jnp.where(line[:8] == index, value, tile)
            lines.clear()
            k = 1 - j // 2
            tiles[p, k] = tile
            for d in range(1, nsp):
                send(tile_copy(p, k, d, at_sp(d)))
        weight_step(j)
        send(first_copy(j))
        if j < KERNELS - 1:
            first_sum(j + 1)
        input_step(j)
    first_sum(0)

    own_back = pltpu.make_async_copy(back.at[p], returned.at[p], local.at[7])
    own_back.start()
    for d in range(1, nsp):
        q = jnp.bitwise_xor(p, d)
        send(remote(back.at[q], returned.at[p], back_out.at[d - 1], back_in.at[p], at_sp(d)))

    for j in sorted(by_z)[1:]:
        second_sum(j)
    for j in reversed(by_near):
        near_sum(j)
    for d in range(1, nsp):
        q = jnp.bitwise_xor(p, d)
        for k in range(2):
            tile_copy(q, k, d, sibling).wait_recv()
    spread = nsp * TILE
    column = lax.broadcasted_iota(jnp.int32, (24, spread), 1)
    row = lax.broadcasted_iota(jnp.int32, (24, spread), 0)
    entry = jnp.bitwise_and(column, TILE - 1)
    owner = jnp.right_shift(column, 4)
    tag = jnp.zeros((24, spread), jnp.int32)
    for q in range(nsp):
        tag = jnp.where(owner == q, tags[:, q : q + 1], tag)
    gathered = tiles[...].reshape(spread, ch)
    upper = row >= count
    kind = row - jnp.where(upper, count, 0)
    spot = row - 2 * count
    sigma_slot = jnp.where(spot < 2, jnp.where(spot == 0, 13, 10), jnp.where(spot == 2, 5, 2))
    for blk in range(nsec):
        slot = (8 if blk % 2 == 0 else 0) + blk // 2 + jnp.where(upper, 0, 3)
        chosen = (spot < 0) & (entry == slot) & (tag == kind)
        chosen |= (spot >= 0) & (entry == sigma_slot)
        tables[blk] = dot(jnp.where(chosen, 1.0, 0.0), gathered, NN, HIGHEST)
    for d in range(1, nsec):
        send(remote(tables.at[sec(d)], tables_in.at[d - 1], table_out_sem.at[d - 1], table_in_sem.at[d - 1], at_section(d)))
    @pl.when(is_one_of(by_near))
    def _():
        joined[...] = wide_sum(0).astype(BF16)
        last_copy().start()

    second_sum(min(by_z))

    table = tables[s]
    for d in range(1, nsec):
        remote(tables.at[sec(d)], tables_in.at[d - 1], table_out_sem.at[d - 1], table_in_sem.at[d - 1], at_section(d)).wait_recv()
        table += tables_in[d - 1]
    table_out[...] = table

    mine = pieces[s, z, c].astype(F32)
    proj = jnp.sum(mine * vector, axis=1, keepdims=True)
    q_row = rows_ref[pl.ds(8 + s, 1)]
    length = jnp.sqrt(rows_ref[pl.ds(12 + s, 1)][:, 0:1] + 1e-06)
    unit = q_row / length
    sigma = jnp.sqrt(jnp.sum(unit * unit, axis=1, keepdims=True) + 1e-06)
    along = unit / sigma
    reach = jnp.sum(mine * along, axis=1, keepdims=True)
    crossing = jnp.sum(q_row * along, axis=1, keepdims=True)
    slope = (reach - proj * (crossing / (length * length))) / length
    dsigma = table_out[pl.ds(2 * count + s, 1)]
    dsigma = jnp.sum(dsigma, axis=1, keepdims=True)
    weight_out[...] = dsigma * ((proj / length) * along + slope * vector)

    @pl.when(is_one_of(by_z))
    def _():
        value = weight_out[...] + total[s].astype(F32)
        for d in range(1, nsec):
            remote(total.at[0], third.at[d - 1], three_out.at[0], three_in.at[d - 1], sibling).wait_recv()
            value += third[d - 1].astype(F32)
        weight_out[...] = value

    @pl.when(is_one_of(by_near))
    def _():
        value = weight_out[...] + wide_sum(1)
        last_copy().wait_recv()
        weight_out[...] = value + last[...].astype(F32)
        last_copy().wait_send()

    for d in range(1, nsp):
        q = jnp.bitwise_xor(p, d)
        remote(back.at[q], returned.at[q], back_out.at[d - 1], back_in.at[q], sibling).wait_recv()
    own_back.wait()
    for copy in sends:
        copy.wait_send()
    for j in by_z:
        pl.when(s != j)(lambda j=j: third_copy(j).wait_send())
    for j in by_near:
        for k in range(2):
            pl.when(s != j)(lambda j=j, k=k: wide_copy(j, k).wait_send())


def finish_kernel(count, energy_in, returned, weight_in, table, energy, grad, weight, affine, wide, sems):
    copies = [
        pltpu.make_async_copy(energy_in, energy, sems.at[0]),
        pltpu.make_async_copy(weight_in, weight, sems.at[1]),
    ]
    for copy in copies:
        copy.start()
    for i in range(returned.shape[0]):
        wide[i] = returned[i].astype(F32)
        copies.append(pltpu.make_async_copy(wide.at[i], grad.at[i], sems.at[2 + i]))
        copies[-1].start()
    ch = table.shape[1]
    p = lax.axis_index("sp")
    start = 5 * p // 2
    block = table[pl.ds(start, 3)]
    odd = jnp.full((1, ch), p % 2, jnp.int32) == 1
    middle = ch // 2
    swapped = [jnp.concatenate([block[i : i + 1, middle:], block[i : i + 1, :middle]], 1) for i in range(3)]
    low = lax.broadcasted_iota(jnp.int32, (1, ch), 1) < middle
    later = [jnp.where(low, swapped[i], swapped[i + 1]) for i in range(2)]
    affine[pl.ds(0, ch)] = jnp.where(odd, later[0], block[0:1]).reshape(ch)
    affine[pl.ds(ch, ch)] = jnp.where(odd, later[1], block[1:2]).reshape(ch)
    affine[pl.ds(2 * ch, middle)] = jnp.where(odd, swapped[2], block[2:3])[:, :middle].reshape(middle)
    for copy in copies:
        copy.wait()


def whole_body(images, labels, chain_steps, conv_weights, class_affine, power_vectors, cotangent):
    nsec, nsp = lax.axis_size("section"), lax.axis_size("sp")
    nz = nsp // 2
    own, band, side, ch = images.shape
    half = side // 2
    rows = conv_weights.shape[0] // ch
    share = class_affine.shape[0]
    count = share * nsec * nsp // (2 * KERNELS * ch)
    anywhere = pl.BlockSpec(memory_space=pltpu.MemorySpace.HBM)
    vmem = pl.BlockSpec(memory_space=pltpu.VMEM)
    pixels = half * side
    dma = pltpu.SemaphoreType.DMA
    results = pl.pallas_call(
        partial(whole_kernel, nsec, nz, count, LANGEVIN_T, MODES),
        out_shape=[
            pltpu.VMEM((half, half, ch), F32),
            pltpu.VMEM((own, band // 2, 2, side, ch), BF16),
            pltpu.VMEM((rows, ch), F32),
            pltpu.VMEM((24, ch), F32),
        ],
        in_specs=[anywhere] * 7,
        out_specs=[vmem] * 4,
        scratch_shapes=[
            pltpu.VMEM(labels.shape[::-1], jnp.int32),
            pltpu.VMEM(chain_steps.shape, jnp.int32),
            pltpu.VMEM((rows, ch), F32),
            pltpu.VMEM((share,), F32),
            pltpu.VMEM(power_vectors.shape, F32),
            pltpu.VMEM((half, half, ch), BF16),
            pltpu.VMEM((nsec, nz, 2, rows, ch), BF16),
            pltpu.VMEM((nsec, nz, 2, TILE, ch), BF16),
            pltpu.VMEM((nsp, band, side, ch), BF16),
            pltpu.VMEM((KERNELS, half + 2, 2, side, 3 * ch), BF16),
            pltpu.VMEM((2, half + 2, 2, side, 3 * ch), BF16),
            pltpu.VMEM((KERNELS, 12 * ch, 2 * ch), BF16),
            pltpu.VMEM((KERNELS, pixels, 2 * ch), F32),
            pltpu.VMEM((KERNELS, pixels, 2 * ch), F32),
            pltpu.VMEM((pixels, ch), F32),
            pltpu.VMEM((pixels, ch), F32),
            pltpu.VMEM((TILE, ch), F32),
            pltpu.VMEM((KERNELS, nz, 2, rows, ch), BF16),
            pltpu.VMEM((KERNELS, nz, rows, ch), BF16),
            pltpu.VMEM((KERNELS, nz, rows, ch), BF16),
            pltpu.VMEM((KERNELS, nz - 1, rows, ch), BF16),
            pltpu.VMEM((KERNELS, rows, ch), BF16),
            pltpu.VMEM((nsec - 1, rows, ch), BF16),
            pltpu.VMEM((KERNELS, 2, rows, ch), BF16),
            pltpu.VMEM((KERNELS, 2, rows, ch), BF16),
            pltpu.VMEM((nsec - 1, 2, rows, ch), BF16),
            pltpu.VMEM((rows, ch), BF16),
            pltpu.VMEM((rows, ch), BF16),
            pltpu.VMEM((nsp, band // 2, 2, side, ch), BF16),
            pltpu.VMEM((nsp, 2, 8, ch), F32),
            pltpu.VMEM((nsec, 24, ch), F32),
            pltpu.VMEM((nsec - 1, 24, ch), F32),
            dma((8,)),
            dma((nsec, nz, 2)),
            dma((nz - 1,)),
            dma((nz, nsec - 1)),
            dma((nz,)),
            dma((nsec, nz)),
            dma((nsec + nz - 1,)),
            dma((nsec + nz - 1,)),
            dma((nsp - 1,)),
            dma((nsp,)),
            dma((KERNELS,)),
            dma((KERNELS,)),
            dma((KERNELS, nz - 1)),
            dma((KERNELS, nz - 1)),
            dma((KERNELS,)),
            dma((nsec - 1,)),
            dma((KERNELS, 2)),
            dma((KERNELS, 2)),
            dma((KERNELS, 2)),
            dma((nsec - 1, 2)),
            dma((2,)),
            dma((nsp - 1,)),
            dma((nsp,)),
            dma((2, nsp - 1)),
            dma((2, nsp)),
            dma((nsec - 1,)),
            dma((nsec - 1,)),
        ],
        compiler_params=pltpu.CompilerParams(
            collective_id=0, has_side_effects=True, vmem_limit_bytes=56 * 2**20
        ),
    )(
        images,
        labels.reshape(labels.shape[::-1]),
        chain_steps,
        conv_weights.reshape(rows, ch),
        class_affine,
        power_vectors,
        cotangent.reshape(half, half, ch),
    )
    energy, returned, weight_grad, affine_grad = pl.pallas_call(
        partial(finish_kernel, count),
        out_shape=[
            jax.ShapeDtypeStruct((half, half, ch), F32),
            jax.ShapeDtypeStruct((own, band // 2, 2, side, ch), F32),
            jax.ShapeDtypeStruct((rows, ch), F32),
            jax.ShapeDtypeStruct((share,), F32),
        ],
        in_specs=[vmem] * 4,
        out_specs=[anywhere] * 3 + [vmem],
        scratch_shapes=[pltpu.VMEM((own, band // 2, 2, side, ch), F32), dma((own + 2,))],
    )(*(pltpu.with_memory_space_constraint(r, pltpu.VMEM) for r in results))
    return (
        energy[None],
        returned.reshape(own, band, side, ch),
        weight_grad.reshape(-1),
        affine_grad,
    )


def body(images, labels, chain_steps, conv_weights, class_affine, power_vectors, cotangent):
    nsec, nsp = lax.axis_size("section"), lax.axis_size("sp")
    channels = images.shape[3]
    rows = conv_weights.shape[0] // channels
    fits = (
        nsec == KERNELS
        and nsp == 8
        and images.shape[0] == nsp
        and images.shape[1] * nsp == images.shape[2]
        and images.shape[1] % 2 == 0
        and chain_steps.shape == (1, 1)
        and rows % 16 == 0
        and class_affine.shape[0] * 2 == 5 * channels
    )
    chosen = whole_body if fits else general_body
    return chosen(
        images, labels, chain_steps, conv_weights, class_affine, power_vectors, cotangent
    )


def solution(mesh):
    in_specs = (
        P("section", "sp", None, None),
        P("section", None),
        P(("section", "sp"), None),
        P(("section", "sp")),
        P(("section", "sp")),
        P(),
        P(("section", "sp"), None, None, None),
    )
    out_specs = (
        P(("section", "sp"), None, None, None),
        P("section", "sp", None, None),
        P(("section", "sp")),
        P(("section", "sp")),
    )
    return jax.shard_map(body, mesh=mesh, in_specs=in_specs, out_specs=out_specs, check_vma=False)
```

```python
from functools import partial

import jax
import jax.numpy as jnp
from jax import lax
from jax.experimental import pallas as pl
from jax.experimental.pallas import tpu as pltpu
from jax.sharding import PartitionSpec as P

LANGEVIN_T = 40


HIGHEST = lax.Precision.HIGHEST


def extended_2(block, sides, width):
    for axis, dim in sides:
        count = lax.axis_size(axis)
        forward = [(i, i + 1) for i in range(count - 1)]
        backward = [(target, source) for source, target in forward]
        low = lax.ppermute(
            lax.slice_in_dim(block, block.shape[dim] - width, None, axis=dim), axis, forward
        )
        high = lax.ppermute(lax.slice_in_dim(block, 0, width, axis=dim), axis, backward)
        block = jnp.concatenate([low, block, high], axis=dim)
    return block


def leaky(value):
    return 0.2 * value + 0.8 * jax.nn.softplus(value)


def leaky_slope(value):
    return 0.2 + 0.8 * jax.nn.sigmoid(value)


def spectral(matrix, vector):
    forward = jnp.dot(matrix, vector, precision=HIGHEST)
    unit = forward / jnp.sqrt(jnp.sum(forward * forward) + 1e-06)
    backward = jnp.dot(unit, matrix, precision=HIGHEST)
    return jnp.sqrt(jnp.sum(backward * backward) + 1e-06)


def taps(padded, kernel):
    return lax.conv_general_dilated(
        padded,
        kernel,
        (1, 1),
        "VALID",
        dimension_numbers=("NHWC", "HWIO", "NHWC"),
        preferred_element_type=jnp.float32,
    )


def kernel_grad(padded, grad):
    result = lax.conv_general_dilated(
        padded,
        grad,
        (1, 1),
        "VALID",
        dimension_numbers=("CHWN", "IHWO", "NHWC"),
        preferred_element_type=jnp.float32,
    )
    return jnp.transpose(result, (1, 2, 0, 3))


def flipped(kernel):
    return jnp.transpose(jnp.flip(kernel, (0, 1)), (0, 1, 3, 2))


def trim_rims(extended, band, side):
    start = lax.axis_index("sp") * band
    keep_top = jnp.where(start % side == 0, 0.0, 1.0).astype(extended.dtype)
    keep_bottom = jnp.where((start + band) % side == 0, 0.0, 1.0).astype(extended.dtype)
    merged = jnp.concatenate(
        [extended[:, :1] * keep_top, extended[:, 1:-1], extended[:, -1:] * keep_bottom], axis=1
    )
    return jnp.pad(merged, ((0, 0), (0, 0), (1, 1), (0, 0)))


def rows_forward(values, band, side):
    extended = extended_2(values, (("sp", 1),), 1)
    return trim_rims(extended, band, side)


def rows_backward(values, band, side):
    extended = extended_2(values, (("sp", 1),), 1)
    return trim_rims(extended, band, side)


def pad_whole(values):
    return jnp.pad(values, ((0, 0), (1, 1), (1, 1), (0, 0)))


def affine_terms(upstream, raw, value, scale, gain, sigma):
    pre = upstream * leaky_slope(value)
    grad_raw = (pre * scale[:, None, None, :]).astype(jnp.bfloat16)
    grad_gain = jnp.sum(pre * raw, axis=(1, 2)) / sigma
    grad_bias = jnp.sum(pre, axis=(1, 2))
    grad_sigma = -jnp.sum(grad_gain * gain) / sigma
    return (grad_raw, grad_gain, grad_bias, grad_sigma)


def general_body(images, labels, chain_steps, conv_weights, class_affine, power_vectors, cotangent):
    channels = images.shape[3]
    band = images.shape[1]
    side = images.shape[2]
    half = side // 2
    across = labels.shape[1]
    groups = chain_steps.shape[0]
    gathered_w, gathered_a = (
        lax.all_gather(conv_weights.astype(jnp.bfloat16), ("section", "sp"), axis=0, tiled=True),
        lax.all_gather(class_affine.astype(jnp.bfloat16), ("section", "sp"), axis=0, tiled=True),
    )
    kernels = gathered_w.reshape(4, 3, 3, channels, channels)
    table = gathered_a.astype(jnp.float32).reshape(2, 4, -1, channels)
    count = table.shape[2]
    matrices = kernels.astype(jnp.float32).reshape(4, 9 * channels, channels)
    sigmas = [spectral(matrices[j], power_vectors[j]) for j in range(4)]
    kinds = jnp.arange(count)
    start = lax.axis_index("sp") * groups
    tags_second = lax.dynamic_slice_in_dim(labels, start, groups, 0).reshape(-1)
    onehot_second = (tags_second[:, None] == kinds[None, :]).astype(jnp.float32)
    active = (chain_steps.reshape(-1) > LANGEVIN_T).astype(jnp.float32)
    column = lax.axis_index("sp") * band // side
    picks = jnp.arange(across) == column
    tags_first = jnp.sum(jnp.where(picks[None, :], labels, 0), axis=1)
    onehot_first = (tags_first[:, None] == kinds[None, :]).astype(jnp.float32)
    pad_forward = partial(rows_forward, band=band, side=side)
    pad_backward = partial(rows_backward, band=band, side=side)
    gains_first = jnp.einsum("nk,jkc->jnc", onehot_first, table[0], precision=HIGHEST)
    biases_first = jnp.einsum("nk,jkc->jnc", onehot_first, table[1], precision=HIGHEST)
    gains_second = jnp.einsum("nk,jkc->jnc", onehot_second, table[0], precision=HIGHEST)
    biases_second = jnp.einsum("nk,jkc->jnc", onehot_second, table[1], precision=HIGHEST)
    scales = [
        gains_first[0] / sigmas[0],
        gains_first[1] / sigmas[1],
        gains_second[2] / sigmas[2],
        gains_second[3] / sigmas[3],
    ]
    input_pad = pad_forward(images)
    raw_zero = taps(input_pad, kernels[0])
    pre_zero = raw_zero * scales[0][:, None, None, :] + biases_first[0][:, None, None, :]
    hidden_zero = leaky(pre_zero).astype(jnp.bfloat16)
    hidden_pad = pad_forward(hidden_zero)
    raw_one = taps(hidden_pad, kernels[1])
    pre_one = raw_one * scales[1][:, None, None, :] + biases_first[1][:, None, None, :]
    first_out = images.astype(jnp.float32) + leaky(pre_one)
    moved = lax.all_to_all(
        first_out.astype(jnp.bfloat16), "sp", split_axis=0, concat_axis=1, tiled=True
    )
    whole = moved.reshape(groups * across, side, side, channels)
    whole_pad = pad_whole(whole)
    raw_two = taps(whole_pad, kernels[2])
    pre_two = raw_two * scales[2][:, None, None, :] + biases_second[2][:, None, None, :]
    hidden_two = leaky(pre_two).astype(jnp.bfloat16)
    hidden_two_pad = pad_whole(hidden_two)
    raw_three = taps(hidden_two_pad, kernels[3])
    pre_three = raw_three * scales[3][:, None, None, :] + biases_second[3][:, None, None, :]
    second_out = whole.astype(jnp.float32) + leaky(pre_three)
    pooled = (
        jnp.mean(second_out.reshape(-1, half, 2, half, 2, channels), axis=(2, 4))
        * active[:, None, None, None]
    )
    energy = pooled.reshape(groups, across * half, half, channels)
    upstream = (
        cotangent.astype(jnp.float32).reshape(-1, half, half, channels)
        * (0.25 * active)[:, None, None, None]
    )
    images_n = upstream.shape[0]
    grad_out = jnp.broadcast_to(
        upstream[:, :, None, :, None, :], (images_n, half, 2, half, 2, channels)
    ).reshape(images_n, side, side, channels)
    dz_three, dg_three, db_three, dsig_three = affine_terms(
        grad_out, raw_three, pre_three, scales[3], gains_second[3], sigmas[3]
    )
    kg_three = kernel_grad(hidden_two_pad, dz_three)
    grad_hidden = taps(pad_whole(dz_three), flipped(kernels[3]))
    dz_two, dg_two, db_two, dsig_two = affine_terms(
        grad_hidden, raw_two, pre_two, scales[2], gains_second[2], sigmas[2]
    )
    kg_two = kernel_grad(whole_pad, dz_two)
    grad_whole = grad_out + taps(pad_whole(dz_two), flipped(kernels[2]))
    back_rows = grad_whole.astype(jnp.bfloat16).reshape(groups, across * side, side, channels)
    returned = lax.all_to_all(back_rows, "sp", split_axis=1, concat_axis=0, tiled=True)
    grad_first = returned.astype(jnp.float32)
    dz_one, dg_one, db_one, dsig_one = affine_terms(
        grad_first, raw_one, pre_one, scales[1], gains_first[1], sigmas[1]
    )
    kg_one = kernel_grad(hidden_pad, dz_one)
    grad_hidden_first = taps(pad_backward(dz_one), flipped(kernels[1]))
    dz_zero, dg_zero, db_zero, dsig_zero = affine_terms(
        grad_hidden_first, raw_zero, pre_zero, scales[0], gains_first[0], sigmas[0]
    )
    kg_zero = kernel_grad(input_pad, dz_zero)
    local_grad = grad_first + taps(pad_backward(dz_zero), flipped(kernels[0]))
    conv_grads = [kg_zero, kg_one, kg_two, kg_three]
    sigma_grads = [dsig_zero, dsig_one, dsig_two, dsig_three]
    pieces = []
    for index in range(4):
        unused, pullback = jax.vjp(partial(spectral, vector=power_vectors[index]), matrices[index])
        pieces.append(
            conv_grads[index].reshape(9 * channels, channels) + pullback(sigma_grads[index])[0]
        )
    weight_total = jnp.stack(pieces).reshape(-1)
    gain_rows = [
        jnp.einsum("nk,nc->kc", onehot_first, dg_zero, precision=HIGHEST),
        jnp.einsum("nk,nc->kc", onehot_first, dg_one, precision=HIGHEST),
        jnp.einsum("nk,nc->kc", onehot_second, dg_two, precision=HIGHEST),
        jnp.einsum("nk,nc->kc", onehot_second, dg_three, precision=HIGHEST),
    ]
    bias_rows = [
        jnp.einsum("nk,nc->kc", onehot_first, db_zero, precision=HIGHEST),
        jnp.einsum("nk,nc->kc", onehot_first, db_one, precision=HIGHEST),
        jnp.einsum("nk,nc->kc", onehot_second, db_two, precision=HIGHEST),
        jnp.einsum("nk,nc->kc", onehot_second, db_three, precision=HIGHEST),
    ]
    affine_total = jnp.stack([jnp.stack(gain_rows), jnp.stack(bias_rows)]).reshape(-1)
    weight_grad, affine_grad = (
        lax.psum_scatter(weight_total, ("section", "sp"), scatter_dimension=0, tiled=True),
        lax.psum_scatter(affine_total, ("section", "sp"), scatter_dimension=0, tiled=True),
    )
    return (energy, local_grad, weight_grad, affine_grad)

F32 = jnp.float32
BF16 = jnp.bfloat16
MESH = pl.DeviceIdType.MESH
NN = (((1,), (0,)), ((), ()))
NT = (((1,), (1,)), ((), ()))
TN = (((0,), (0,)), ((), ()))
KERNELS = 4
MODES = ("z", "h", "h", "h")
TILE = 16


def dot(left, right, dims, precision=None):
    return lax.dot_general(left, right, dims, precision=precision, preferred_element_type=F32)


def twice(row):
    return jnp.concatenate([row, row], 1)


def beside(value, side):
    rows = value.shape[0]
    column = lax.broadcasted_iota(jnp.int32, (rows, 1), 0) % side
    left = jnp.where(column == 0, 0.0, pltpu.roll(value, 1, 0))
    right = jnp.where(column == side - 1, 0.0, pltpu.roll(value, rows - 1, 0))
    return (left, value, right)


def put_patches(ref, pair, value, side, ch):
    count = value.shape[0] // side
    rows = pl.ds(pair + 1, count)
    for b, part in enumerate(beside(value, side)):
        part = part.astype(BF16)
        for e in range(2):
            half = part[:, e * ch : (e + 1) * ch].reshape(count, side, ch)
            ref[rows, e, :, b * ch : (b + 1) * ch] = half


def patch_rows(ref, at, count):
    side, width = ref.shape[2], ref.shape[3]
    end = at + count
    parts = [ref[at:end, 1], ref[at + 1 : end + 1, 0], ref[at + 1 : end + 1, 1], ref[at + 2 : end + 2, 0]]
    return jnp.concatenate(parts, -1).reshape(count * side, 4 * width)


def pair_weights(kernel):
    rows = kernel.shape[0] // 3
    zero = jnp.zeros((rows, kernel.shape[1]), kernel.dtype)
    a, b, c = (kernel[i * rows : (i + 1) * rows] for i in range(3))
    pairs = ((a, zero), (b, a), (c, b), (zero, c))
    return jnp.concatenate([jnp.concatenate(pair, 1) for pair in pairs], 0)


def pair_weights_back(kernel):
    ch = kernel.shape[1]
    zero = jnp.zeros((ch, ch), kernel.dtype)
    blocks = []
    for e in range(2):
        row = []
        for r in range(4):
            for b in range(3):
                a = 2 - (r - e)
                tap = (a * 3 + 2 - b) * ch
                row.append(kernel[tap : tap + ch] if 0 <= a <= 2 else zero)
        blocks.append(jnp.concatenate(row, 1))
    return jnp.concatenate(blocks, 0)


def leaky_terms(value):
    small = jnp.exp(-jnp.abs(value))
    result = 0.2 * value + 0.8 * (jnp.maximum(value, 0.0) + jnp.log(1.0 + small))
    return result, 0.6 + 0.4 * jnp.tanh(0.5 * value)


def halves(pairs, ch):
    wide = jnp.concatenate([pairs[:, 0], pairs[:, 1]], -1)
    return wide.reshape(-1, 2 * ch)


def three(row):
    high = row.astype(BF16).astype(F32)
    middle = (row - high).astype(BF16).astype(F32)
    return (high, middle, row - high - middle)


def whole_kernel(
    nsec, nz, count, active_above, modes,
    images, labels_in, steps_in, weights_in, affine_in, vectors_in, cotangent_in,
    energy, returned, weight_out, table_out,
    labels, steps, weights, affine, vectors, cotangent,
    pieces, lines_all, xin, patches, grads, back_weights, raws, slopes, up_rows, pool_rows, rows_ref,
    dk, first, summed, second, total, third, near, paired, wide, joined, last, back, tiles, tables, tables_in,
    local, piece_in, piece_z, piece_s, piece_c, piece_k, line_out, line_in, image_out, image_in,
    one_out, one_in, two_out, two_in, three_out, three_in, near_out, near_in, wide_out, wide_in, last_sems,
    back_out, back_in, tile_out, tile_in, table_out_sem, table_in_sem,
):
    nsp = 2 * nz
    side, ch = images.shape[2], images.shape[3]
    band = images.shape[1]
    half = side // 2
    rows = weights.shape[0]
    s = lax.axis_index("section")
    p = lax.axis_index("sp")
    z = p // 2
    c = p % 2

    def sec(d):
        return jnp.bitwise_xor(s, d)

    def zed(d):
        return jnp.bitwise_xor(z, d)

    def remote(src, dst, out_sem, in_sem, where):
        return pltpu.make_async_remote_copy(
            src_ref=src, dst_ref=dst, send_sem=out_sem, recv_sem=in_sem,
            device_id=where, device_id_type=MESH,
        )

    sibling = (s, p + 1 - 2 * c)

    def at_section(d):
        return (sec(d), p)

    def at_z(d):
        return (s, 2 * zed(d) + c)

    def at_sp(d):
        return (s, jnp.bitwise_xor(p, d))

    barrier = pltpu.get_barrier_semaphore()
    for d in range(1, nsec):
        pl.semaphore_signal(barrier, inc=1, device_id=at_section(d), device_id_type=MESH)
    for d in range(1, nsp):
        pl.semaphore_signal(barrier, inc=1, device_id=at_sp(d), device_id_type=MESH)

    arrivals = [
        pltpu.make_async_copy(src, dst, local.at[i])
        for i, (src, dst) in enumerate((
            (weights_in, weights), (vectors_in, vectors), (affine_in, affine), (labels_in, labels),
            (steps_in, steps), (cotangent_in, cotangent), (images.at[p], xin.at[p]),
        ))
    ]
    for copy in arrivals:
        copy.start()

    patches[:, 0:1] = jnp.zeros_like(patches[:, 0:1])
    patches[:, half + 1 :] = jnp.zeros_like(patches[:, half + 1 :])
    grads[:, 0:1] = jnp.zeros_like(grads[:, 0:1])
    grads[:, half + 1 :] = jnp.zeros_like(grads[:, half + 1 :])

    for copy in arrivals[:3]:
        copy.wait()
    mine = weights[...].astype(BF16)
    pieces[s, z, c] = mine
    matrix = mine.astype(F32)
    vector = vectors[pl.ds(s, 1)]
    proj = jnp.sum(matrix * vector, axis=1, keepdims=True)
    crossed = jnp.sum(proj * matrix, axis=0, keepdims=True)
    norm = jnp.broadcast_to(jnp.sum(proj * proj, axis=0, keepdims=True), (1, ch))
    cuts = ((0, ch), (ch, ch), (2 * ch, ch // 2))
    flat = jnp.concatenate([affine[pl.ds(at, n)].reshape(1, n) for at, n in cuts], 1)
    flat = flat.astype(BF16).astype(F32)
    hollow = jnp.zeros((1, ch // 2), F32)
    even = [flat[:, 0:ch], flat[:, ch : 2 * ch], jnp.concatenate([flat[:, 2 * ch :], hollow], 1)]
    odd = [
        jnp.concatenate([hollow, flat[:, 0 : ch // 2]], 1),
        flat[:, ch // 2 : 3 * ch // 2],
        flat[:, 3 * ch // 2 :],
    ]
    is_odd = jnp.full((1, ch), c, jnp.int32) == 1
    lines = [jnp.where(is_odd, b, a) for a, b in zip(even, odd)] + [*three(crossed), *three(norm)]
    tile = jnp.zeros((TILE, ch), F32)
    line = lax.broadcasted_iota(jnp.int32, (TILE, ch), 0)
    for index, value in enumerate(lines):
        tile = jnp.where(line == index, value, tile)
    lines_all[s, z, c] = tile.astype(BF16)

    pl.semaphore_wait(barrier, nsec - 1 + nsp - 1)

    def piece_copy(a, b, e, out_sem, where):
        ref = pieces.at[a, b, e]
        return remote(ref, ref, out_sem, piece_in.at[a, b, e], where)

    def line_copy(ref, index, where):
        return remote(ref, ref, line_out.at[index], line_in.at[index], where)

    sends = []

    def send(copy):
        copy.start()
        sends.append(copy)

    for d in range(1, nsec):
        send(line_copy(lines_all.at[s, z, c], d - 1, at_section(d)))
    for d in range(1, nz):
        send(piece_copy(s, z, c, piece_z.at[d - 1], at_z(d)))
    for d in range(1, nsec):
        send(piece_copy(s, z, c, piece_s.at[0, d - 1], at_section(d)))
    send(piece_copy(s, z, c, piece_c.at[0], sibling))

    for copy in arrivals[3:]:
        copy.wait()
    active = jnp.where(steps[...] > active_above, 1.0, 0.0)
    pulled = cotangent[...].astype(F32).reshape(half * half, ch) * (0.25 * active)
    up_rows[pl.ds(0, half * half, stride=2), :] = pulled
    up_rows[pl.ds(1, half * half, stride=2), :] = pulled

    for d in range(1, nsec):
        line_copy(lines_all.at[sec(d), z, c], d - 1, sibling).wait_recv()
    for d in range(1, nz):
        send(line_copy(lines_all.at[:, z, c], nsec - 2 + d, at_z(d)))
    for d in range(1, nsp):
        q = jnp.bitwise_xor(p, d)
        send(remote(images.at[q], xin.at[p], image_out.at[d - 1], image_in.at[p], at_sp(d)))
    for d in range(1, nz):
        piece_copy(s, zed(d), c, piece_z.at[d - 1], sibling).wait_recv()
        for e in range(1, nsec):
            send(piece_copy(s, zed(d), c, piece_s.at[d, e - 1], at_section(e)))
        send(piece_copy(s, zed(d), c, piece_c.at[d], sibling))
    for d in range(1, nz):
        line_copy(lines_all.at[:, zed(d), c], nsec - 2 + d, sibling).wait_recv()
    lines_last = nsec + nz - 2
    send(line_copy(lines_all.at[:, :, c], lines_last, sibling))

    def pass_on(e):
        for d in range(1, nsec):
            copy = piece_copy(sec(d), zed(e), c, piece_k.at[d, e], sibling)
            copy.wait_recv()
            send(copy)

    per = band // 2

    def take_image(d):
        q = jnp.bitwise_xor(p, d)
        if d:
            remote(images.at[q], xin.at[q], image_out.at[d - 1], image_in.at[q], sibling).wait_recv()
        block = xin[q].astype(F32).reshape(per, 2, side, ch)
        put_patches(patches.at[0], q * per, halves(block, ch), side, ch)

    for e in range(nz):
        pass_on(e)
        take_image(2 * e)
        take_image(2 * e + 1)
    line_copy(lines_all.at[:, :, 1 - c], lines_last, sibling).wait_recv()

    tags = labels[...]
    at = lax.broadcasted_iota(jnp.int32, tags.shape, 1)
    label = jnp.sum(jnp.where(at == p, tags, 0).astype(F32), axis=1, keepdims=True).astype(jnp.int32)
    width = nsec * nsp * TILE
    column = lax.broadcasted_iota(jnp.int32, (TILE, width), 1)
    picked = lax.broadcasted_iota(jnp.int32, (TILE, width), 0)
    device = jnp.right_shift(column, 4)
    entry = jnp.bitwise_and(column, TILE - 1)
    wanted = picked * count + label
    at_row = jnp.right_shift(device * 5, 1) + entry
    section = jnp.right_shift(column, (nsp * TILE).bit_length() - 1)
    chosen = (picked < 8) & (entry < 3) & (at_row == wanted)
    chosen |= (picked >= 8) & (picked < 12) & (section == picked - 8) & (entry >= 3) & (entry < 6)
    chosen |= (picked >= 12) & (section == picked - 12) & (entry >= 6) & (entry < 9)
    everything = lines_all[...].reshape(width, ch)
    rows_ref[...] = dot(jnp.where(chosen, 1.0, 0.0).astype(BF16), everything, NN)
    gains, biases = rows_ref[0:4], rows_ref[4:8]
    lengths = jnp.sqrt(rows_ref[12:16] + 1e-06)
    units = rows_ref[8:12] / lengths
    sigmas = jnp.sqrt(jnp.sum(units * units, axis=1, keepdims=True) + 1e-06)
    scales = gains / sigmas

    def kernel_of(j):
        parts = [pieces[j, b, e] for b in range(nz) for e in range(2)]
        return jnp.concatenate(parts, 0)

    chunks = 8
    step = half // chunks
    spans = [(i * step, pl.ds(i * step * side, step * side)) for i in range(chunks)]
    part = half // 4
    parts = [(i * part, pl.ds(i * part * side, part * side)) for i in range(4)]

    for j in range(KERNELS):
        for b in range(nz):
            piece_copy(j, b, 1 - c, piece_c.at[0], sibling).wait_recv()
        matrix = pair_weights(kernel_of(j))
        for pair, span in parts:
            raws[j, span] = dot(patch_rows(patches.at[j], pair, part), matrix, NN)
        back_weights[j] = pair_weights_back(kernel_of(j)).T
        scale, bias = twice(scales[j : j + 1]), twice(biases[j : j + 1])
        for pair, span in spans:
            value, slope = leaky_terms(raws[j, span] * scale + bias)
            slopes[j, span] = slope
            if j % 2 == 1:
                source = patches[j - 1, pair + 1 : pair + 1 + step, :, :, ch : 2 * ch]
                value = halves(source.astype(F32), ch) + value
            if j < KERNELS - 1:
                put_patches(patches.at[j + 1], pair, value, side, ch)
            else:
                pool_rows[span] = value[:, :ch] + value[:, ch:]
    pooled = pool_rows[pl.ds(0, half * half, stride=2), :] + pool_rows[pl.ds(1, half * half, stride=2), :]
    energy[...] = (pooled * (0.25 * active)).reshape(half, half, ch)

    def first_copy(j):
        return remote(dk.at[j, :, 1 - c], first.at[j], one_out.at[j], one_in.at[j], sibling)

    def second_copy(j, d):
        return remote(
            summed.at[j, zed(d)], second.at[j, d - 1], two_out.at[j, d - 1], two_in.at[j, d - 1], at_z(d)
        )

    def third_copy(j):
        d = jnp.maximum(jnp.bitwise_xor(s, j) - 1, 0)
        return remote(total.at[j], third.at[d], three_out.at[j], three_in.at[d], (j, p))

    def near_copy(j, k):
        return remote(
            summed.at[j, zed(3 - 2 * k)], near.at[j, k], near_out.at[j, k], near_in.at[j, k], at_z(1)
        )

    def wide_copy(j, k):
        d = jnp.maximum(jnp.bitwise_xor(s, j) - 1, 0)
        return remote(paired.at[j, k], wide.at[d, k], wide_out.at[j, k], wide_in.at[d, k], (j, p))

    def last_copy():
        return remote(joined, last, last_sems.at[0], last_sems.at[1], at_z(2))

    def first_sum(j):
        first_copy(j).wait_recv()
        summed[j] = (dk[j, :, c].astype(F32) + first[j].astype(F32)).astype(BF16)
        if modes[j] == "z":
            for d in reversed(range(1, nz)):
                send(second_copy(j, d))
        else:
            for k in range(2):
                send(near_copy(j, k))

    def near_sum(j):
        for k in range(2):
            near_copy(j, k).wait_recv()
            paired[j, k] = (summed[j, zed(2 - 2 * k)].astype(F32) + near[j, k].astype(F32)).astype(BF16)
            pl.when(s != j)(lambda: wide_copy(j, k).start())

    def wide_sum(k):
        value = paired[s, k].astype(F32)
        for d in range(1, nsec):
            remote(paired.at[0, k], wide.at[d - 1, k], wide_out.at[0, k], wide_in.at[d - 1, k], sibling).wait_recv()
            value += wide[d - 1, k].astype(F32)
        return value

    def second_sum(j):
        value = summed[j, z].astype(F32)
        for d in range(1, nz):
            second_copy(j, d).wait_recv()
            value += second[j, d - 1].astype(F32)
        total[j] = value.astype(BF16)
        pl.when(s != j)(lambda: third_copy(j).start())

    by_z = [j for j in range(KERNELS) if modes[j] == "z"]
    by_near = [j for j in range(KERNELS) if modes[j] != "z"]

    def is_one_of(kernels):
        found = s < 0
        for j in kernels:
            found = jnp.logical_or(found, s == j)
        return found

    lines = []

    def tile_copy(q, k, d, where):
        ref = tiles.at[q, c, k]
        return remote(ref, ref, tile_out.at[k, d - 1], tile_in.at[k, q], where)

    def tiles_copy(e):
        return remote(tiles.at[:, e], tiles.at[:, e], tile_out.at[0, nz - 1], tile_in.at[0, nz], sibling)

    def pixel_step(j):
        scale = twice(scales[j : j + 1])
        gain_sum = jnp.zeros((1, 2 * ch), F32)
        bias_sum = jnp.zeros((1, 2 * ch), F32)
        for pair, span in spans:
            upstream = twice(up_rows[span]) if j == KERNELS - 1 else slopes[j + 1, span]
            pre = upstream * slopes[j, span]
            gain_sum += jnp.sum(pre * raws[j, span], axis=0, keepdims=True)
            bias_sum += jnp.sum(pre, axis=0, keepdims=True)
            put_patches(grads.at[j % 2], pair, pre * scale, side, ch)
        sigma = sigmas[j : j + 1]
        gain_row = (gain_sum[:, :ch] + gain_sum[:, ch:]) / sigma
        lines.append(gain_row)
        lines.append(bias_sum[:, :ch] + bias_sum[:, ch:])
        lines.append(-gain_row * gains[j : j + 1] / sigma)

    def weight_step(j):
        inputs = patches[j, 1 : half + 1].reshape(2 * half * side, 3 * ch)
        centre = grads[j % 2].reshape(2 * half + 4, side, 3 * ch)[:, :, ch : 2 * ch]
        shifted = [centre[3 - a : 3 - a + 2 * half] for a in range(3)]
        shifted = jnp.concatenate(shifted, -1).reshape(2 * half * side, 3 * ch)
        grad = dot(inputs, shifted, TN)
        grad = jnp.concatenate([grad[:, a * ch : (a + 1) * ch] for a in range(3)], 0).astype(BF16)
        for b in range(nz):
            for e in range(2):
                at = (2 * b + e) * rows
                dk[j, b, e] = grad[at : at + rows]

    def input_step(j):
        for pair, span in parts:
            down = dot(patch_rows(grads.at[j % 2], pair, part), back_weights[j], NN)
            if j == 2:
                down = (down + twice(up_rows[span])).astype(BF16).astype(F32)
                raws[2, span] = down
            if j > 0:
                slopes[j, span] = down
            else:
                down = (down + raws[2, span]).astype(BF16)
                for i in range(part // per):
                    for e in range(2):
                        block = down[i * per * side : (i + 1) * per * side, e * ch : (e + 1) * ch]
                        back[pair // per + i, :, e] = block.reshape(per, side, ch)

    for j in reversed(range(KERNELS)):
        pixel_step(j)
        if j % 2 == 0:
            tile = jnp.zeros((8, ch), F32)
            for index, value in enumerate(lines):
                tile = jnp.where(line[:8] == index, value, tile)
            lines.clear()
            k = 1 - j // 2
            tiles[z, c, k] = tile
            for d in range(1, nz):
                send(tile_copy(z, k, d, at_z(d)))
        weight_step(j)
        send(first_copy(j))
        if j < KERNELS - 1:
            first_sum(j + 1)
        input_step(j)
    first_sum(0)

    own_back = pltpu.make_async_copy(back.at[p], returned.at[p], local.at[7])
    own_back.start()
    for d in range(1, nsp):
        q = jnp.bitwise_xor(p, d)
        send(remote(back.at[q], returned.at[p], back_out.at[d - 1], back_in.at[p], at_sp(d)))

    for j in sorted(by_z)[1:]:
        second_sum(j)
    for j in reversed(by_near):
        near_sum(j)
    def pass_joined():
        joined[...] = wide_sum(0).astype(BF16)
        last_copy().start()

    pl.when(is_one_of(by_near[1:]))(pass_joined)
    for d in range(1, nz):
        for k in range(2):
            tile_copy(zed(d), k, d, sibling).wait_recv()
    send(tiles_copy(c))
    tiles_copy(1 - c).wait_recv()
    spread = nsp * TILE
    column = lax.broadcasted_iota(jnp.int32, (24, spread), 1)
    row = lax.broadcasted_iota(jnp.int32, (24, spread), 0)
    entry = jnp.bitwise_and(column, TILE - 1)
    owner = jnp.right_shift(column, 4)
    tag = jnp.zeros((24, spread), jnp.int32)
    for q in range(nsp):
        tag = jnp.where(owner == q, tags[:, q : q + 1], tag)
    gathered = tiles[...].reshape(spread, ch)
    upper = row >= count
    kind = row - jnp.where(upper, count, 0)
    spot = row - 2 * count
    sigma_slot = jnp.where(spot < 2, jnp.where(spot == 0, 13, 10), jnp.where(spot == 2, 5, 2))
    for blk in range(nsec):
        slot = (8 if blk % 2 == 0 else 0) + blk // 2 + jnp.where(upper, 0, 3)
        chosen = (spot < 0) & (entry == slot) & (tag == kind)
        chosen |= (spot >= 0) & (entry == sigma_slot)
        tables[blk] = dot(jnp.where(chosen, 1.0, 0.0), gathered, NN, HIGHEST)
    for d in range(1, nsec):
        send(remote(tables.at[sec(d)], tables_in.at[d - 1], table_out_sem.at[d - 1], table_in_sem.at[d - 1], at_section(d)))
    pl.when(is_one_of(by_near[:1]))(pass_joined)

    second_sum(min(by_z))

    table = tables[s]
    for d in range(1, nsec):
        remote(tables.at[sec(d)], tables_in.at[d - 1], table_out_sem.at[d - 1], table_in_sem.at[d - 1], at_section(d)).wait_recv()
        table += tables_in[d - 1]
    table_out[...] = table

    mine = pieces[s, z, c].astype(F32)
    proj = jnp.sum(mine * vector, axis=1, keepdims=True)
    q_row = rows_ref[pl.ds(8 + s, 1)]
    length = jnp.sqrt(rows_ref[pl.ds(12 + s, 1)][:, 0:1] + 1e-06)
    unit = q_row / length
    sigma = jnp.sqrt(jnp.sum(unit * unit, axis=1, keepdims=True) + 1e-06)
    along = unit / sigma
    reach = jnp.sum(mine * along, axis=1, keepdims=True)
    crossing = jnp.sum(q_row * along, axis=1, keepdims=True)
    slope = (reach - proj * (crossing / (length * length))) / length
    dsigma = table_out[pl.ds(2 * count + s, 1)]
    dsigma = jnp.sum(dsigma, axis=1, keepdims=True)
    weight_out[...] = dsigma * ((proj / length) * along + slope * vector)

    @pl.when(is_one_of(by_z))
    def _():
        value = weight_out[...] + total[s].astype(F32)
        for d in range(1, nsec):
            remote(total.at[0], third.at[d - 1], three_out.at[0], three_in.at[d - 1], sibling).wait_recv()
            value += third[d - 1].astype(F32)
        weight_out[...] = value

    @pl.when(is_one_of(by_near))
    def _():
        value = weight_out[...] + wide_sum(1)
        last_copy().wait_recv()
        weight_out[...] = value + last[...].astype(F32)
        last_copy().wait_send()

    for d in range(1, nsp):
        q = jnp.bitwise_xor(p, d)
        remote(back.at[q], returned.at[q], back_out.at[d - 1], back_in.at[q], sibling).wait_recv()
    own_back.wait()
    for copy in sends:
        copy.wait_send()
    for j in by_z:
        pl.when(s != j)(lambda j=j: third_copy(j).wait_send())
    for j in by_near:
        for k in range(2):
            pl.when(s != j)(lambda j=j, k=k: wide_copy(j, k).wait_send())


def finish_kernel(count, energy_in, returned, weight_in, table, energy, grad, weight, affine, wide, sems):
    copies = [
        pltpu.make_async_copy(energy_in, energy, sems.at[0]),
        pltpu.make_async_copy(weight_in, weight, sems.at[1]),
    ]
    for copy in copies:
        copy.start()
    for i in range(returned.shape[0]):
        wide[i] = returned[i].astype(F32)
        copies.append(pltpu.make_async_copy(wide.at[i], grad.at[i], sems.at[2 + i]))
        copies[-1].start()
    ch = table.shape[1]
    p = lax.axis_index("sp")
    start = 5 * p // 2
    block = table[pl.ds(start, 3)]
    odd = jnp.full((1, ch), p % 2, jnp.int32) == 1
    middle = ch // 2
    swapped = [jnp.concatenate([block[i : i + 1, middle:], block[i : i + 1, :middle]], 1) for i in range(3)]
    low = lax.broadcasted_iota(jnp.int32, (1, ch), 1) < middle
    later = [jnp.where(low, swapped[i], swapped[i + 1]) for i in range(2)]
    affine[pl.ds(0, ch)] = jnp.where(odd, later[0], block[0:1]).reshape(ch)
    affine[pl.ds(ch, ch)] = jnp.where(odd, later[1], block[1:2]).reshape(ch)
    affine[pl.ds(2 * ch, middle)] = jnp.where(odd, swapped[2], block[2:3])[:, :middle].reshape(middle)
    for copy in copies:
        copy.wait()


def whole_body(images, labels, chain_steps, conv_weights, class_affine, power_vectors, cotangent):
    nsec, nsp = lax.axis_size("section"), lax.axis_size("sp")
    nz = nsp // 2
    own, band, side, ch = images.shape
    half = side // 2
    rows = conv_weights.shape[0] // ch
    share = class_affine.shape[0]
    count = share * nsec * nsp // (2 * KERNELS * ch)
    anywhere = pl.BlockSpec(memory_space=pltpu.MemorySpace.HBM)
    vmem = pl.BlockSpec(memory_space=pltpu.VMEM)
    pixels = half * side
    dma = pltpu.SemaphoreType.DMA
    results = pl.pallas_call(
        partial(whole_kernel, nsec, nz, count, LANGEVIN_T, MODES),
        out_shape=[
            pltpu.VMEM((half, half, ch), F32),
            pltpu.VMEM((own, band // 2, 2, side, ch), BF16),
            pltpu.VMEM((rows, ch), F32),
            pltpu.VMEM((24, ch), F32),
        ],
        in_specs=[anywhere] * 7,
        out_specs=[vmem] * 4,
        scratch_shapes=[
            pltpu.VMEM(labels.shape[::-1], jnp.int32),
            pltpu.VMEM(chain_steps.shape, jnp.int32),
            pltpu.VMEM((rows, ch), F32),
            pltpu.VMEM((share,), F32),
            pltpu.VMEM(power_vectors.shape, F32),
            pltpu.VMEM((half, half, ch), BF16),
            pltpu.VMEM((nsec, nz, 2, rows, ch), BF16),
            pltpu.VMEM((nsec, nz, 2, TILE, ch), BF16),
            pltpu.VMEM((nsp, band, side, ch), BF16),
            pltpu.VMEM((KERNELS, half + 2, 2, side, 3 * ch), BF16),
            pltpu.VMEM((2, half + 2, 2, side, 3 * ch), BF16),
            pltpu.VMEM((KERNELS, 12 * ch, 2 * ch), BF16),
            pltpu.VMEM((KERNELS, pixels, 2 * ch), F32),
            pltpu.VMEM((KERNELS, pixels, 2 * ch), F32),
            pltpu.VMEM((pixels, ch), F32),
            pltpu.VMEM((pixels, ch), F32),
            pltpu.VMEM((TILE, ch), F32),
            pltpu.VMEM((KERNELS, nz, 2, rows, ch), BF16),
            pltpu.VMEM((KERNELS, nz, rows, ch), BF16),
            pltpu.VMEM((KERNELS, nz, rows, ch), BF16),
            pltpu.VMEM((KERNELS, nz - 1, rows, ch), BF16),
            pltpu.VMEM((KERNELS, rows, ch), BF16),
            pltpu.VMEM((nsec - 1, rows, ch), BF16),
            pltpu.VMEM((KERNELS, 2, rows, ch), BF16),
            pltpu.VMEM((KERNELS, 2, rows, ch), BF16),
            pltpu.VMEM((nsec - 1, 2, rows, ch), BF16),
            pltpu.VMEM((rows, ch), BF16),
            pltpu.VMEM((rows, ch), BF16),
            pltpu.VMEM((nsp, band // 2, 2, side, ch), BF16),
            pltpu.VMEM((nz, 2, 2, 8, ch), F32),
            pltpu.VMEM((nsec, 24, ch), F32),
            pltpu.VMEM((nsec - 1, 24, ch), F32),
            dma((8,)),
            dma((nsec, nz, 2)),
            dma((nz - 1,)),
            dma((nz, nsec - 1)),
            dma((nz,)),
            dma((nsec, nz)),
            dma((nsec + nz - 1,)),
            dma((nsec + nz - 1,)),
            dma((nsp - 1,)),
            dma((nsp,)),
            dma((KERNELS,)),
            dma((KERNELS,)),
            dma((KERNELS, nz - 1)),
            dma((KERNELS, nz - 1)),
            dma((KERNELS,)),
            dma((nsec - 1,)),
            dma((KERNELS, 2)),
            dma((KERNELS, 2)),
            dma((KERNELS, 2)),
            dma((nsec - 1, 2)),
            dma((2,)),
            dma((nsp - 1,)),
            dma((nsp,)),
            dma((2, nz)),
            dma((2, nz + 1)),
            dma((nsec - 1,)),
            dma((nsec - 1,)),
        ],
        compiler_params=pltpu.CompilerParams(
            collective_id=0, has_side_effects=True, vmem_limit_bytes=56 * 2**20
        ),
    )(
        images,
        labels.reshape(labels.shape[::-1]),
        chain_steps,
        conv_weights.reshape(rows, ch),
        class_affine,
        power_vectors,
        cotangent.reshape(half, half, ch),
    )
    energy, returned, weight_grad, affine_grad = pl.pallas_call(
        partial(finish_kernel, count),
        out_shape=[
            jax.ShapeDtypeStruct((half, half, ch), F32),
            jax.ShapeDtypeStruct((own, band // 2, 2, side, ch), F32),
            jax.ShapeDtypeStruct((rows, ch), F32),
            jax.ShapeDtypeStruct((share,), F32),
        ],
        in_specs=[vmem] * 4,
        out_specs=[anywhere] * 3 + [vmem],
        scratch_shapes=[pltpu.VMEM((own, band // 2, 2, side, ch), F32), dma((own + 2,))],
    )(*(pltpu.with_memory_space_constraint(r, pltpu.VMEM) for r in results))
    return (
        energy[None],
        returned.reshape(own, band, side, ch),
        weight_grad.reshape(-1),
        affine_grad,
    )


def body(images, labels, chain_steps, conv_weights, class_affine, power_vectors, cotangent):
    nsec, nsp = lax.axis_size("section"), lax.axis_size("sp")
    channels = images.shape[3]
    rows = conv_weights.shape[0] // channels
    fits = (
        nsec == KERNELS
        and nsp == 8
        and images.shape[0] == nsp
        and images.shape[1] * nsp == images.shape[2]
        and images.shape[1] % 2 == 0
        and chain_steps.shape == (1, 1)
        and rows % 16 == 0
        and class_affine.shape[0] * 2 == 5 * channels
    )
    chosen = whole_body if fits else general_body
    return chosen(
        images, labels, chain_steps, conv_weights, class_affine, power_vectors, cotangent
    )


def solution(mesh):
    in_specs = (
        P("section", "sp", None, None),
        P("section", None),
        P(("section", "sp"), None),
        P(("section", "sp")),
        P(("section", "sp")),
        P(),
        P(("section", "sp"), None, None, None),
    )
    out_specs = (
        P(("section", "sp"), None, None, None),
        P("section", "sp", None, None),
        P(("section", "sp")),
        P(("section", "sp")),
    )
    return jax.shard_map(body, mesh=mesh, in_specs=in_specs, out_specs=out_specs, check_vma=False)
```

```python
from functools import partial

import jax
import jax.numpy as jnp
from jax import lax
from jax.experimental import pallas as pl
from jax.experimental.pallas import tpu as pltpu
from jax.sharding import PartitionSpec as P

LANGEVIN_T = 40


HIGHEST = lax.Precision.HIGHEST


def extended_2(block, sides, width):
    for axis, dim in sides:
        count = lax.axis_size(axis)
        forward = [(i, i + 1) for i in range(count - 1)]
        backward = [(target, source) for source, target in forward]
        low = lax.ppermute(
            lax.slice_in_dim(block, block.shape[dim] - width, None, axis=dim), axis, forward
        )
        high = lax.ppermute(lax.slice_in_dim(block, 0, width, axis=dim), axis, backward)
        block = jnp.concatenate([low, block, high], axis=dim)
    return block


def leaky(value):
    return 0.2 * value + 0.8 * jax.nn.softplus(value)


def leaky_slope(value):
    return 0.2 + 0.8 * jax.nn.sigmoid(value)


def spectral(matrix, vector):
    forward = jnp.dot(matrix, vector, precision=HIGHEST)
    unit = forward / jnp.sqrt(jnp.sum(forward * forward) + 1e-06)
    backward = jnp.dot(unit, matrix, precision=HIGHEST)
    return jnp.sqrt(jnp.sum(backward * backward) + 1e-06)


def taps(padded, kernel):
    return lax.conv_general_dilated(
        padded,
        kernel,
        (1, 1),
        "VALID",
        dimension_numbers=("NHWC", "HWIO", "NHWC"),
        preferred_element_type=jnp.float32,
    )


def kernel_grad(padded, grad):
    result = lax.conv_general_dilated(
        padded,
        grad,
        (1, 1),
        "VALID",
        dimension_numbers=("CHWN", "IHWO", "NHWC"),
        preferred_element_type=jnp.float32,
    )
    return jnp.transpose(result, (1, 2, 0, 3))


def flipped(kernel):
    return jnp.transpose(jnp.flip(kernel, (0, 1)), (0, 1, 3, 2))


def trim_rims(extended, band, side):
    start = lax.axis_index("sp") * band
    keep_top = jnp.where(start % side == 0, 0.0, 1.0).astype(extended.dtype)
    keep_bottom = jnp.where((start + band) % side == 0, 0.0, 1.0).astype(extended.dtype)
    merged = jnp.concatenate(
        [extended[:, :1] * keep_top, extended[:, 1:-1], extended[:, -1:] * keep_bottom], axis=1
    )
    return jnp.pad(merged, ((0, 0), (0, 0), (1, 1), (0, 0)))


def rows_forward(values, band, side):
    extended = extended_2(values, (("sp", 1),), 1)
    return trim_rims(extended, band, side)


def rows_backward(values, band, side):
    extended = extended_2(values, (("sp", 1),), 1)
    return trim_rims(extended, band, side)


def pad_whole(values):
    return jnp.pad(values, ((0, 0), (1, 1), (1, 1), (0, 0)))


def affine_terms(upstream, raw, value, scale, gain, sigma):
    pre = upstream * leaky_slope(value)
    grad_raw = (pre * scale[:, None, None, :]).astype(jnp.bfloat16)
    grad_gain = jnp.sum(pre * raw, axis=(1, 2)) / sigma
    grad_bias = jnp.sum(pre, axis=(1, 2))
    grad_sigma = -jnp.sum(grad_gain * gain) / sigma
    return (grad_raw, grad_gain, grad_bias, grad_sigma)


def general_body(images, labels, chain_steps, conv_weights, class_affine, power_vectors, cotangent):
    channels = images.shape[3]
    band = images.shape[1]
    side = images.shape[2]
    half = side // 2
    across = labels.shape[1]
    groups = chain_steps.shape[0]
    gathered_w, gathered_a = (
        lax.all_gather(conv_weights.astype(jnp.bfloat16), ("section", "sp"), axis=0, tiled=True),
        lax.all_gather(class_affine.astype(jnp.bfloat16), ("section", "sp"), axis=0, tiled=True),
    )
    kernels = gathered_w.reshape(4, 3, 3, channels, channels)
    table = gathered_a.astype(jnp.float32).reshape(2, 4, -1, channels)
    count = table.shape[2]
    matrices = kernels.astype(jnp.float32).reshape(4, 9 * channels, channels)
    sigmas = [spectral(matrices[j], power_vectors[j]) for j in range(4)]
    kinds = jnp.arange(count)
    start = lax.axis_index("sp") * groups
    tags_second = lax.dynamic_slice_in_dim(labels, start, groups, 0).reshape(-1)
    onehot_second = (tags_second[:, None] == kinds[None, :]).astype(jnp.float32)
    active = (chain_steps.reshape(-1) > LANGEVIN_T).astype(jnp.float32)
    column = lax.axis_index("sp") * band // side
    picks = jnp.arange(across) == column
    tags_first = jnp.sum(jnp.where(picks[None, :], labels, 0), axis=1)
    onehot_first = (tags_first[:, None] == kinds[None, :]).astype(jnp.float32)
    pad_forward = partial(rows_forward, band=band, side=side)
    pad_backward = partial(rows_backward, band=band, side=side)
    gains_first = jnp.einsum("nk,jkc->jnc", onehot_first, table[0], precision=HIGHEST)
    biases_first = jnp.einsum("nk,jkc->jnc", onehot_first, table[1], precision=HIGHEST)
    gains_second = jnp.einsum("nk,jkc->jnc", onehot_second, table[0], precision=HIGHEST)
    biases_second = jnp.einsum("nk,jkc->jnc", onehot_second, table[1], precision=HIGHEST)
    scales = [
        gains_first[0] / sigmas[0],
        gains_first[1] / sigmas[1],
        gains_second[2] / sigmas[2],
        gains_second[3] / sigmas[3],
    ]
    input_pad = pad_forward(images)
    raw_zero = taps(input_pad, kernels[0])
    pre_zero = raw_zero * scales[0][:, None, None, :] + biases_first[0][:, None, None, :]
    hidden_zero = leaky(pre_zero).astype(jnp.bfloat16)
    hidden_pad = pad_forward(hidden_zero)
    raw_one = taps(hidden_pad, kernels[1])
    pre_one = raw_one * scales[1][:, None, None, :] + biases_first[1][:, None, None, :]
    first_out = images.astype(jnp.float32) + leaky(pre_one)
    moved = lax.all_to_all(
        first_out.astype(jnp.bfloat16), "sp", split_axis=0, concat_axis=1, tiled=True
    )
    whole = moved.reshape(groups * across, side, side, channels)
    whole_pad = pad_whole(whole)
    raw_two = taps(whole_pad, kernels[2])
    pre_two = raw_two * scales[2][:, None, None, :] + biases_second[2][:, None, None, :]
    hidden_two = leaky(pre_two).astype(jnp.bfloat16)
    hidden_two_pad = pad_whole(hidden_two)
    raw_three = taps(hidden_two_pad, kernels[3])
    pre_three = raw_three * scales[3][:, None, None, :] + biases_second[3][:, None, None, :]
    second_out = whole.astype(jnp.float32) + leaky(pre_three)
    pooled = (
        jnp.mean(second_out.reshape(-1, half, 2, half, 2, channels), axis=(2, 4))
        * active[:, None, None, None]
    )
    energy = pooled.reshape(groups, across * half, half, channels)
    upstream = (
        cotangent.astype(jnp.float32).reshape(-1, half, half, channels)
        * (0.25 * active)[:, None, None, None]
    )
    images_n = upstream.shape[0]
    grad_out = jnp.broadcast_to(
        upstream[:, :, None, :, None, :], (images_n, half, 2, half, 2, channels)
    ).reshape(images_n, side, side, channels)
    dz_three, dg_three, db_three, dsig_three = affine_terms(
        grad_out, raw_three, pre_three, scales[3], gains_second[3], sigmas[3]
    )
    kg_three = kernel_grad(hidden_two_pad, dz_three)
    grad_hidden = taps(pad_whole(dz_three), flipped(kernels[3]))
    dz_two, dg_two, db_two, dsig_two = affine_terms(
        grad_hidden, raw_two, pre_two, scales[2], gains_second[2], sigmas[2]
    )
    kg_two = kernel_grad(whole_pad, dz_two)
    grad_whole = grad_out + taps(pad_whole(dz_two), flipped(kernels[2]))
    back_rows = grad_whole.astype(jnp.bfloat16).reshape(groups, across * side, side, channels)
    returned = lax.all_to_all(back_rows, "sp", split_axis=1, concat_axis=0, tiled=True)
    grad_first = returned.astype(jnp.float32)
    dz_one, dg_one, db_one, dsig_one = affine_terms(
        grad_first, raw_one, pre_one, scales[1], gains_first[1], sigmas[1]
    )
    kg_one = kernel_grad(hidden_pad, dz_one)
    grad_hidden_first = taps(pad_backward(dz_one), flipped(kernels[1]))
    dz_zero, dg_zero, db_zero, dsig_zero = affine_terms(
        grad_hidden_first, raw_zero, pre_zero, scales[0], gains_first[0], sigmas[0]
    )
    kg_zero = kernel_grad(input_pad, dz_zero)
    local_grad = grad_first + taps(pad_backward(dz_zero), flipped(kernels[0]))
    conv_grads = [kg_zero, kg_one, kg_two, kg_three]
    sigma_grads = [dsig_zero, dsig_one, dsig_two, dsig_three]
    pieces = []
    for index in range(4):
        unused, pullback = jax.vjp(partial(spectral, vector=power_vectors[index]), matrices[index])
        pieces.append(
            conv_grads[index].reshape(9 * channels, channels) + pullback(sigma_grads[index])[0]
        )
    weight_total = jnp.stack(pieces).reshape(-1)
    gain_rows = [
        jnp.einsum("nk,nc->kc", onehot_first, dg_zero, precision=HIGHEST),
        jnp.einsum("nk,nc->kc", onehot_first, dg_one, precision=HIGHEST),
        jnp.einsum("nk,nc->kc", onehot_second, dg_two, precision=HIGHEST),
        jnp.einsum("nk,nc->kc", onehot_second, dg_three, precision=HIGHEST),
    ]
    bias_rows = [
        jnp.einsum("nk,nc->kc", onehot_first, db_zero, precision=HIGHEST),
        jnp.einsum("nk,nc->kc", onehot_first, db_one, precision=HIGHEST),
        jnp.einsum("nk,nc->kc", onehot_second, db_two, precision=HIGHEST),
        jnp.einsum("nk,nc->kc", onehot_second, db_three, precision=HIGHEST),
    ]
    affine_total = jnp.stack([jnp.stack(gain_rows), jnp.stack(bias_rows)]).reshape(-1)
    weight_grad, affine_grad = (
        lax.psum_scatter(weight_total, ("section", "sp"), scatter_dimension=0, tiled=True),
        lax.psum_scatter(affine_total, ("section", "sp"), scatter_dimension=0, tiled=True),
    )
    return (energy, local_grad, weight_grad, affine_grad)

F32 = jnp.float32
BF16 = jnp.bfloat16
MESH = pl.DeviceIdType.MESH
NN = (((1,), (0,)), ((), ()))
NT = (((1,), (1,)), ((), ()))
TN = (((0,), (0,)), ((), ()))
KERNELS = 4
MODES = ("z", "h", "h", "h")
TILE = 16


def dot(left, right, dims, precision=None):
    return lax.dot_general(left, right, dims, precision=precision, preferred_element_type=F32)


def twice(row):
    return jnp.concatenate([row, row], 1)


def beside(value, side):
    rows = value.shape[0]
    column = lax.broadcasted_iota(jnp.int32, (rows, 1), 0) % side
    left = jnp.where(column == 0, 0.0, pltpu.roll(value, 1, 0))
    right = jnp.where(column == side - 1, 0.0, pltpu.roll(value, rows - 1, 0))
    return (left, value, right)


def put_patches(ref, pair, value, side, ch):
    count = value.shape[0] // side
    rows = pl.ds(pair + 1, count)
    for b, part in enumerate(beside(value, side)):
        part = part.astype(BF16)
        for e in range(2):
            half = part[:, e * ch : (e + 1) * ch].reshape(count, side, ch)
            ref[rows, e, :, b * ch : (b + 1) * ch] = half


def patch_rows(ref, at, count):
    side, width = ref.shape[2], ref.shape[3]
    end = at + count
    parts = [ref[at:end, 1], ref[at + 1 : end + 1, 0], ref[at + 1 : end + 1, 1], ref[at + 2 : end + 2, 0]]
    return jnp.concatenate(parts, -1).reshape(count * side, 4 * width)


def pair_weights(kernel):
    rows = kernel.shape[0] // 3
    zero = jnp.zeros((rows, kernel.shape[1]), kernel.dtype)
    a, b, c = (kernel[i * rows : (i + 1) * rows] for i in range(3))
    pairs = ((a, zero), (b, a), (c, b), (zero, c))
    return jnp.concatenate([jnp.concatenate(pair, 1) for pair in pairs], 0)


def pair_weights_back(kernel):
    ch = kernel.shape[1]
    zero = jnp.zeros((ch, ch), kernel.dtype)
    blocks = []
    for e in range(2):
        row = []
        for r in range(4):
            for b in range(3):
                a = 2 - (r - e)
                tap = (a * 3 + 2 - b) * ch
                row.append(kernel[tap : tap + ch] if 0 <= a <= 2 else zero)
        blocks.append(jnp.concatenate(row, 1))
    return jnp.concatenate(blocks, 0)


def leaky_terms(value):
    small = jnp.exp(-jnp.abs(value))
    result = 0.2 * value + 0.8 * (jnp.maximum(value, 0.0) + jnp.log(1.0 + small))
    return result, 0.6 + 0.4 * jnp.tanh(0.5 * value)


def halves(pairs, ch):
    wide = jnp.concatenate([pairs[:, 0], pairs[:, 1]], -1)
    return wide.reshape(-1, 2 * ch)


def three(row):
    high = row.astype(BF16).astype(F32)
    middle = (row - high).astype(BF16).astype(F32)
    return (high, middle, row - high - middle)


def whole_kernel(
    nsec, nz, count, active_above, modes,
    images, labels_in, steps_in, weights_in, affine_in, vectors_in, cotangent_in,
    energy, returned, weight_out, table_out,
    labels, steps, weights, affine, vectors, cotangent,
    pieces, lines_all, xin, patches, grads, back_weights, raws, slopes, up_rows, pool_rows, rows_ref,
    dk, first, summed, second, total, third, near, paired, wide, joined, last, back, tiles, tables, tables_in,
    local, piece_in, piece_z, piece_s, piece_c, piece_k, line_out, line_in, image_out, image_in,
    one_out, one_in, two_out, two_in, three_out, three_in, near_out, near_in, wide_out, wide_in, last_sems,
    back_out, back_in, tile_out, tile_in, table_out_sem, table_in_sem,
):
    nsp = 2 * nz
    side, ch = images.shape[2], images.shape[3]
    band = images.shape[1]
    half = side // 2
    rows = weights.shape[0]
    s = lax.axis_index("section")
    p = lax.axis_index("sp")
    z = p // 2
    c = p % 2

    def sec(d):
        return jnp.bitwise_xor(s, d)

    def zed(d):
        return jnp.bitwise_xor(z, d)

    def remote(src, dst, out_sem, in_sem, where):
        return pltpu.make_async_remote_copy(
            src_ref=src, dst_ref=dst, send_sem=out_sem, recv_sem=in_sem,
            device_id=where, device_id_type=MESH,
        )

    sibling = (s, p + 1 - 2 * c)

    def at_section(d):
        return (sec(d), p)

    def at_z(d):
        return (s, 2 * zed(d) + c)

    def at_sp(d):
        return (s, jnp.bitwise_xor(p, d))

    barrier = pltpu.get_barrier_semaphore()
    for d in range(1, nsec):
        pl.semaphore_signal(barrier, inc=1, device_id=at_section(d), device_id_type=MESH)
    for d in range(1, nsp):
        pl.semaphore_signal(barrier, inc=1, device_id=at_sp(d), device_id_type=MESH)

    arrivals = [
        pltpu.make_async_copy(src, dst, local.at[i])
        for i, (src, dst) in enumerate((
            (weights_in, weights), (vectors_in, vectors), (affine_in, affine), (labels_in, labels),
            (steps_in, steps), (cotangent_in, cotangent), (images.at[p], xin.at[p]),
        ))
    ]
    for copy in arrivals:
        copy.start()

    patches[:, 0:1] = jnp.zeros_like(patches[:, 0:1])
    patches[:, half + 1 :] = jnp.zeros_like(patches[:, half + 1 :])
    grads[:, 0:1] = jnp.zeros_like(grads[:, 0:1])
    grads[:, half + 1 :] = jnp.zeros_like(grads[:, half + 1 :])

    for copy in arrivals[:3]:
        copy.wait()
    mine = weights[...].astype(BF16)
    pieces[s, z, c] = mine
    matrix = mine.astype(F32)
    vector = vectors[pl.ds(s, 1)]
    proj = jnp.sum(matrix * vector, axis=1, keepdims=True)
    crossed = jnp.sum(proj * matrix, axis=0, keepdims=True)
    norm = jnp.broadcast_to(jnp.sum(proj * proj, axis=0, keepdims=True), (1, ch))
    cuts = ((0, ch), (ch, ch), (2 * ch, ch // 2))
    flat = jnp.concatenate([affine[pl.ds(at, n)].reshape(1, n) for at, n in cuts], 1)
    flat = flat.astype(BF16).astype(F32)
    hollow = jnp.zeros((1, ch // 2), F32)
    even = [flat[:, 0:ch], flat[:, ch : 2 * ch], jnp.concatenate([flat[:, 2 * ch :], hollow], 1)]
    odd = [
        jnp.concatenate([hollow, flat[:, 0 : ch // 2]], 1),
        flat[:, ch // 2 : 3 * ch // 2],
        flat[:, 3 * ch // 2 :],
    ]
    is_odd = jnp.full((1, ch), c, jnp.int32) == 1
    lines = [jnp.where(is_odd, b, a) for a, b in zip(even, odd)] + [*three(crossed), *three(norm)]
    tile = jnp.zeros((TILE, ch), F32)
    line = lax.broadcasted_iota(jnp.int32, (TILE, ch), 0)
    for index, value in enumerate(lines):
        tile = jnp.where(line == index, value, tile)
    lines_all[s, z, c] = tile.astype(BF16)

    pl.semaphore_wait(barrier, nsec - 1 + nsp - 1)

    def piece_copy(a, b, e, out_sem, where):
        ref = pieces.at[a, b, e]
        return remote(ref, ref, out_sem, piece_in.at[a, b, e], where)

    def line_copy(ref, index, where):
        return remote(ref, ref, line_out.at[index], line_in.at[index], where)

    sends = []

    def send(copy):
        copy.start()
        sends.append(copy)

    def drain(count):
        for copy in sends[:count]:
            copy.wait_send()
        del sends[:count]

    for d in range(1, nsec):
        send(line_copy(lines_all.at[s, z, c], d - 1, at_section(d)))
    for d in range(1, nz):
        send(piece_copy(s, z, c, piece_z.at[d - 1], at_z(d)))
    for d in range(1, nsec):
        send(piece_copy(s, z, c, piece_s.at[0, d - 1], at_section(d)))
    send(piece_copy(s, z, c, piece_c.at[0], sibling))
    for d in (1, 2, 3):
        q = jnp.bitwise_xor(p, d)
        send(remote(images.at[q], xin.at[p], image_out.at[d - 1], image_in.at[p], at_sp(d)))

    for copy in arrivals[3:]:
        copy.wait()
    active = jnp.where(steps[...] > active_above, 1.0, 0.0)
    pulled = cotangent[...].astype(F32).reshape(half * half, ch) * (0.25 * active)
    up_rows[pl.ds(0, half * half, stride=2), :] = pulled
    up_rows[pl.ds(1, half * half, stride=2), :] = pulled

    for d in range(1, nsec):
        line_copy(lines_all.at[sec(d), z, c], d - 1, sibling).wait_recv()
    for d in range(1, nz):
        send(line_copy(lines_all.at[:, z, c], nsec - 2 + d, at_z(d)))
    for d in (4, 5, 6, 7):
        q = jnp.bitwise_xor(p, d)
        send(remote(images.at[q], xin.at[p], image_out.at[d - 1], image_in.at[p], at_sp(d)))
    for d in range(1, nz):
        piece_copy(s, zed(d), c, piece_z.at[d - 1], sibling).wait_recv()
        for e in range(1, nsec):
            send(piece_copy(s, zed(d), c, piece_s.at[d, e - 1], at_section(e)))
        send(piece_copy(s, zed(d), c, piece_c.at[d], sibling))
    for d in range(1, nz):
        line_copy(lines_all.at[:, zed(d), c], nsec - 2 + d, sibling).wait_recv()
    lines_last = nsec + nz - 2
    send(line_copy(lines_all.at[:, :, c], lines_last, sibling))

    def pass_on(e):
        for d in range(1, nsec):
            copy = piece_copy(sec(d), zed(e), c, piece_k.at[d, e], sibling)
            copy.wait_recv()
            send(copy)

    per = band // 2

    def take_image(d):
        q = jnp.bitwise_xor(p, d)
        if d:
            remote(images.at[q], xin.at[q], image_out.at[d - 1], image_in.at[q], sibling).wait_recv()
        block = xin[q].astype(F32).reshape(per, 2, side, ch)
        put_patches(patches.at[0], q * per, halves(block, ch), side, ch)

    for e in range(nz):
        pass_on(e)
        take_image(2 * e)
        take_image(2 * e + 1)
    line_copy(lines_all.at[:, :, 1 - c], lines_last, sibling).wait_recv()

    tags = labels[...]
    at = lax.broadcasted_iota(jnp.int32, tags.shape, 1)
    label = jnp.sum(jnp.where(at == p, tags, 0).astype(F32), axis=1, keepdims=True).astype(jnp.int32)
    width = nsec * nsp * TILE
    column = lax.broadcasted_iota(jnp.int32, (TILE, width), 1)
    picked = lax.broadcasted_iota(jnp.int32, (TILE, width), 0)
    device = jnp.right_shift(column, 4)
    entry = jnp.bitwise_and(column, TILE - 1)
    wanted = picked * count + label
    at_row = jnp.right_shift(device * 5, 1) + entry
    section = jnp.right_shift(column, (nsp * TILE).bit_length() - 1)
    chosen = (picked < 8) & (entry < 3) & (at_row == wanted)
    chosen |= (picked >= 8) & (picked < 12) & (section == picked - 8) & (entry >= 3) & (entry < 6)
    chosen |= (picked >= 12) & (section == picked - 12) & (entry >= 6) & (entry < 9)
    everything = lines_all[...].reshape(width, ch)
    rows_ref[...] = dot(jnp.where(chosen, 1.0, 0.0).astype(BF16), everything, NN)
    gains, biases = rows_ref[0:4], rows_ref[4:8]
    lengths = jnp.sqrt(rows_ref[12:16] + 1e-06)
    units = rows_ref[8:12] / lengths
    sigmas = jnp.sqrt(jnp.sum(units * units, axis=1, keepdims=True) + 1e-06)
    scales = gains / sigmas

    def kernel_of(j):
        parts = [pieces[j, b, e] for b in range(nz) for e in range(2)]
        return jnp.concatenate(parts, 0)

    chunks = 8
    step = half // chunks
    spans = [(i * step, pl.ds(i * step * side, step * side)) for i in range(chunks)]
    part = half // 4
    parts = [(i * part, pl.ds(i * part * side, part * side)) for i in range(4)]

    for j in range(KERNELS):
        for b in range(nz):
            piece_copy(j, b, 1 - c, piece_c.at[0], sibling).wait_recv()
        matrix = pair_weights(kernel_of(j))
        for pair, span in parts:
            raws[j, span] = dot(patch_rows(patches.at[j], pair, part), matrix, NN)
        back_weights[j] = pair_weights_back(kernel_of(j)).T
        scale, bias = twice(scales[j : j + 1]), twice(biases[j : j + 1])
        for pair, span in spans:
            value, slope = leaky_terms(raws[j, span] * scale + bias)
            slopes[j, span] = slope
            if j % 2 == 1:
                source = patches[j - 1, pair + 1 : pair + 1 + step, :, :, ch : 2 * ch]
                value = halves(source.astype(F32), ch) + value
            if j < KERNELS - 1:
                put_patches(patches.at[j + 1], pair, value, side, ch)
            else:
                pool_rows[span] = value[:, :ch] + value[:, ch:]
    pooled = pool_rows[pl.ds(0, half * half, stride=2), :] + pool_rows[pl.ds(1, half * half, stride=2), :]
    energy[...] = (pooled * (0.25 * active)).reshape(half, half, ch)

    def first_copy(j):
        return remote(dk.at[j, :, 1 - c], first.at[j], one_out.at[j], one_in.at[j], sibling)

    def second_copy(j, d):
        return remote(
            summed.at[j, zed(d)], second.at[j, d - 1], two_out.at[j, d - 1], two_in.at[j, d - 1], at_z(d)
        )

    def third_copy(j):
        d = jnp.maximum(jnp.bitwise_xor(s, j) - 1, 0)
        return remote(total.at[j], third.at[d], three_out.at[j], three_in.at[d], (j, p))

    def near_copy(j, k):
        return remote(
            summed.at[j, zed(3 - 2 * k)], near.at[j, k], near_out.at[j, k], near_in.at[j, k], at_z(1)
        )

    def wide_copy(j, k):
        d = jnp.maximum(jnp.bitwise_xor(s, j) - 1, 0)
        return remote(paired.at[j, k], wide.at[d, k], wide_out.at[j, k], wide_in.at[d, k], (j, p))

    def last_copy():
        return remote(joined, last, last_sems.at[0], last_sems.at[1], at_z(2))

    def first_sum(j):
        first_copy(j).wait_recv()
        summed[j] = (dk[j, :, c].astype(F32) + first[j].astype(F32)).astype(BF16)
        if modes[j] == "z":
            for d in reversed(range(1, nz)):
                send(second_copy(j, d))
        else:
            for k in range(2):
                send(near_copy(j, k))

    def near_sum(j):
        for k in range(2):
            near_copy(j, k).wait_recv()
            paired[j, k] = (summed[j, zed(2 - 2 * k)].astype(F32) + near[j, k].astype(F32)).astype(BF16)
            pl.when(s != j)(lambda: wide_copy(j, k).start())

    def wide_sum(k):
        value = paired[s, k].astype(F32)
        for d in range(1, nsec):
            remote(paired.at[0, k], wide.at[d - 1, k], wide_out.at[0, k], wide_in.at[d - 1, k], sibling).wait_recv()
            value += wide[d - 1, k].astype(F32)
        return value

    def second_sum(j):
        value = summed[j, z].astype(F32)
        for d in range(1, nz):
            second_copy(j, d).wait_recv()
            value += second[j, d - 1].astype(F32)
        total[j] = value.astype(BF16)
        pl.when(s != j)(lambda: third_copy(j).start())

    by_z = [j for j in range(KERNELS) if modes[j] == "z"]
    by_near = [j for j in range(KERNELS) if modes[j] != "z"]

    def is_one_of(kernels):
        found = s < 0
        for j in kernels:
            found = jnp.logical_or(found, s == j)
        return found

    gathered_sends = len(sends)
    lines = []

    def tile_copy(q, k, d, where):
        ref = tiles.at[q, c, k]
        return remote(ref, ref, tile_out.at[k, d - 1], tile_in.at[k, q], where)

    def tiles_copy(e):
        return remote(tiles.at[:, e], tiles.at[:, e], tile_out.at[0, nz - 1], tile_in.at[0, nz], sibling)

    def pixel_step(j):
        scale = twice(scales[j : j + 1])
        gain_sum = jnp.zeros((1, 2 * ch), F32)
        bias_sum = jnp.zeros((1, 2 * ch), F32)
        for pair, span in spans:
            upstream = twice(up_rows[span]) if j == KERNELS - 1 else slopes[j + 1, span]
            pre = upstream * slopes[j, span]
            gain_sum += jnp.sum(pre * raws[j, span], axis=0, keepdims=True)
            bias_sum += jnp.sum(pre, axis=0, keepdims=True)
            put_patches(grads.at[j % 2], pair, pre * scale, side, ch)
        sigma = sigmas[j : j + 1]
        gain_row = (gain_sum[:, :ch] + gain_sum[:, ch:]) / sigma
        lines.append(gain_row)
        lines.append(bias_sum[:, :ch] + bias_sum[:, ch:])
        lines.append(-gain_row * gains[j : j + 1] / sigma)

    def weight_step(j):
        inputs = patches[j, 1 : half + 1].reshape(2 * half * side, 3 * ch)
        centre = grads[j % 2].reshape(2 * half + 4, side, 3 * ch)[:, :, ch : 2 * ch]
        shifted = [centre[3 - a : 3 - a + 2 * half] for a in range(3)]
        shifted = jnp.concatenate(shifted, -1).reshape(2 * half * side, 3 * ch)
        grad = dot(inputs, shifted, TN)
        grad = jnp.concatenate([grad[:, a * ch : (a + 1) * ch] for a in range(3)], 0).astype(BF16)
        for b in range(nz):
            for e in range(2):
                at = (2 * b + e) * rows
                dk[j, b, e] = grad[at : at + rows]

    def input_step(j):
        for pair, span in parts:
            down = dot(patch_rows(grads.at[j % 2], pair, part), back_weights[j], NN)
            if j == 2:
                down = (down + twice(up_rows[span])).astype(BF16).astype(F32)
                raws[2, span] = down
            if j > 0:
                slopes[j, span] = down
            else:
                down = (down + raws[2, span]).astype(BF16)
                for i in range(part // per):
                    for e in range(2):
                        block = down[i * per * side : (i + 1) * per * side, e * ch : (e + 1) * ch]
                        back[pair // per + i, :, e] = block.reshape(per, side, ch)

    for j in reversed(range(KERNELS)):
        pixel_step(j)
        if j % 2 == 0:
            tile = jnp.zeros((8, ch), F32)
            for index, value in enumerate(lines):
                tile = jnp.where(line[:8] == index, value, tile)
            lines.clear()
            k = 1 - j // 2
            tiles[z, c, k] = tile
            for d in range(1, nz):
                send(tile_copy(z, k, d, at_z(d)))
        weight_step(j)
        send(first_copy(j))
        if j < KERNELS - 1:
            first_sum(j + 1)
        input_step(j)
    first_sum(0)

    own_back = pltpu.make_async_copy(back.at[p], returned.at[p], local.at[7])
    own_back.start()
    for d in range(1, nsp):
        q = jnp.bitwise_xor(p, d)
        send(remote(back.at[q], returned.at[p], back_out.at[d - 1], back_in.at[p], at_sp(d)))

    for j in sorted(by_z)[1:]:
        second_sum(j)
    for j in reversed(by_near):
        near_sum(j)
    def pass_joined():
        joined[...] = wide_sum(0).astype(BF16)
        last_copy().start()

    pl.when(is_one_of(by_near[1:]))(pass_joined)
    drain(gathered_sends)
    for d in range(1, nz):
        for k in range(2):
            tile_copy(zed(d), k, d, sibling).wait_recv()
    send(tiles_copy(c))
    tiles_copy(1 - c).wait_recv()
    spread = nsp * TILE
    column = lax.broadcasted_iota(jnp.int32, (24, spread), 1)
    row = lax.broadcasted_iota(jnp.int32, (24, spread), 0)
    entry = jnp.bitwise_and(column, TILE - 1)
    owner = jnp.right_shift(column, 4)
    tag = jnp.zeros((24, spread), jnp.int32)
    for q in range(nsp):
        tag = jnp.where(owner == q, tags[:, q : q + 1], tag)
    gathered = tiles[...].reshape(spread, ch)
    upper = row >= count
    kind = row - jnp.where(upper, count, 0)
    spot = row - 2 * count
    sigma_slot = jnp.where(spot < 2, jnp.where(spot == 0, 13, 10), jnp.where(spot == 2, 5, 2))
    for blk in range(nsec):
        slot = (8 if blk % 2 == 0 else 0) + blk // 2 + jnp.where(upper, 0, 3)
        chosen = (spot < 0) & (entry == slot) & (tag == kind)
        chosen |= (spot >= 0) & (entry == sigma_slot)
        tables[blk] = dot(jnp.where(chosen, 1.0, 0.0), gathered, NN, HIGHEST)
    for d in range(1, nsec):
        send(remote(tables.at[sec(d)], tables_in.at[d - 1], table_out_sem.at[d - 1], table_in_sem.at[d - 1], at_section(d)))
    pl.when(is_one_of(by_near[:1]))(pass_joined)

    second_sum(min(by_z))
    drain(len(sends))

    table = tables[s]
    for d in range(1, nsec):
        remote(tables.at[sec(d)], tables_in.at[d - 1], table_out_sem.at[d - 1], table_in_sem.at[d - 1], at_section(d)).wait_recv()
        table += tables_in[d - 1]
    table_out[...] = table

    mine = pieces[s, z, c].astype(F32)
    proj = jnp.sum(mine * vector, axis=1, keepdims=True)
    q_row = rows_ref[pl.ds(8 + s, 1)]
    length = jnp.sqrt(rows_ref[pl.ds(12 + s, 1)][:, 0:1] + 1e-06)
    unit = q_row / length
    sigma = jnp.sqrt(jnp.sum(unit * unit, axis=1, keepdims=True) + 1e-06)
    along = unit / sigma
    reach = jnp.sum(mine * along, axis=1, keepdims=True)
    crossing = jnp.sum(q_row * along, axis=1, keepdims=True)
    slope = (reach - proj * (crossing / (length * length))) / length
    dsigma = table_out[pl.ds(2 * count + s, 1)]
    dsigma = jnp.sum(dsigma, axis=1, keepdims=True)
    weight_out[...] = dsigma * ((proj / length) * along + slope * vector)

    @pl.when(is_one_of(by_z))
    def _():
        value = weight_out[...] + total[s].astype(F32)
        for d in range(1, nsec):
            remote(total.at[0], third.at[d - 1], three_out.at[0], three_in.at[d - 1], sibling).wait_recv()
            value += third[d - 1].astype(F32)
        weight_out[...] = value

    @pl.when(is_one_of(by_near))
    def _():
        value = weight_out[...] + wide_sum(1)
        last_copy().wait_recv()
        weight_out[...] = value + last[...].astype(F32)
        last_copy().wait_send()

    for d in range(1, nsp):
        q = jnp.bitwise_xor(p, d)
        remote(back.at[q], returned.at[q], back_out.at[d - 1], back_in.at[q], sibling).wait_recv()
    own_back.wait()
    for j in by_z:
        pl.when(s != j)(lambda j=j: third_copy(j).wait_send())
    for j in by_near:
        for k in range(2):
            pl.when(s != j)(lambda j=j, k=k: wide_copy(j, k).wait_send())


def finish_kernel(count, energy_in, returned, weight_in, table, energy, grad, weight, affine, wide, sems):
    copies = [
        pltpu.make_async_copy(energy_in, energy, sems.at[0]),
        pltpu.make_async_copy(weight_in, weight, sems.at[1]),
    ]
    for copy in copies:
        copy.start()
    for i in range(returned.shape[0]):
        wide[i] = returned[i].astype(F32)
        copies.append(pltpu.make_async_copy(wide.at[i], grad.at[i], sems.at[2 + i]))
        copies[-1].start()
    ch = table.shape[1]
    p = lax.axis_index("sp")
    start = 5 * p // 2
    block = table[pl.ds(start, 3)]
    odd = jnp.full((1, ch), p % 2, jnp.int32) == 1
    middle = ch // 2
    swapped = [jnp.concatenate([block[i : i + 1, middle:], block[i : i + 1, :middle]], 1) for i in range(3)]
    low = lax.broadcasted_iota(jnp.int32, (1, ch), 1) < middle
    later = [jnp.where(low, swapped[i], swapped[i + 1]) for i in range(2)]
    affine[pl.ds(0, ch)] = jnp.where(odd, later[0], block[0:1]).reshape(ch)
    affine[pl.ds(ch, ch)] = jnp.where(odd, later[1], block[1:2]).reshape(ch)
    affine[pl.ds(2 * ch, middle)] = jnp.where(odd, swapped[2], block[2:3])[:, :middle].reshape(middle)
    for copy in copies:
        copy.wait()


def whole_body(images, labels, chain_steps, conv_weights, class_affine, power_vectors, cotangent):
    nsec, nsp = lax.axis_size("section"), lax.axis_size("sp")
    nz = nsp // 2
    own, band, side, ch = images.shape
    half = side // 2
    rows = conv_weights.shape[0] // ch
    share = class_affine.shape[0]
    count = share * nsec * nsp // (2 * KERNELS * ch)
    anywhere = pl.BlockSpec(memory_space=pltpu.MemorySpace.HBM)
    vmem = pl.BlockSpec(memory_space=pltpu.VMEM)
    pixels = half * side
    dma = pltpu.SemaphoreType.DMA
    results = pl.pallas_call(
        partial(whole_kernel, nsec, nz, count, LANGEVIN_T, MODES),
        out_shape=[
            pltpu.VMEM((half, half, ch), F32),
            pltpu.VMEM((own, band // 2, 2, side, ch), BF16),
            pltpu.VMEM((rows, ch), F32),
            pltpu.VMEM((24, ch), F32),
        ],
        in_specs=[anywhere] * 7,
        out_specs=[vmem] * 4,
        scratch_shapes=[
            pltpu.VMEM(labels.shape[::-1], jnp.int32),
            pltpu.VMEM(chain_steps.shape, jnp.int32),
            pltpu.VMEM((rows, ch), F32),
            pltpu.VMEM((share,), F32),
            pltpu.VMEM(power_vectors.shape, F32),
            pltpu.VMEM((half, half, ch), BF16),
            pltpu.VMEM((nsec, nz, 2, rows, ch), BF16),
            pltpu.VMEM((nsec, nz, 2, TILE, ch), BF16),
            pltpu.VMEM((nsp, band, side, ch), BF16),
            pltpu.VMEM((KERNELS, half + 2, 2, side, 3 * ch), BF16),
            pltpu.VMEM((2, half + 2, 2, side, 3 * ch), BF16),
            pltpu.VMEM((KERNELS, 12 * ch, 2 * ch), BF16),
            pltpu.VMEM((KERNELS, pixels, 2 * ch), F32),
            pltpu.VMEM((KERNELS, pixels, 2 * ch), F32),
            pltpu.VMEM((pixels, ch), F32),
            pltpu.VMEM((pixels, ch), F32),
            pltpu.VMEM((TILE, ch), F32),
            pltpu.VMEM((KERNELS, nz, 2, rows, ch), BF16),
            pltpu.VMEM((KERNELS, nz, rows, ch), BF16),
            pltpu.VMEM((KERNELS, nz, rows, ch), BF16),
            pltpu.VMEM((KERNELS, nz - 1, rows, ch), BF16),
            pltpu.VMEM((KERNELS, rows, ch), BF16),
            pltpu.VMEM((nsec - 1, rows, ch), BF16),
            pltpu.VMEM((KERNELS, 2, rows, ch), BF16),
            pltpu.VMEM((KERNELS, 2, rows, ch), BF16),
            pltpu.VMEM((nsec - 1, 2, rows, ch), BF16),
            pltpu.VMEM((rows, ch), BF16),
            pltpu.VMEM((rows, ch), BF16),
            pltpu.VMEM((nsp, band // 2, 2, side, ch), BF16),
            pltpu.VMEM((nz, 2, 2, 8, ch), F32),
            pltpu.VMEM((nsec, 24, ch), F32),
            pltpu.VMEM((nsec - 1, 24, ch), F32),
            dma((8,)),
            dma((nsec, nz, 2)),
            dma((nz - 1,)),
            dma((nz, nsec - 1)),
            dma((nz,)),
            dma((nsec, nz)),
            dma((nsec + nz - 1,)),
            dma((nsec + nz - 1,)),
            dma((nsp - 1,)),
            dma((nsp,)),
            dma((KERNELS,)),
            dma((KERNELS,)),
            dma((KERNELS, nz - 1)),
            dma((KERNELS, nz - 1)),
            dma((KERNELS,)),
            dma((nsec - 1,)),
            dma((KERNELS, 2)),
            dma((KERNELS, 2)),
            dma((KERNELS, 2)),
            dma((nsec - 1, 2)),
            dma((2,)),
            dma((nsp - 1,)),
            dma((nsp,)),
            dma((2, nz)),
            dma((2, nz + 1)),
            dma((nsec - 1,)),
            dma((nsec - 1,)),
        ],
        compiler_params=pltpu.CompilerParams(
            collective_id=0, has_side_effects=True, vmem_limit_bytes=56 * 2**20
        ),
    )(
        images,
        labels.reshape(labels.shape[::-1]),
        chain_steps,
        conv_weights.reshape(rows, ch),
        class_affine,
        power_vectors,
        cotangent.reshape(half, half, ch),
    )
    energy, returned, weight_grad, affine_grad = pl.pallas_call(
        partial(finish_kernel, count),
        out_shape=[
            jax.ShapeDtypeStruct((half, half, ch), F32),
            jax.ShapeDtypeStruct((own, band // 2, 2, side, ch), F32),
            jax.ShapeDtypeStruct((rows, ch), F32),
            jax.ShapeDtypeStruct((share,), F32),
        ],
        in_specs=[vmem] * 4,
        out_specs=[anywhere] * 3 + [vmem],
        scratch_shapes=[pltpu.VMEM((own, band // 2, 2, side, ch), F32), dma((own + 2,))],
    )(*(pltpu.with_memory_space_constraint(r, pltpu.VMEM) for r in results))
    return (
        energy[None],
        returned.reshape(own, band, side, ch),
        weight_grad.reshape(-1),
        affine_grad,
    )


def body(images, labels, chain_steps, conv_weights, class_affine, power_vectors, cotangent):
    nsec, nsp = lax.axis_size("section"), lax.axis_size("sp")
    channels = images.shape[3]
    rows = conv_weights.shape[0] // channels
    fits = (
        nsec == KERNELS
        and nsp == 8
        and images.shape[0] == nsp
        and images.shape[1] * nsp == images.shape[2]
        and images.shape[1] % 2 == 0
        and chain_steps.shape == (1, 1)
        and rows % 16 == 0
        and class_affine.shape[0] * 2 == 5 * channels
    )
    chosen = whole_body if fits else general_body
    return chosen(
        images, labels, chain_steps, conv_weights, class_affine, power_vectors, cotangent
    )


def solution(mesh):
    in_specs = (
        P("section", "sp", None, None),
        P("section", None),
        P(("section", "sp"), None),
        P(("section", "sp")),
        P(("section", "sp")),
        P(),
        P(("section", "sp"), None, None, None),
    )
    out_specs = (
        P(("section", "sp"), None, None, None),
        P("section", "sp", None, None),
        P(("section", "sp")),
        P(("section", "sp")),
    )
    return jax.shard_map(body, mesh=mesh, in_specs=in_specs, out_specs=out_specs, check_vma=False)
```

```python
from functools import partial

import jax
import jax.numpy as jnp
from jax import lax
from jax.experimental import pallas as pl
from jax.experimental.pallas import tpu as pltpu
from jax.sharding import PartitionSpec as P

LANGEVIN_T = 40


HIGHEST = lax.Precision.HIGHEST


def extended_2(block, sides, width):
    for axis, dim in sides:
        count = lax.axis_size(axis)
        forward = [(i, i + 1) for i in range(count - 1)]
        backward = [(target, source) for source, target in forward]
        low = lax.ppermute(
            lax.slice_in_dim(block, block.shape[dim] - width, None, axis=dim), axis, forward
        )
        high = lax.ppermute(lax.slice_in_dim(block, 0, width, axis=dim), axis, backward)
        block = jnp.concatenate([low, block, high], axis=dim)
    return block


def leaky(value):
    return 0.2 * value + 0.8 * jax.nn.softplus(value)


def leaky_slope(value):
    return 0.2 + 0.8 * jax.nn.sigmoid(value)


def spectral(matrix, vector):
    forward = jnp.dot(matrix, vector, precision=HIGHEST)
    unit = forward / jnp.sqrt(jnp.sum(forward * forward) + 1e-06)
    backward = jnp.dot(unit, matrix, precision=HIGHEST)
    return jnp.sqrt(jnp.sum(backward * backward) + 1e-06)


def taps(padded, kernel):
    return lax.conv_general_dilated(
        padded,
        kernel,
        (1, 1),
        "VALID",
        dimension_numbers=("NHWC", "HWIO", "NHWC"),
        preferred_element_type=jnp.float32,
    )


def kernel_grad(padded, grad):
    result = lax.conv_general_dilated(
        padded,
        grad,
        (1, 1),
        "VALID",
        dimension_numbers=("CHWN", "IHWO", "NHWC"),
        preferred_element_type=jnp.float32,
    )
    return jnp.transpose(result, (1, 2, 0, 3))


def flipped(kernel):
    return jnp.transpose(jnp.flip(kernel, (0, 1)), (0, 1, 3, 2))


def trim_rims(extended, band, side):
    start = lax.axis_index("sp") * band
    keep_top = jnp.where(start % side == 0, 0.0, 1.0).astype(extended.dtype)
    keep_bottom = jnp.where((start + band) % side == 0, 0.0, 1.0).astype(extended.dtype)
    merged = jnp.concatenate(
        [extended[:, :1] * keep_top, extended[:, 1:-1], extended[:, -1:] * keep_bottom], axis=1
    )
    return jnp.pad(merged, ((0, 0), (0, 0), (1, 1), (0, 0)))


def rows_forward(values, band, side):
    extended = extended_2(values, (("sp", 1),), 1)
    return trim_rims(extended, band, side)


def rows_backward(values, band, side):
    extended = extended_2(values, (("sp", 1),), 1)
    return trim_rims(extended, band, side)


def pad_whole(values):
    return jnp.pad(values, ((0, 0), (1, 1), (1, 1), (0, 0)))


def affine_terms(upstream, raw, value, scale, gain, sigma):
    pre = upstream * leaky_slope(value)
    grad_raw = (pre * scale[:, None, None, :]).astype(jnp.bfloat16)
    grad_gain = jnp.sum(pre * raw, axis=(1, 2)) / sigma
    grad_bias = jnp.sum(pre, axis=(1, 2))
    grad_sigma = -jnp.sum(grad_gain * gain) / sigma
    return (grad_raw, grad_gain, grad_bias, grad_sigma)


def general_body(images, labels, chain_steps, conv_weights, class_affine, power_vectors, cotangent):
    channels = images.shape[3]
    band = images.shape[1]
    side = images.shape[2]
    half = side // 2
    across = labels.shape[1]
    groups = chain_steps.shape[0]
    gathered_w, gathered_a = (
        lax.all_gather(conv_weights.astype(jnp.bfloat16), ("section", "sp"), axis=0, tiled=True),
        lax.all_gather(class_affine.astype(jnp.bfloat16), ("section", "sp"), axis=0, tiled=True),
    )
    kernels = gathered_w.reshape(4, 3, 3, channels, channels)
    table = gathered_a.astype(jnp.float32).reshape(2, 4, -1, channels)
    count = table.shape[2]
    matrices = kernels.astype(jnp.float32).reshape(4, 9 * channels, channels)
    sigmas = [spectral(matrices[j], power_vectors[j]) for j in range(4)]
    kinds = jnp.arange(count)
    start = lax.axis_index("sp") * groups
    tags_second = lax.dynamic_slice_in_dim(labels, start, groups, 0).reshape(-1)
    onehot_second = (tags_second[:, None] == kinds[None, :]).astype(jnp.float32)
    active = (chain_steps.reshape(-1) > LANGEVIN_T).astype(jnp.float32)
    column = lax.axis_index("sp") * band // side
    picks = jnp.arange(across) == column
    tags_first = jnp.sum(jnp.where(picks[None, :], labels, 0), axis=1)
    onehot_first = (tags_first[:, None] == kinds[None, :]).astype(jnp.float32)
    pad_forward = partial(rows_forward, band=band, side=side)
    pad_backward = partial(rows_backward, band=band, side=side)
    gains_first = jnp.einsum("nk,jkc->jnc", onehot_first, table[0], precision=HIGHEST)
    biases_first = jnp.einsum("nk,jkc->jnc", onehot_first, table[1], precision=HIGHEST)
    gains_second = jnp.einsum("nk,jkc->jnc", onehot_second, table[0], precision=HIGHEST)
    biases_second = jnp.einsum("nk,jkc->jnc", onehot_second, table[1], precision=HIGHEST)
    scales = [
        gains_first[0] / sigmas[0],
        gains_first[1] / sigmas[1],
        gains_second[2] / sigmas[2],
        gains_second[3] / sigmas[3],
    ]
    input_pad = pad_forward(images)
    raw_zero = taps(input_pad, kernels[0])
    pre_zero = raw_zero * scales[0][:, None, None, :] + biases_first[0][:, None, None, :]
    hidden_zero = leaky(pre_zero).astype(jnp.bfloat16)
    hidden_pad = pad_forward(hidden_zero)
    raw_one = taps(hidden_pad, kernels[1])
    pre_one = raw_one * scales[1][:, None, None, :] + biases_first[1][:, None, None, :]
    first_out = images.astype(jnp.float32) + leaky(pre_one)
    moved = lax.all_to_all(
        first_out.astype(jnp.bfloat16), "sp", split_axis=0, concat_axis=1, tiled=True
    )
    whole = moved.reshape(groups * across, side, side, channels)
    whole_pad = pad_whole(whole)
    raw_two = taps(whole_pad, kernels[2])
    pre_two = raw_two * scales[2][:, None, None, :] + biases_second[2][:, None, None, :]
    hidden_two = leaky(pre_two).astype(jnp.bfloat16)
    hidden_two_pad = pad_whole(hidden_two)
    raw_three = taps(hidden_two_pad, kernels[3])
    pre_three = raw_three * scales[3][:, None, None, :] + biases_second[3][:, None, None, :]
    second_out = whole.astype(jnp.float32) + leaky(pre_three)
    pooled = (
        jnp.mean(second_out.reshape(-1, half, 2, half, 2, channels), axis=(2, 4))
        * active[:, None, None, None]
    )
    energy = pooled.reshape(groups, across * half, half, channels)
    upstream = (
        cotangent.astype(jnp.float32).reshape(-1, half, half, channels)
        * (0.25 * active)[:, None, None, None]
    )
    images_n = upstream.shape[0]
    grad_out = jnp.broadcast_to(
        upstream[:, :, None, :, None, :], (images_n, half, 2, half, 2, channels)
    ).reshape(images_n, side, side, channels)
    dz_three, dg_three, db_three, dsig_three = affine_terms(
        grad_out, raw_three, pre_three, scales[3], gains_second[3], sigmas[3]
    )
    kg_three = kernel_grad(hidden_two_pad, dz_three)
    grad_hidden = taps(pad_whole(dz_three), flipped(kernels[3]))
    dz_two, dg_two, db_two, dsig_two = affine_terms(
        grad_hidden, raw_two, pre_two, scales[2], gains_second[2], sigmas[2]
    )
    kg_two = kernel_grad(whole_pad, dz_two)
    grad_whole = grad_out + taps(pad_whole(dz_two), flipped(kernels[2]))
    back_rows = grad_whole.astype(jnp.bfloat16).reshape(groups, across * side, side, channels)
    returned = lax.all_to_all(back_rows, "sp", split_axis=1, concat_axis=0, tiled=True)
    grad_first = returned.astype(jnp.float32)
    dz_one, dg_one, db_one, dsig_one = affine_terms(
        grad_first, raw_one, pre_one, scales[1], gains_first[1], sigmas[1]
    )
    kg_one = kernel_grad(hidden_pad, dz_one)
    grad_hidden_first = taps(pad_backward(dz_one), flipped(kernels[1]))
    dz_zero, dg_zero, db_zero, dsig_zero = affine_terms(
        grad_hidden_first, raw_zero, pre_zero, scales[0], gains_first[0], sigmas[0]
    )
    kg_zero = kernel_grad(input_pad, dz_zero)
    local_grad = grad_first + taps(pad_backward(dz_zero), flipped(kernels[0]))
    conv_grads = [kg_zero, kg_one, kg_two, kg_three]
    sigma_grads = [dsig_zero, dsig_one, dsig_two, dsig_three]
    pieces = []
    for index in range(4):
        unused, pullback = jax.vjp(partial(spectral, vector=power_vectors[index]), matrices[index])
        pieces.append(
            conv_grads[index].reshape(9 * channels, channels) + pullback(sigma_grads[index])[0]
        )
    weight_total = jnp.stack(pieces).reshape(-1)
    gain_rows = [
        jnp.einsum("nk,nc->kc", onehot_first, dg_zero, precision=HIGHEST),
        jnp.einsum("nk,nc->kc", onehot_first, dg_one, precision=HIGHEST),
        jnp.einsum("nk,nc->kc", onehot_second, dg_two, precision=HIGHEST),
        jnp.einsum("nk,nc->kc", onehot_second, dg_three, precision=HIGHEST),
    ]
    bias_rows = [
        jnp.einsum("nk,nc->kc", onehot_first, db_zero, precision=HIGHEST),
        jnp.einsum("nk,nc->kc", onehot_first, db_one, precision=HIGHEST),
        jnp.einsum("nk,nc->kc", onehot_second, db_two, precision=HIGHEST),
        jnp.einsum("nk,nc->kc", onehot_second, db_three, precision=HIGHEST),
    ]
    affine_total = jnp.stack([jnp.stack(gain_rows), jnp.stack(bias_rows)]).reshape(-1)
    weight_grad, affine_grad = (
        lax.psum_scatter(weight_total, ("section", "sp"), scatter_dimension=0, tiled=True),
        lax.psum_scatter(affine_total, ("section", "sp"), scatter_dimension=0, tiled=True),
    )
    return (energy, local_grad, weight_grad, affine_grad)

F32 = jnp.float32
BF16 = jnp.bfloat16
MESH = pl.DeviceIdType.MESH
NN = (((1,), (0,)), ((), ()))
NT = (((1,), (1,)), ((), ()))
TN = (((0,), (0,)), ((), ()))
KERNELS = 4
MODES = ("z", "h", "h", "h")
TILE = 16


def dot(left, right, dims, precision=None):
    return lax.dot_general(left, right, dims, precision=precision, preferred_element_type=F32)


def twice(row):
    return jnp.concatenate([row, row], 1)


def beside(value, side):
    rows = value.shape[0]
    column = lax.broadcasted_iota(jnp.int32, (rows, 1), 0) % side
    left = jnp.where(column == 0, 0.0, pltpu.roll(value, 1, 0))
    right = jnp.where(column == side - 1, 0.0, pltpu.roll(value, rows - 1, 0))
    return (left, value, right)


def put_patches(ref, pair, value, side, ch):
    count = value.shape[0] // side
    rows = pl.ds(pair + 1, count)
    for b, part in enumerate(beside(value, side)):
        part = part.astype(BF16)
        for e in range(2):
            half = part[:, e * ch : (e + 1) * ch].reshape(count, side, ch)
            ref[rows, e, :, b * ch : (b + 1) * ch] = half


def patch_rows(ref, at, count):
    side, width = ref.shape[2], ref.shape[3]
    end = at + count
    parts = [ref[at:end, 1], ref[at + 1 : end + 1, 0], ref[at + 1 : end + 1, 1], ref[at + 2 : end + 2, 0]]
    return jnp.concatenate(parts, -1).reshape(count * side, 4 * width)


def pair_weights(kernel):
    rows = kernel.shape[0] // 3
    zero = jnp.zeros((rows, kernel.shape[1]), kernel.dtype)
    a, b, c = (kernel[i * rows : (i + 1) * rows] for i in range(3))
    pairs = ((a, zero), (b, a), (c, b), (zero, c))
    return jnp.concatenate([jnp.concatenate(pair, 1) for pair in pairs], 0)


def pair_weights_back(kernel):
    ch = kernel.shape[1]
    zero = jnp.zeros((ch, ch), kernel.dtype)
    blocks = []
    for e in range(2):
        row = []
        for r in range(4):
            for b in range(3):
                a = 2 - (r - e)
                tap = (a * 3 + 2 - b) * ch
                row.append(kernel[tap : tap + ch] if 0 <= a <= 2 else zero)
        blocks.append(jnp.concatenate(row, 1))
    return jnp.concatenate(blocks, 0)


def leaky_terms(value):
    small = jnp.exp(-jnp.abs(value))
    result = 0.2 * value + 0.8 * (jnp.maximum(value, 0.0) + jnp.log(1.0 + small))
    return result, 0.6 + 0.4 * jnp.tanh(0.5 * value)


def halves(pairs, ch):
    wide = jnp.concatenate([pairs[:, 0], pairs[:, 1]], -1)
    return wide.reshape(-1, 2 * ch)


def three(row):
    high = row.astype(BF16).astype(F32)
    middle = (row - high).astype(BF16).astype(F32)
    return (high, middle, row - high - middle)


def whole_kernel(
    nsec, nz, count, active_above, modes,
    images, labels_in, steps_in, weights_in, affine_in, vectors_in, cotangent_in,
    energy, returned, weight_out, table_out,
    labels, steps, weights, affine, vectors, cotangent,
    pieces, lines_all, xin, patches, grads, back_weights, raws, slopes, up_rows, pool_rows, rows_ref,
    dk, first, summed, second, total, third, near, paired, wide, joined, last, back, tiles, tables, tables_in,
    local, piece_in, piece_z, piece_s, piece_c, piece_k, line_out, line_in, image_out, image_in,
    one_out, one_in, two_out, two_in, three_out, three_in, near_out, near_in, wide_out, wide_in, last_sems,
    back_out, back_in, tile_out, tile_in, table_out_sem, table_in_sem,
):
    nsp = 2 * nz
    side, ch = images.shape[2], images.shape[3]
    band = images.shape[1]
    half = side // 2
    rows = weights.shape[0]
    s = lax.axis_index("section")
    p = lax.axis_index("sp")
    z = p // 2
    c = p % 2

    def sec(d):
        return jnp.bitwise_xor(s, d)

    def zed(d):
        return jnp.bitwise_xor(z, d)

    def remote(src, dst, out_sem, in_sem, where):
        return pltpu.make_async_remote_copy(
            src_ref=src, dst_ref=dst, send_sem=out_sem, recv_sem=in_sem,
            device_id=where, device_id_type=MESH,
        )

    sibling = (s, p + 1 - 2 * c)

    def at_section(d):
        return (sec(d), p)

    def at_z(d):
        return (s, 2 * zed(d) + c)

    def at_sp(d):
        return (s, jnp.bitwise_xor(p, d))

    barrier = pltpu.get_barrier_semaphore()
    for d in range(1, nsec):
        pl.semaphore_signal(barrier, inc=1, device_id=at_section(d), device_id_type=MESH)
    for d in range(1, nsp):
        pl.semaphore_signal(barrier, inc=1, device_id=at_sp(d), device_id_type=MESH)

    arrivals = [
        pltpu.make_async_copy(src, dst, local.at[i])
        for i, (src, dst) in enumerate((
            (weights_in, weights), (vectors_in, vectors), (affine_in, affine), (labels_in, labels),
            (steps_in, steps), (cotangent_in, cotangent), (images.at[p], xin.at[p]),
        ))
    ]
    for copy in arrivals:
        copy.start()

    patches[:, 0:1] = jnp.zeros_like(patches[:, 0:1])
    patches[:, half + 1 :] = jnp.zeros_like(patches[:, half + 1 :])
    grads[:, 0:1] = jnp.zeros_like(grads[:, 0:1])
    grads[:, half + 1 :] = jnp.zeros_like(grads[:, half + 1 :])

    for copy in arrivals[:3]:
        copy.wait()
    mine = weights[...].astype(BF16)
    pieces[s, z, c] = mine
    matrix = mine.astype(F32)
    vector = vectors[pl.ds(s, 1)]
    proj = jnp.sum(matrix * vector, axis=1, keepdims=True)
    crossed = jnp.sum(proj * matrix, axis=0, keepdims=True)
    norm = jnp.broadcast_to(jnp.sum(proj * proj, axis=0, keepdims=True), (1, ch))
    cuts = ((0, ch), (ch, ch), (2 * ch, ch // 2))
    flat = jnp.concatenate([affine[pl.ds(at, n)].reshape(1, n) for at, n in cuts], 1)
    flat = flat.astype(BF16).astype(F32)
    hollow = jnp.zeros((1, ch // 2), F32)
    even = [flat[:, 0:ch], flat[:, ch : 2 * ch], jnp.concatenate([flat[:, 2 * ch :], hollow], 1)]
    odd = [
        jnp.concatenate([hollow, flat[:, 0 : ch // 2]], 1),
        flat[:, ch // 2 : 3 * ch // 2],
        flat[:, 3 * ch // 2 :],
    ]
    is_odd = jnp.full((1, ch), c, jnp.int32) == 1
    lines = [jnp.where(is_odd, b, a) for a, b in zip(even, odd)] + [*three(crossed), *three(norm)]
    tile = jnp.zeros((TILE, ch), F32)
    line = lax.broadcasted_iota(jnp.int32, (TILE, ch), 0)
    for index, value in enumerate(lines):
        tile = jnp.where(line == index, value, tile)
    lines_all[s, z, c] = tile.astype(BF16)

    pl.semaphore_wait(barrier, nsec - 1 + nsp - 1)

    def piece_copy(a, b, e, out_sem, where):
        ref = pieces.at[a, b, e]
        return remote(ref, ref, out_sem, piece_in.at[a, b, e], where)

    def line_copy(ref, index, where):
        return remote(ref, ref, line_out.at[index], line_in.at[index], where)

    sends = []

    def send(copy):
        copy.start()
        sends.append(copy)

    for d in range(1, nsec):
        send(line_copy(lines_all.at[s, z, c], d - 1, at_section(d)))
    for d in range(1, nz):
        send(piece_copy(s, z, c, piece_z.at[d - 1], at_z(d)))
    for d in range(1, nsec):
        send(piece_copy(s, z, c, piece_s.at[0, d - 1], at_section(d)))
    send(piece_copy(s, z, c, piece_c.at[0], sibling))

    for copy in arrivals[3:]:
        copy.wait()
    active = jnp.where(steps[...] > active_above, 1.0, 0.0)
    pulled = cotangent[...].astype(F32).reshape(half * half, ch) * (0.25 * active)
    up_rows[pl.ds(0, half * half, stride=2), :] = pulled
    up_rows[pl.ds(1, half * half, stride=2), :] = pulled

    for d in range(1, nsec):
        line_copy(lines_all.at[sec(d), z, c], d - 1, sibling).wait_recv()
    for d in range(1, nz):
        send(line_copy(lines_all.at[:, z, c], nsec - 2 + d, at_z(d)))
    for d in range(1, nsp):
        q = jnp.bitwise_xor(p, d)
        send(remote(images.at[q], xin.at[p], image_out.at[d - 1], image_in.at[p], at_sp(d)))
    for d in range(1, nz):
        piece_copy(s, zed(d), c, piece_z.at[d - 1], sibling).wait_recv()
        for e in range(1, nsec):
            send(piece_copy(s, zed(d), c, piece_s.at[d, e - 1], at_section(e)))
        send(piece_copy(s, zed(d), c, piece_c.at[d], sibling))
    for d in range(1, nz):
        line_copy(lines_all.at[:, zed(d), c], nsec - 2 + d, sibling).wait_recv()
    lines_last = nsec + nz - 2
    send(line_copy(lines_all.at[:, :, c], lines_last, sibling))

    def pass_on(e):
        for d in range(1, nsec):
            copy = piece_copy(sec(d), zed(e), c, piece_k.at[d, e], sibling)
            copy.wait_recv()
            send(copy)

    per = band // 2

    def take_image(d):
        q = jnp.bitwise_xor(p, d)
        if d:
            remote(images.at[q], xin.at[q], image_out.at[d - 1], image_in.at[q], sibling).wait_recv()
        block = xin[q].astype(F32).reshape(per, 2, side, ch)
        put_patches(patches.at[0], q * per, halves(block, ch), side, ch)

    for e in range(nz):
        pass_on(e)
        take_image(2 * e)
        take_image(2 * e + 1)
    line_copy(lines_all.at[:, :, 1 - c], lines_last, sibling).wait_recv()

    tags = labels[...]
    at = lax.broadcasted_iota(jnp.int32, tags.shape, 1)
    label = jnp.sum(jnp.where(at == p, tags, 0).astype(F32), axis=1, keepdims=True).astype(jnp.int32)
    width = nsec * nsp * TILE
    column = lax.broadcasted_iota(jnp.int32, (TILE, width), 1)
    picked = lax.broadcasted_iota(jnp.int32, (TILE, width), 0)
    device = jnp.right_shift(column, 4)
    entry = jnp.bitwise_and(column, TILE - 1)
    wanted = picked * count + label
    at_row = jnp.right_shift(device * 5, 1) + entry
    section = jnp.right_shift(column, (nsp * TILE).bit_length() - 1)
    chosen = (picked < 8) & (entry < 3) & (at_row == wanted)
    chosen |= (picked >= 8) & (picked < 12) & (section == picked - 8) & (entry >= 3) & (entry < 6)
    chosen |= (picked >= 12) & (section == picked - 12) & (entry >= 6) & (entry < 9)
    everything = lines_all[...].reshape(width, ch)
    rows_ref[...] = dot(jnp.where(chosen, 1.0, 0.0).astype(BF16), everything, NN)
    gains, biases = rows_ref[0:4], rows_ref[4:8]
    lengths = jnp.sqrt(rows_ref[12:16] + 1e-06)
    units = rows_ref[8:12] / lengths
    sigmas = jnp.sqrt(jnp.sum(units * units, axis=1, keepdims=True) + 1e-06)
    scales = gains / sigmas

    def kernel_of(j):
        parts = [pieces[j, b, e] for b in range(nz) for e in range(2)]
        return jnp.concatenate(parts, 0)

    chunks = 8
    step = half // chunks
    spans = [(i * step, pl.ds(i * step * side, step * side)) for i in range(chunks)]
    part = half // 4
    parts = [(i * part, pl.ds(i * part * side, part * side)) for i in range(4)]

    for j in range(KERNELS):
        for b in range(nz):
            piece_copy(j, b, 1 - c, piece_c.at[0], sibling).wait_recv()
        matrix = pair_weights(kernel_of(j))
        for pair, span in parts:
            raws[j, span] = dot(patch_rows(patches.at[j], pair, part), matrix, NN)
        back_weights[j] = pair_weights_back(kernel_of(j)).T
        scale, bias = twice(scales[j : j + 1]), twice(biases[j : j + 1])
        for pair, span in spans:
            value, slope = leaky_terms(raws[j, span] * scale + bias)
            slopes[j, span] = slope
            if j % 2 == 1:
                source = patches[j - 1, pair + 1 : pair + 1 + step, :, :, ch : 2 * ch]
                value = halves(source.astype(F32), ch) + value
            if j < KERNELS - 1:
                put_patches(patches.at[j + 1], pair, value, side, ch)
            else:
                pool_rows[span] = value[:, :ch] + value[:, ch:]
    pooled = pool_rows[pl.ds(0, half * half, stride=2), :] + pool_rows[pl.ds(1, half * half, stride=2), :]
    energy[...] = (pooled * (0.25 * active)).reshape(half, half, ch)

    def first_copy(j):
        return remote(dk.at[j, :, 1 - c], first.at[j], one_out.at[j], one_in.at[j], sibling)

    def second_copy(j, d):
        return remote(
            summed.at[j, zed(d)], second.at[j, d - 1], two_out.at[j, d - 1], two_in.at[j, d - 1], at_z(d)
        )

    def third_copy(j):
        d = jnp.maximum(jnp.bitwise_xor(s, j) - 1, 0)
        return remote(total.at[j], third.at[d], three_out.at[j], three_in.at[d], (j, p))

    def near_copy(j, k):
        return remote(
            summed.at[j, zed(3 - 2 * k)], near.at[j, k], near_out.at[j, k], near_in.at[j, k], at_z(1)
        )

    def wide_copy(j, k):
        d = jnp.maximum(jnp.bitwise_xor(s, j) - 1, 0)
        return remote(paired.at[j, k], wide.at[d, k], wide_out.at[j, k], wide_in.at[d, k], (j, p))

    def last_copy():
        return remote(joined, last, last_sems.at[0], last_sems.at[1], at_z(2))

    def first_sum(j):
        first_copy(j).wait_recv()
        summed[j] = (dk[j, :, c].astype(F32) + first[j].astype(F32)).astype(BF16)
        if modes[j] == "z":
            for d in reversed(range(1, nz)):
                send(second_copy(j, d))
        else:
            for k in range(2):
                send(near_copy(j, k))

    def near_sum(j):
        for k in range(2):
            near_copy(j, k).wait_recv()
            paired[j, k] = (summed[j, zed(2 - 2 * k)].astype(F32) + near[j, k].astype(F32)).astype(BF16)
            pl.when(s != j)(lambda: wide_copy(j, k).start())

    def wide_sum(k):
        value = paired[s, k].astype(F32)
        for d in range(1, nsec):
            remote(paired.at[0, k], wide.at[d - 1, k], wide_out.at[0, k], wide_in.at[d - 1, k], sibling).wait_recv()
            value += wide[d - 1, k].astype(F32)
        return value

    def second_sum(j):
        value = summed[j, z].astype(F32)
        for d in range(1, nz):
            second_copy(j, d).wait_recv()
            value += second[j, d - 1].astype(F32)
        total[j] = value.astype(BF16)
        pl.when(s != j)(lambda: third_copy(j).start())

    by_z = [j for j in range(KERNELS) if modes[j] == "z"]
    by_near = [j for j in range(KERNELS) if modes[j] != "z"]

    def is_one_of(kernels):
        found = s < 0
        for j in kernels:
            found = jnp.logical_or(found, s == j)
        return found

    lines = []

    def tile_copy(q, k, d, where):
        ref = tiles.at[q, c, k]
        return remote(ref, ref, tile_out.at[k, d - 1], tile_in.at[k, q], where)

    def tiles_copy(e):
        return remote(tiles.at[:, e], tiles.at[:, e], tile_out.at[0, nz - 1], tile_in.at[0, nz], sibling)

    def pixel_step(j):
        scale = twice(scales[j : j + 1])
        gain_sum = jnp.zeros((1, 2 * ch), F32)
        bias_sum = jnp.zeros((1, 2 * ch), F32)
        for pair, span in spans:
            upstream = twice(up_rows[span]) if j == KERNELS - 1 else slopes[j + 1, span]
            pre = upstream * slopes[j, span]
            gain_sum += jnp.sum(pre * raws[j, span], axis=0, keepdims=True)
            bias_sum += jnp.sum(pre, axis=0, keepdims=True)
            put_patches(grads.at[j % 2], pair, pre * scale, side, ch)
        sigma = sigmas[j : j + 1]
        gain_row = (gain_sum[:, :ch] + gain_sum[:, ch:]) / sigma
        lines.append(gain_row)
        lines.append(bias_sum[:, :ch] + bias_sum[:, ch:])
        lines.append(-gain_row * gains[j : j + 1] / sigma)

    def weight_step(j):
        inputs = patches[j, 1 : half + 1].reshape(2 * half * side, 3 * ch)
        centre = grads[j % 2].reshape(2 * half + 4, side, 3 * ch)[:, :, ch : 2 * ch]
        shifted = [centre[3 - a : 3 - a + 2 * half] for a in range(3)]
        shifted = jnp.concatenate(shifted, -1).reshape(2 * half * side, 3 * ch)
        grad = dot(inputs, shifted, TN)
        grad = jnp.concatenate([grad[:, a * ch : (a + 1) * ch] for a in range(3)], 0).astype(BF16)
        for b in range(nz):
            for e in range(2):
                at = (2 * b + e) * rows
                dk[j, b, e] = grad[at : at + rows]

    def input_step(j):
        for pair, span in parts:
            down = dot(patch_rows(grads.at[j % 2], pair, part), back_weights[j], NN)
            if j == 2:
                down = (down + twice(up_rows[span])).astype(BF16).astype(F32)
                raws[2, span] = down
            if j > 0:
                slopes[j, span] = down
            else:
                down = (down + raws[2, span]).astype(BF16)
                for i in range(part // per):
                    for e in range(2):
                        block = down[i * per * side : (i + 1) * per * side, e * ch : (e + 1) * ch]
                        back[pair // per + i, :, e] = block.reshape(per, side, ch)

    for j in reversed(range(KERNELS)):
        pixel_step(j)
        if j % 2 == 0:
            tile = jnp.zeros((8, ch), F32)
            for index, value in enumerate(lines):
                tile = jnp.where(line[:8] == index, value, tile)
            lines.clear()
            k = 1 - j // 2
            tiles[z, c, k] = tile
            for d in range(1, nz):
                send(tile_copy(z, k, d, at_z(d)))
        weight_step(j)
        send(first_copy(j))
        if j < KERNELS - 1:
            first_sum(j + 1)
        input_step(j)
    first_sum(0)

    own_back = pltpu.make_async_copy(back.at[p], returned.at[p], local.at[7])
    own_back.start()
    for d in range(1, nsp):
        q = jnp.bitwise_xor(p, d)
        send(remote(back.at[q], returned.at[p], back_out.at[d - 1], back_in.at[p], at_sp(d)))

    for j in sorted(by_z)[1:]:
        second_sum(j)
    for j in reversed(by_near):
        near_sum(j)
    def pass_joined():
        joined[...] = wide_sum(0).astype(BF16)
        last_copy().start()

    pl.when(is_one_of(by_near[1:]))(pass_joined)
    mine = pieces[s, z, c].astype(F32)
    proj = jnp.sum(mine * vector, axis=1, keepdims=True)
    q_row = rows_ref[pl.ds(8 + s, 1)]
    length = jnp.sqrt(rows_ref[pl.ds(12 + s, 1)][:, 0:1] + 1e-06)
    unit = q_row / length
    sigma = jnp.sqrt(jnp.sum(unit * unit, axis=1, keepdims=True) + 1e-06)
    along = unit / sigma
    reach = jnp.sum(mine * along, axis=1, keepdims=True)
    crossing = jnp.sum(q_row * along, axis=1, keepdims=True)
    slope = (reach - proj * (crossing / (length * length))) / length
    weight_out[...] = (proj / length) * along + slope * vector

    for d in range(1, nz):
        for k in range(2):
            tile_copy(zed(d), k, d, sibling).wait_recv()
    send(tiles_copy(c))
    tiles_copy(1 - c).wait_recv()
    spread = nsp * TILE
    column = lax.broadcasted_iota(jnp.int32, (24, spread), 1)
    row = lax.broadcasted_iota(jnp.int32, (24, spread), 0)
    entry = jnp.bitwise_and(column, TILE - 1)
    owner = jnp.right_shift(column, 4)
    tag = jnp.zeros((24, spread), jnp.int32)
    for q in range(nsp):
        tag = jnp.where(owner == q, tags[:, q : q + 1], tag)
    gathered = tiles[...].reshape(spread, ch)
    upper = row >= count
    kind = row - jnp.where(upper, count, 0)
    spot = row - 2 * count
    sigma_slot = jnp.where(spot < 2, jnp.where(spot == 0, 13, 10), jnp.where(spot == 2, 5, 2))
    for blk in range(nsec):
        slot = (8 if blk % 2 == 0 else 0) + blk // 2 + jnp.where(upper, 0, 3)
        chosen = (spot < 0) & (entry == slot) & (tag == kind)
        chosen |= (spot >= 0) & (entry == sigma_slot)
        tables[blk] = dot(jnp.where(chosen, 1.0, 0.0), gathered, NN, HIGHEST)
    for d in range(1, nsec):
        send(remote(tables.at[sec(d)], tables_in.at[d - 1], table_out_sem.at[d - 1], table_in_sem.at[d - 1], at_section(d)))
    pl.when(is_one_of(by_near[:1]))(pass_joined)

    second_sum(min(by_z))

    table = tables[s]
    for d in range(1, nsec):
        remote(tables.at[sec(d)], tables_in.at[d - 1], table_out_sem.at[d - 1], table_in_sem.at[d - 1], at_section(d)).wait_recv()
        table += tables_in[d - 1]
    table_out[...] = table

    dsigma = table_out[pl.ds(2 * count + s, 1)]
    dsigma = jnp.sum(dsigma, axis=1, keepdims=True)
    weight_out[...] = dsigma * weight_out[...]

    @pl.when(is_one_of(by_z))
    def _():
        value = weight_out[...] + total[s].astype(F32)
        for d in range(1, nsec):
            remote(total.at[0], third.at[d - 1], three_out.at[0], three_in.at[d - 1], sibling).wait_recv()
            value += third[d - 1].astype(F32)
        weight_out[...] = value

    @pl.when(is_one_of(by_near))
    def _():
        value = weight_out[...] + wide_sum(1)
        last_copy().wait_recv()
        weight_out[...] = value + last[...].astype(F32)
        last_copy().wait_send()

    for d in range(1, nsp):
        q = jnp.bitwise_xor(p, d)
        remote(back.at[q], returned.at[q], back_out.at[d - 1], back_in.at[q], sibling).wait_recv()
    own_back.wait()
    for copy in sends:
        copy.wait_send()
    for j in by_z:
        pl.when(s != j)(lambda j=j: third_copy(j).wait_send())
    for j in by_near:
        for k in range(2):
            pl.when(s != j)(lambda j=j, k=k: wide_copy(j, k).wait_send())


def finish_kernel(count, energy_in, returned, weight_in, table, energy, grad, weight, affine, wide, sems):
    copies = [
        pltpu.make_async_copy(energy_in, energy, sems.at[0]),
        pltpu.make_async_copy(weight_in, weight, sems.at[1]),
    ]
    for copy in copies:
        copy.start()
    for i in range(returned.shape[0]):
        wide[i] = returned[i].astype(F32)
        copies.append(pltpu.make_async_copy(wide.at[i], grad.at[i], sems.at[2 + i]))
        copies[-1].start()
    ch = table.shape[1]
    p = lax.axis_index("sp")
    start = 5 * p // 2
    block = table[pl.ds(start, 3)]
    odd = jnp.full((1, ch), p % 2, jnp.int32) == 1
    middle = ch // 2
    swapped = [jnp.concatenate([block[i : i + 1, middle:], block[i : i + 1, :middle]], 1) for i in range(3)]
    low = lax.broadcasted_iota(jnp.int32, (1, ch), 1) < middle
    later = [jnp.where(low, swapped[i], swapped[i + 1]) for i in range(2)]
    affine[pl.ds(0, ch)] = jnp.where(odd, later[0], block[0:1]).reshape(ch)
    affine[pl.ds(ch, ch)] = jnp.where(odd, later[1], block[1:2]).reshape(ch)
    affine[pl.ds(2 * ch, middle)] = jnp.where(odd, swapped[2], block[2:3])[:, :middle].reshape(middle)
    for copy in copies:
        copy.wait()


def whole_body(images, labels, chain_steps, conv_weights, class_affine, power_vectors, cotangent):
    nsec, nsp = lax.axis_size("section"), lax.axis_size("sp")
    nz = nsp // 2
    own, band, side, ch = images.shape
    half = side // 2
    rows = conv_weights.shape[0] // ch
    share = class_affine.shape[0]
    count = share * nsec * nsp // (2 * KERNELS * ch)
    anywhere = pl.BlockSpec(memory_space=pltpu.MemorySpace.HBM)
    vmem = pl.BlockSpec(memory_space=pltpu.VMEM)
    pixels = half * side
    dma = pltpu.SemaphoreType.DMA
    results = pl.pallas_call(
        partial(whole_kernel, nsec, nz, count, LANGEVIN_T, MODES),
        out_shape=[
            pltpu.VMEM((half, half, ch), F32),
            pltpu.VMEM((own, band // 2, 2, side, ch), BF16),
            pltpu.VMEM((rows, ch), F32),
            pltpu.VMEM((24, ch), F32),
        ],
        in_specs=[anywhere] * 7,
        out_specs=[vmem] * 4,
        scratch_shapes=[
            pltpu.VMEM(labels.shape[::-1], jnp.int32),
            pltpu.VMEM(chain_steps.shape, jnp.int32),
            pltpu.VMEM((rows, ch), F32),
            pltpu.VMEM((share,), F32),
            pltpu.VMEM(power_vectors.shape, F32),
            pltpu.VMEM((half, half, ch), BF16),
            pltpu.VMEM((nsec, nz, 2, rows, ch), BF16),
            pltpu.VMEM((nsec, nz, 2, TILE, ch), BF16),
            pltpu.VMEM((nsp, band, side, ch), BF16),
            pltpu.VMEM((KERNELS, half + 2, 2, side, 3 * ch), BF16),
            pltpu.VMEM((2, half + 2, 2, side, 3 * ch), BF16),
            pltpu.VMEM((KERNELS, 12 * ch, 2 * ch), BF16),
            pltpu.VMEM((KERNELS, pixels, 2 * ch), F32),
            pltpu.VMEM((KERNELS, pixels, 2 * ch), F32),
            pltpu.VMEM((pixels, ch), F32),
            pltpu.VMEM((pixels, ch), F32),
            pltpu.VMEM((TILE, ch), F32),
            pltpu.VMEM((KERNELS, nz, 2, rows, ch), BF16),
            pltpu.VMEM((KERNELS, nz, rows, ch), BF16),
            pltpu.VMEM((KERNELS, nz, rows, ch), BF16),
            pltpu.VMEM((KERNELS, nz - 1, rows, ch), BF16),
            pltpu.VMEM((KERNELS, rows, ch), BF16),
            pltpu.VMEM((nsec - 1, rows, ch), BF16),
            pltpu.VMEM((KERNELS, 2, rows, ch), BF16),
            pltpu.VMEM((KERNELS, 2, rows, ch), BF16),
            pltpu.VMEM((nsec - 1, 2, rows, ch), BF16),
            pltpu.VMEM((rows, ch), BF16),
            pltpu.VMEM((rows, ch), BF16),
            pltpu.VMEM((nsp, band // 2, 2, side, ch), BF16),
            pltpu.VMEM((nz, 2, 2, 8, ch), F32),
            pltpu.VMEM((nsec, 24, ch), F32),
            pltpu.VMEM((nsec - 1, 24, ch), F32),
            dma((8,)),
            dma((nsec, nz, 2)),
            dma((nz - 1,)),
            dma((nz, nsec - 1)),
            dma((nz,)),
            dma((nsec, nz)),
            dma((nsec + nz - 1,)),
            dma((nsec + nz - 1,)),
            dma((nsp - 1,)),
            dma((nsp,)),
            dma((KERNELS,)),
            dma((KERNELS,)),
            dma((KERNELS, nz - 1)),
            dma((KERNELS, nz - 1)),
            dma((KERNELS,)),
            dma((nsec - 1,)),
            dma((KERNELS, 2)),
            dma((KERNELS, 2)),
            dma((KERNELS, 2)),
            dma((nsec - 1, 2)),
            dma((2,)),
            dma((nsp - 1,)),
            dma((nsp,)),
            dma((2, nz)),
            dma((2, nz + 1)),
            dma((nsec - 1,)),
            dma((nsec - 1,)),
        ],
        compiler_params=pltpu.CompilerParams(
            collective_id=0, has_side_effects=True, vmem_limit_bytes=56 * 2**20
        ),
    )(
        images,
        labels.reshape(labels.shape[::-1]),
        chain_steps,
        conv_weights.reshape(rows, ch),
        class_affine,
        power_vectors,
        cotangent.reshape(half, half, ch),
    )
    energy, returned, weight_grad, affine_grad = pl.pallas_call(
        partial(finish_kernel, count),
        out_shape=[
            jax.ShapeDtypeStruct((half, half, ch), F32),
            jax.ShapeDtypeStruct((own, band // 2, 2, side, ch), F32),
            jax.ShapeDtypeStruct((rows, ch), F32),
            jax.ShapeDtypeStruct((share,), F32),
        ],
        in_specs=[vmem] * 4,
        out_specs=[anywhere] * 3 + [vmem],
        scratch_shapes=[pltpu.VMEM((own, band // 2, 2, side, ch), F32), dma((own + 2,))],
    )(*(pltpu.with_memory_space_constraint(r, pltpu.VMEM) for r in results))
    return (
        energy[None],
        returned.reshape(own, band, side, ch),
        weight_grad.reshape(-1),
        affine_grad,
    )


def body(images, labels, chain_steps, conv_weights, class_affine, power_vectors, cotangent):
    nsec, nsp = lax.axis_size("section"), lax.axis_size("sp")
    channels = images.shape[3]
    rows = conv_weights.shape[0] // channels
    fits = (
        nsec == KERNELS
        and nsp == 8
        and images.shape[0] == nsp
        and images.shape[1] * nsp == images.shape[2]
        and images.shape[1] % 2 == 0
        and chain_steps.shape == (1, 1)
        and rows % 16 == 0
        and class_affine.shape[0] * 2 == 5 * channels
    )
    chosen = whole_body if fits else general_body
    return chosen(
        images, labels, chain_steps, conv_weights, class_affine, power_vectors, cotangent
    )


def solution(mesh):
    in_specs = (
        P("section", "sp", None, None),
        P("section", None),
        P(("section", "sp"), None),
        P(("section", "sp")),
        P(("section", "sp")),
        P(),
        P(("section", "sp"), None, None, None),
    )
    out_specs = (
        P(("section", "sp"), None, None, None),
        P("section", "sp", None, None),
        P(("section", "sp")),
        P(("section", "sp")),
    )
    return jax.shard_map(body, mesh=mesh, in_specs=in_specs, out_specs=out_specs, check_vma=False)
```

```python
from functools import partial

import jax
import jax.numpy as jnp
from jax import lax
from jax.experimental import pallas as pl
from jax.experimental.pallas import tpu as pltpu
from jax.sharding import PartitionSpec as P

LANGEVIN_T = 40


HIGHEST = lax.Precision.HIGHEST


def extended_2(block, sides, width):
    for axis, dim in sides:
        count = lax.axis_size(axis)
        forward = [(i, i + 1) for i in range(count - 1)]
        backward = [(target, source) for source, target in forward]
        low = lax.ppermute(
            lax.slice_in_dim(block, block.shape[dim] - width, None, axis=dim), axis, forward
        )
        high = lax.ppermute(lax.slice_in_dim(block, 0, width, axis=dim), axis, backward)
        block = jnp.concatenate([low, block, high], axis=dim)
    return block


def leaky(value):
    return 0.2 * value + 0.8 * jax.nn.softplus(value)


def leaky_slope(value):
    return 0.2 + 0.8 * jax.nn.sigmoid(value)


def spectral(matrix, vector):
    forward = jnp.dot(matrix, vector, precision=HIGHEST)
    unit = forward / jnp.sqrt(jnp.sum(forward * forward) + 1e-06)
    backward = jnp.dot(unit, matrix, precision=HIGHEST)
    return jnp.sqrt(jnp.sum(backward * backward) + 1e-06)


def taps(padded, kernel):
    return lax.conv_general_dilated(
        padded,
        kernel,
        (1, 1),
        "VALID",
        dimension_numbers=("NHWC", "HWIO", "NHWC"),
        preferred_element_type=jnp.float32,
    )


def kernel_grad(padded, grad):
    result = lax.conv_general_dilated(
        padded,
        grad,
        (1, 1),
        "VALID",
        dimension_numbers=("CHWN", "IHWO", "NHWC"),
        preferred_element_type=jnp.float32,
    )
    return jnp.transpose(result, (1, 2, 0, 3))


def flipped(kernel):
    return jnp.transpose(jnp.flip(kernel, (0, 1)), (0, 1, 3, 2))


def trim_rims(extended, band, side):
    start = lax.axis_index("sp") * band
    keep_top = jnp.where(start % side == 0, 0.0, 1.0).astype(extended.dtype)
    keep_bottom = jnp.where((start + band) % side == 0, 0.0, 1.0).astype(extended.dtype)
    merged = jnp.concatenate(
        [extended[:, :1] * keep_top, extended[:, 1:-1], extended[:, -1:] * keep_bottom], axis=1
    )
    return jnp.pad(merged, ((0, 0), (0, 0), (1, 1), (0, 0)))


def rows_forward(values, band, side):
    extended = extended_2(values, (("sp", 1),), 1)
    return trim_rims(extended, band, side)


def rows_backward(values, band, side):
    extended = extended_2(values, (("sp", 1),), 1)
    return trim_rims(extended, band, side)


def pad_whole(values):
    return jnp.pad(values, ((0, 0), (1, 1), (1, 1), (0, 0)))


def affine_terms(upstream, raw, value, scale, gain, sigma):
    pre = upstream * leaky_slope(value)
    grad_raw = (pre * scale[:, None, None, :]).astype(jnp.bfloat16)
    grad_gain = jnp.sum(pre * raw, axis=(1, 2)) / sigma
    grad_bias = jnp.sum(pre, axis=(1, 2))
    grad_sigma = -jnp.sum(grad_gain * gain) / sigma
    return (grad_raw, grad_gain, grad_bias, grad_sigma)


def general_body(images, labels, chain_steps, conv_weights, class_affine, power_vectors, cotangent):
    channels = images.shape[3]
    band = images.shape[1]
    side = images.shape[2]
    half = side // 2
    across = labels.shape[1]
    groups = chain_steps.shape[0]
    gathered_w, gathered_a = (
        lax.all_gather(conv_weights.astype(jnp.bfloat16), ("section", "sp"), axis=0, tiled=True),
        lax.all_gather(class_affine.astype(jnp.bfloat16), ("section", "sp"), axis=0, tiled=True),
    )
    kernels = gathered_w.reshape(4, 3, 3, channels, channels)
    table = gathered_a.astype(jnp.float32).reshape(2, 4, -1, channels)
    count = table.shape[2]
    matrices = kernels.astype(jnp.float32).reshape(4, 9 * channels, channels)
    sigmas = [spectral(matrices[j], power_vectors[j]) for j in range(4)]
    kinds = jnp.arange(count)
    start = lax.axis_index("sp") * groups
    tags_second = lax.dynamic_slice_in_dim(labels, start, groups, 0).reshape(-1)
    onehot_second = (tags_second[:, None] == kinds[None, :]).astype(jnp.float32)
    active = (chain_steps.reshape(-1) > LANGEVIN_T).astype(jnp.float32)
    column = lax.axis_index("sp") * band // side
    picks = jnp.arange(across) == column
    tags_first = jnp.sum(jnp.where(picks[None, :], labels, 0), axis=1)
    onehot_first = (tags_first[:, None] == kinds[None, :]).astype(jnp.float32)
    pad_forward = partial(rows_forward, band=band, side=side)
    pad_backward = partial(rows_backward, band=band, side=side)
    gains_first = jnp.einsum("nk,jkc->jnc", onehot_first, table[0], precision=HIGHEST)
    biases_first = jnp.einsum("nk,jkc->jnc", onehot_first, table[1], precision=HIGHEST)
    gains_second = jnp.einsum("nk,jkc->jnc", onehot_second, table[0], precision=HIGHEST)
    biases_second = jnp.einsum("nk,jkc->jnc", onehot_second, table[1], precision=HIGHEST)
    scales = [
        gains_first[0] / sigmas[0],
        gains_first[1] / sigmas[1],
        gains_second[2] / sigmas[2],
        gains_second[3] / sigmas[3],
    ]
    input_pad = pad_forward(images)
    raw_zero = taps(input_pad, kernels[0])
    pre_zero = raw_zero * scales[0][:, None, None, :] + biases_first[0][:, None, None, :]
    hidden_zero = leaky(pre_zero).astype(jnp.bfloat16)
    hidden_pad = pad_forward(hidden_zero)
    raw_one = taps(hidden_pad, kernels[1])
    pre_one = raw_one * scales[1][:, None, None, :] + biases_first[1][:, None, None, :]
    first_out = images.astype(jnp.float32) + leaky(pre_one)
    moved = lax.all_to_all(
        first_out.astype(jnp.bfloat16), "sp", split_axis=0, concat_axis=1, tiled=True
    )
    whole = moved.reshape(groups * across, side, side, channels)
    whole_pad = pad_whole(whole)
    raw_two = taps(whole_pad, kernels[2])
    pre_two = raw_two * scales[2][:, None, None, :] + biases_second[2][:, None, None, :]
    hidden_two = leaky(pre_two).astype(jnp.bfloat16)
    hidden_two_pad = pad_whole(hidden_two)
    raw_three = taps(hidden_two_pad, kernels[3])
    pre_three = raw_three * scales[3][:, None, None, :] + biases_second[3][:, None, None, :]
    second_out = whole.astype(jnp.float32) + leaky(pre_three)
    pooled = (
        jnp.mean(second_out.reshape(-1, half, 2, half, 2, channels), axis=(2, 4))
        * active[:, None, None, None]
    )
    energy = pooled.reshape(groups, across * half, half, channels)
    upstream = (
        cotangent.astype(jnp.float32).reshape(-1, half, half, channels)
        * (0.25 * active)[:, None, None, None]
    )
    images_n = upstream.shape[0]
    grad_out = jnp.broadcast_to(
        upstream[:, :, None, :, None, :], (images_n, half, 2, half, 2, channels)
    ).reshape(images_n, side, side, channels)
    dz_three, dg_three, db_three, dsig_three = affine_terms(
        grad_out, raw_three, pre_three, scales[3], gains_second[3], sigmas[3]
    )
    kg_three = kernel_grad(hidden_two_pad, dz_three)
    grad_hidden = taps(pad_whole(dz_three), flipped(kernels[3]))
    dz_two, dg_two, db_two, dsig_two = affine_terms(
        grad_hidden, raw_two, pre_two, scales[2], gains_second[2], sigmas[2]
    )
    kg_two = kernel_grad(whole_pad, dz_two)
    grad_whole = grad_out + taps(pad_whole(dz_two), flipped(kernels[2]))
    back_rows = grad_whole.astype(jnp.bfloat16).reshape(groups, across * side, side, channels)
    returned = lax.all_to_all(back_rows, "sp", split_axis=1, concat_axis=0, tiled=True)
    grad_first = returned.astype(jnp.float32)
    dz_one, dg_one, db_one, dsig_one = affine_terms(
        grad_first, raw_one, pre_one, scales[1], gains_first[1], sigmas[1]
    )
    kg_one = kernel_grad(hidden_pad, dz_one)
    grad_hidden_first = taps(pad_backward(dz_one), flipped(kernels[1]))
    dz_zero, dg_zero, db_zero, dsig_zero = affine_terms(
        grad_hidden_first, raw_zero, pre_zero, scales[0], gains_first[0], sigmas[0]
    )
    kg_zero = kernel_grad(input_pad, dz_zero)
    local_grad = grad_first + taps(pad_backward(dz_zero), flipped(kernels[0]))
    conv_grads = [kg_zero, kg_one, kg_two, kg_three]
    sigma_grads = [dsig_zero, dsig_one, dsig_two, dsig_three]
    pieces = []
    for index in range(4):
        unused, pullback = jax.vjp(partial(spectral, vector=power_vectors[index]), matrices[index])
        pieces.append(
            conv_grads[index].reshape(9 * channels, channels) + pullback(sigma_grads[index])[0]
        )
    weight_total = jnp.stack(pieces).reshape(-1)
    gain_rows = [
        jnp.einsum("nk,nc->kc", onehot_first, dg_zero, precision=HIGHEST),
        jnp.einsum("nk,nc->kc", onehot_first, dg_one, precision=HIGHEST),
        jnp.einsum("nk,nc->kc", onehot_second, dg_two, precision=HIGHEST),
        jnp.einsum("nk,nc->kc", onehot_second, dg_three, precision=HIGHEST),
    ]
    bias_rows = [
        jnp.einsum("nk,nc->kc", onehot_first, db_zero, precision=HIGHEST),
        jnp.einsum("nk,nc->kc", onehot_first, db_one, precision=HIGHEST),
        jnp.einsum("nk,nc->kc", onehot_second, db_two, precision=HIGHEST),
        jnp.einsum("nk,nc->kc", onehot_second, db_three, precision=HIGHEST),
    ]
    affine_total = jnp.stack([jnp.stack(gain_rows), jnp.stack(bias_rows)]).reshape(-1)
    weight_grad, affine_grad = (
        lax.psum_scatter(weight_total, ("section", "sp"), scatter_dimension=0, tiled=True),
        lax.psum_scatter(affine_total, ("section", "sp"), scatter_dimension=0, tiled=True),
    )
    return (energy, local_grad, weight_grad, affine_grad)

F32 = jnp.float32
BF16 = jnp.bfloat16
MESH = pl.DeviceIdType.MESH
NN = (((1,), (0,)), ((), ()))
NT = (((1,), (1,)), ((), ()))
TN = (((0,), (0,)), ((), ()))
KERNELS = 4
MODES = ("z", "h", "h", "h")
TILE = 16


def dot(left, right, dims, precision=None):
    return lax.dot_general(left, right, dims, precision=precision, preferred_element_type=F32)


def twice(row):
    return jnp.concatenate([row, row], 1)


def beside(value, side):
    rows = value.shape[0]
    column = lax.broadcasted_iota(jnp.int32, (rows, 1), 0) % side
    left = jnp.where(column == 0, 0.0, pltpu.roll(value, 1, 0))
    right = jnp.where(column == side - 1, 0.0, pltpu.roll(value, rows - 1, 0))
    return (left, value, right)


def put_patches(ref, pair, value, side, ch):
    count = value.shape[0] // side
    rows = pl.ds(pair + 1, count)
    for b, part in enumerate(beside(value, side)):
        part = part.astype(BF16)
        for e in range(2):
            half = part[:, e * ch : (e + 1) * ch].reshape(count, side, ch)
            ref[rows, e, :, b * ch : (b + 1) * ch] = half


def patch_rows(ref, at, count):
    side, width = ref.shape[2], ref.shape[3]
    end = at + count
    parts = [ref[at:end, 1], ref[at + 1 : end + 1, 0], ref[at + 1 : end + 1, 1], ref[at + 2 : end + 2, 0]]
    return jnp.concatenate(parts, -1).reshape(count * side, 4 * width)


def pair_weights(kernel):
    rows = kernel.shape[0] // 3
    zero = jnp.zeros((rows, kernel.shape[1]), kernel.dtype)
    a, b, c = (kernel[i * rows : (i + 1) * rows] for i in range(3))
    pairs = ((a, zero), (b, a), (c, b), (zero, c))
    return jnp.concatenate([jnp.concatenate(pair, 1) for pair in pairs], 0)


def pair_weights_back(kernel):
    ch = kernel.shape[1]
    zero = jnp.zeros((ch, ch), kernel.dtype)
    blocks = []
    for e in range(2):
        row = []
        for r in range(4):
            for b in range(3):
                a = 2 - (r - e)
                tap = (a * 3 + 2 - b) * ch
                row.append(kernel[tap : tap + ch] if 0 <= a <= 2 else zero)
        blocks.append(jnp.concatenate(row, 1))
    return jnp.concatenate(blocks, 0)


def leaky_terms(value):
    small = jnp.exp(-jnp.abs(value))
    result = 0.2 * value + 0.8 * (jnp.maximum(value, 0.0) + jnp.log(1.0 + small))
    return result, 0.6 + 0.4 * jnp.tanh(0.5 * value)


def halves(pairs, ch):
    wide = jnp.concatenate([pairs[:, 0], pairs[:, 1]], -1)
    return wide.reshape(-1, 2 * ch)


def three(row):
    high = row.astype(BF16).astype(F32)
    middle = (row - high).astype(BF16).astype(F32)
    return (high, middle, row - high - middle)


def whole_kernel(
    nsec, nz, count, active_above, modes,
    images, labels_in, steps_in, weights_in, affine_in, vectors_in, cotangent_in,
    energy, returned, weight_out, table_out,
    labels, steps, weights, affine, vectors, cotangent,
    pieces, lines_all, xin, patches, grads, back_weights, raws, slopes, up_rows, pool_rows, rows_ref,
    dk, first, summed, second, total, third, near, paired, wide, joined, last, back, tiles, tables, tables_in,
    local, piece_in, piece_z, piece_s, piece_c, piece_k, line_out, line_in, image_out, image_in,
    one_out, one_in, two_out, two_in, three_out, three_in, near_out, near_in, wide_out, wide_in, last_sems,
    back_out, back_in, tile_out, tile_in, table_out_sem, table_in_sem,
):
    nsp = 2 * nz
    side, ch = images.shape[2], images.shape[3]
    band = images.shape[1]
    half = side // 2
    rows = weights.shape[0]
    s = lax.axis_index("section")
    p = lax.axis_index("sp")
    z = p // 2
    c = p % 2

    def sec(d):
        return jnp.bitwise_xor(s, d)

    def zed(d):
        return jnp.bitwise_xor(z, d)

    def remote(src, dst, out_sem, in_sem, where):
        return pltpu.make_async_remote_copy(
            src_ref=src, dst_ref=dst, send_sem=out_sem, recv_sem=in_sem,
            device_id=where, device_id_type=MESH,
        )

    sibling = (s, p + 1 - 2 * c)

    def at_section(d):
        return (sec(d), p)

    def at_z(d):
        return (s, 2 * zed(d) + c)

    def at_sp(d):
        return (s, jnp.bitwise_xor(p, d))

    barrier = pltpu.get_barrier_semaphore()
    for d in range(1, nsec):
        pl.semaphore_signal(barrier, inc=1, device_id=at_section(d), device_id_type=MESH)
    for d in range(1, nsp):
        pl.semaphore_signal(barrier, inc=1, device_id=at_sp(d), device_id_type=MESH)

    arrivals = [
        pltpu.make_async_copy(src, dst, local.at[i])
        for i, (src, dst) in enumerate((
            (weights_in, weights), (vectors_in, vectors), (affine_in, affine), (labels_in, labels),
            (steps_in, steps), (cotangent_in, cotangent), (images.at[p], xin.at[p]),
        ))
    ]
    for copy in arrivals:
        copy.start()

    patches[:, 0:1] = jnp.zeros_like(patches[:, 0:1])
    patches[:, half + 1 :] = jnp.zeros_like(patches[:, half + 1 :])
    grads[:, 0:1] = jnp.zeros_like(grads[:, 0:1])
    grads[:, half + 1 :] = jnp.zeros_like(grads[:, half + 1 :])

    for copy in arrivals[:3]:
        copy.wait()
    mine = weights[...].astype(BF16)
    pieces[s, z, c] = mine
    matrix = mine.astype(F32)
    vector = vectors[pl.ds(s, 1)]
    proj = jnp.sum(matrix * vector, axis=1, keepdims=True)
    crossed = jnp.sum(proj * matrix, axis=0, keepdims=True)
    norm = jnp.broadcast_to(jnp.sum(proj * proj, axis=0, keepdims=True), (1, ch))
    cuts = ((0, ch), (ch, ch), (2 * ch, ch // 2))
    flat = jnp.concatenate([affine[pl.ds(at, n)].reshape(1, n) for at, n in cuts], 1)
    flat = flat.astype(BF16).astype(F32)
    hollow = jnp.zeros((1, ch // 2), F32)
    even = [flat[:, 0:ch], flat[:, ch : 2 * ch], jnp.concatenate([flat[:, 2 * ch :], hollow], 1)]
    odd = [
        jnp.concatenate([hollow, flat[:, 0 : ch // 2]], 1),
        flat[:, ch // 2 : 3 * ch // 2],
        flat[:, 3 * ch // 2 :],
    ]
    is_odd = jnp.full((1, ch), c, jnp.int32) == 1
    lines = [jnp.where(is_odd, b, a) for a, b in zip(even, odd)] + [*three(crossed), *three(norm)]
    tile = jnp.zeros((TILE, ch), F32)
    line = lax.broadcasted_iota(jnp.int32, (TILE, ch), 0)
    for index, value in enumerate(lines):
        tile = jnp.where(line == index, value, tile)
    lines_all[s, z, c] = tile.astype(BF16)

    pl.semaphore_wait(barrier, nsec - 1 + nsp - 1)

    def piece_copy(a, b, e, out_sem, where):
        ref = pieces.at[a, b, e]
        return remote(ref, ref, out_sem, piece_in.at[a, b, e], where)

    def line_copy(ref, index, where):
        return remote(ref, ref, line_out.at[index], line_in.at[index], where)

    sends = []

    def send(copy):
        copy.start()
        sends.append(copy)

    for d in range(1, nsec):
        send(line_copy(lines_all.at[s, z, c], d - 1, at_section(d)))
    for d in range(1, nz):
        send(piece_copy(s, z, c, piece_z.at[d - 1], at_z(d)))
    for d in range(1, nsec):
        send(piece_copy(s, z, c, piece_s.at[0, d - 1], at_section(d)))
    send(piece_copy(s, z, c, piece_c.at[0], sibling))

    for copy in arrivals[3:]:
        copy.wait()
    active = jnp.where(steps[...] > active_above, 1.0, 0.0)
    pulled = cotangent[...].astype(F32).reshape(half * half, ch) * (0.25 * active)
    up_rows[pl.ds(0, half * half, stride=2), :] = pulled
    up_rows[pl.ds(1, half * half, stride=2), :] = pulled

    for d in range(1, nsec):
        line_copy(lines_all.at[sec(d), z, c], d - 1, sibling).wait_recv()
    for d in range(1, nz):
        send(line_copy(lines_all.at[:, z, c], nsec - 2 + d, at_z(d)))
    for d in range(1, nsp):
        q = jnp.bitwise_xor(p, d)
        send(remote(images.at[q], xin.at[p], image_out.at[d - 1], image_in.at[p], at_sp(d)))
    for d in range(1, nz):
        piece_copy(s, zed(d), c, piece_z.at[d - 1], sibling).wait_recv()
        for e in range(1, nsec):
            send(piece_copy(s, zed(d), c, piece_s.at[d, e - 1], at_section(e)))
        send(piece_copy(s, zed(d), c, piece_c.at[d], sibling))
    for d in range(1, nz):
        line_copy(lines_all.at[:, zed(d), c], nsec - 2 + d, sibling).wait_recv()
    lines_last = nsec + nz - 2
    send(line_copy(lines_all.at[:, :, c], lines_last, sibling))

    def pass_on(e):
        for d in range(1, nsec):
            copy = piece_copy(sec(d), zed(e), c, piece_k.at[d, e], sibling)
            copy.wait_recv()
            send(copy)

    per = band // 2

    def take_image(d):
        q = jnp.bitwise_xor(p, d)
        if d:
            remote(images.at[q], xin.at[q], image_out.at[d - 1], image_in.at[q], sibling).wait_recv()
        block = xin[q].astype(F32).reshape(per, 2, side, ch)
        put_patches(patches.at[0], q * per, halves(block, ch), side, ch)

    for e in range(nz):
        pass_on(e)
        take_image(2 * e)
        take_image(2 * e + 1)
    line_copy(lines_all.at[:, :, 1 - c], lines_last, sibling).wait_recv()

    tags = labels[...]
    at = lax.broadcasted_iota(jnp.int32, tags.shape, 1)
    label = jnp.sum(jnp.where(at == p, tags, 0).astype(F32), axis=1, keepdims=True).astype(jnp.int32)
    width = nsec * nsp * TILE
    column = lax.broadcasted_iota(jnp.int32, (TILE, width), 1)
    picked = lax.broadcasted_iota(jnp.int32, (TILE, width), 0)
    device = jnp.right_shift(column, 4)
    entry = jnp.bitwise_and(column, TILE - 1)
    wanted = picked * count + label
    at_row = jnp.right_shift(device * 5, 1) + entry
    section = jnp.right_shift(column, (nsp * TILE).bit_length() - 1)
    chosen = (picked < 8) & (entry < 3) & (at_row == wanted)
    chosen |= (picked >= 8) & (picked < 12) & (section == picked - 8) & (entry >= 3) & (entry < 6)
    chosen |= (picked >= 12) & (section == picked - 12) & (entry >= 6) & (entry < 9)
    everything = lines_all[...].reshape(width, ch)
    rows_ref[...] = dot(jnp.where(chosen, 1.0, 0.0).astype(BF16), everything, NN)
    gains, biases = rows_ref[0:4], rows_ref[4:8]
    lengths = jnp.sqrt(rows_ref[12:16] + 1e-06)
    units = rows_ref[8:12] / lengths
    sigmas = jnp.sqrt(jnp.sum(units * units, axis=1, keepdims=True) + 1e-06)
    scales = gains / sigmas

    def kernel_of(j):
        parts = [pieces[j, b, e] for b in range(nz) for e in range(2)]
        return jnp.concatenate(parts, 0)

    chunks = 8
    step = half // chunks
    spans = [(i * step, pl.ds(i * step * side, step * side)) for i in range(chunks)]
    part = half // 4
    parts = [(i * part, pl.ds(i * part * side, part * side)) for i in range(4)]

    for j in range(KERNELS):
        for b in range(nz):
            piece_copy(j, b, 1 - c, piece_c.at[0], sibling).wait_recv()
        matrix = pair_weights(kernel_of(j))
        for pair, span in parts:
            raws[j, span] = dot(patch_rows(patches.at[j], pair, part), matrix, NN)
        back_weights[j] = pair_weights_back(kernel_of(j)).T
        scale, bias = twice(scales[j : j + 1]), twice(biases[j : j + 1])
        for pair, span in spans:
            value, slope = leaky_terms(raws[j, span] * scale + bias)
            slopes[j, span] = slope
            if j % 2 == 1:
                source = patches[j - 1, pair + 1 : pair + 1 + step, :, :, ch : 2 * ch]
                value = halves(source.astype(F32), ch) + value
            if j < KERNELS - 1:
                put_patches(patches.at[j + 1], pair, value, side, ch)
            else:
                pool_rows[span] = value[:, :ch] + value[:, ch:]
    pooled = pool_rows[pl.ds(0, half * half, stride=2), :] + pool_rows[pl.ds(1, half * half, stride=2), :]
    energy[...] = (pooled * (0.25 * active)).reshape(half, half, ch)

    def first_copy(j):
        return remote(dk.at[j, :, 1 - c], first.at[j], one_out.at[j], one_in.at[j], sibling)

    def second_copy(j, d):
        return remote(
            summed.at[j, zed(d)], second.at[j, d - 1], two_out.at[j, d - 1], two_in.at[j, d - 1], at_z(d)
        )

    def third_copy(j):
        d = jnp.maximum(jnp.bitwise_xor(s, j) - 1, 0)
        return remote(total.at[j], third.at[d], three_out.at[j], three_in.at[d], (j, p))

    def near_copy(j, k):
        return remote(
            summed.at[j, zed(3 - 2 * k)], near.at[j, k], near_out.at[j, k], near_in.at[j, k], at_z(1)
        )

    def wide_copy(j, k):
        d = jnp.maximum(jnp.bitwise_xor(s, j) - 1, 0)
        return remote(paired.at[j, k], wide.at[d, k], wide_out.at[j, k], wide_in.at[d, k], (j, p))

    def last_copy():
        return remote(joined, last, last_sems.at[0], last_sems.at[1], at_z(2))

    def first_sum(j):
        first_copy(j).wait_recv()
        summed[j] = (dk[j, :, c].astype(F32) + first[j].astype(F32)).astype(BF16)
        if modes[j] == "z":
            for d in reversed(range(1, nz)):
                send(second_copy(j, d))
        else:
            for k in range(2):
                send(near_copy(j, k))

    def near_sum(j):
        for k in range(2):
            near_copy(j, k).wait_recv()
            paired[j, k] = (summed[j, zed(2 - 2 * k)].astype(F32) + near[j, k].astype(F32)).astype(BF16)
            pl.when(s != j)(lambda: wide_copy(j, k).start())

    def wide_sum(k):
        value = paired[s, k].astype(F32)
        for d in range(1, nsec):
            remote(paired.at[0, k], wide.at[d - 1, k], wide_out.at[0, k], wide_in.at[d - 1, k], sibling).wait_recv()
            value += wide[d - 1, k].astype(F32)
        return value

    def second_sum(j):
        value = summed[j, z].astype(F32)
        for d in range(1, nz):
            second_copy(j, d).wait_recv()
            value += second[j, d - 1].astype(F32)
        total[j] = value.astype(BF16)
        pl.when(s != j)(lambda: third_copy(j).start())

    by_z = [j for j in range(KERNELS) if modes[j] == "z"]
    by_near = [j for j in range(KERNELS) if modes[j] != "z"]

    def is_one_of(kernels):
        found = s < 0
        for j in kernels:
            found = jnp.logical_or(found, s == j)
        return found

    lines = []

    def tile_copy(q, k, d, where):
        ref = tiles.at[q, c, k]
        return remote(ref, ref, tile_out.at[k, d - 1], tile_in.at[k, q], where)

    def tiles_copy(e):
        return remote(tiles.at[:, e], tiles.at[:, e], tile_out.at[0, nz - 1], tile_in.at[0, nz], sibling)

    def pixel_step(j):
        scale = twice(scales[j : j + 1])
        gain_sum = jnp.zeros((1, 2 * ch), F32)
        bias_sum = jnp.zeros((1, 2 * ch), F32)
        for pair, span in spans:
            upstream = twice(up_rows[span]) if j == KERNELS - 1 else slopes[j + 1, span]
            pre = upstream * slopes[j, span]
            gain_sum += jnp.sum(pre * raws[j, span], axis=0, keepdims=True)
            bias_sum += jnp.sum(pre, axis=0, keepdims=True)
            put_patches(grads.at[j % 2], pair, pre * scale, side, ch)
        sigma = sigmas[j : j + 1]
        gain_row = (gain_sum[:, :ch] + gain_sum[:, ch:]) / sigma
        lines.append(gain_row)
        lines.append(bias_sum[:, :ch] + bias_sum[:, ch:])
        lines.append(-gain_row * gains[j : j + 1] / sigma)

    def weight_step(j):
        inputs = patches[j, 1 : half + 1].reshape(2 * half * side, 3 * ch)
        centre = grads[j % 2].reshape(2 * half + 4, side, 3 * ch)[:, :, ch : 2 * ch]
        shifted = [centre[3 - a : 3 - a + 2 * half] for a in range(3)]
        shifted = jnp.concatenate(shifted, -1).reshape(2 * half * side, 3 * ch)
        grad = dot(inputs, shifted, TN)
        grad = jnp.concatenate([grad[:, a * ch : (a + 1) * ch] for a in range(3)], 0).astype(BF16)
        for b in range(nz):
            for e in range(2):
                at = (2 * b + e) * rows
                dk[j, b, e] = grad[at : at + rows]

    def input_step(j):
        for pair, span in parts:
            down = dot(patch_rows(grads.at[j % 2], pair, part), back_weights[j], NN)
            if j == 2:
                down = (down + twice(up_rows[span])).astype(BF16).astype(F32)
                raws[2, span] = down
            if j > 0:
                slopes[j, span] = down
            else:
                down = (down + raws[2, span]).astype(BF16)
                for i in range(part // per):
                    for e in range(2):
                        block = down[i * per * side : (i + 1) * per * side, e * ch : (e + 1) * ch]
                        back[pair // per + i, :, e] = block.reshape(per, side, ch)

    for j in reversed(range(KERNELS)):
        pixel_step(j)
        if j % 2 == 0:
            tile = jnp.zeros((8, ch), F32)
            for index, value in enumerate(lines):
                tile = jnp.where(line[:8] == index, value, tile)
            lines.clear()
            k = 1 - j // 2
            tiles[z, c, k] = tile
            for d in range(1, nz):
                send(tile_copy(z, k, d, at_z(d)))
        weight_step(j)
        send(first_copy(j))
        if j < KERNELS - 1:
            first_sum(j + 1)
        input_step(j)
    first_sum(0)

    own_back = pltpu.make_async_copy(back.at[p], returned.at[p], local.at[7])
    own_back.start()
    for d in range(1, nsp):
        q = jnp.bitwise_xor(p, d)
        send(remote(back.at[q], returned.at[p], back_out.at[d - 1], back_in.at[p], at_sp(d)))

    for j in sorted(by_z)[1:]:
        second_sum(j)
    for j in reversed(by_near):
        near_sum(j)
    def pass_joined():
        joined[...] = wide_sum(0).astype(BF16)
        last_copy().start()

    pl.when(is_one_of(by_near[1:]))(pass_joined)
    mine = pieces[s, z, c].astype(F32)
    proj = jnp.sum(mine * vector, axis=1, keepdims=True)
    q_row = rows_ref[pl.ds(8 + s, 1)]
    length = jnp.sqrt(rows_ref[pl.ds(12 + s, 1)][:, 0:1] + 1e-06)
    unit = q_row / length
    sigma = jnp.sqrt(jnp.sum(unit * unit, axis=1, keepdims=True) + 1e-06)
    along = unit / sigma
    reach = jnp.sum(mine * along, axis=1, keepdims=True)
    crossing = jnp.sum(q_row * along, axis=1, keepdims=True)
    slope = (reach - proj * (crossing / (length * length))) / length
    weight_out[...] = (proj / length) * along + slope * vector

    for d in range(1, nz):
        for k in range(2):
            tile_copy(zed(d), k, d, sibling).wait_recv()
    send(tiles_copy(c))
    tiles_copy(1 - c).wait_recv()
    spread = nsp * TILE
    column = lax.broadcasted_iota(jnp.int32, (24, spread), 1)
    row = lax.broadcasted_iota(jnp.int32, (24, spread), 0)
    entry = jnp.bitwise_and(column, TILE - 1)
    owner = jnp.right_shift(column, 4)
    tag = jnp.zeros((24, spread), jnp.int32)
    for q in range(nsp):
        tag = jnp.where(owner == q, tags[:, q : q + 1], tag)
    gathered = tiles[...].reshape(spread, ch)
    upper = row >= count
    kind = row - jnp.where(upper, count, 0)
    spot = row - 2 * count
    sigma_slot = jnp.where(spot < 2, jnp.where(spot == 0, 13, 10), jnp.where(spot == 2, 5, 2))
    picks = []
    for blk in range(nsec):
        slot = (8 if blk % 2 == 0 else 0) + blk // 2 + jnp.where(upper, 0, 3)
        chosen = (spot < 0) & (entry == slot) & (tag == kind)
        chosen |= (spot >= 0) & (entry == sigma_slot)
        picks.append(jnp.where(chosen, 1.0, 0.0))
    tables[...] = dot(jnp.concatenate(picks, 0), gathered, NN, HIGHEST).reshape(nsec, 24, ch)
    for d in range(1, nsec):
        send(remote(tables.at[sec(d)], tables_in.at[d - 1], table_out_sem.at[d - 1], table_in_sem.at[d - 1], at_section(d)))
    pl.when(is_one_of(by_near[:1]))(pass_joined)

    second_sum(min(by_z))

    table = tables[s]
    for d in range(1, nsec):
        remote(tables.at[sec(d)], tables_in.at[d - 1], table_out_sem.at[d - 1], table_in_sem.at[d - 1], at_section(d)).wait_recv()
        table += tables_in[d - 1]
    table_out[...] = table

    dsigma = table_out[pl.ds(2 * count + s, 1)]
    dsigma = jnp.sum(dsigma, axis=1, keepdims=True)
    weight_out[...] = dsigma * weight_out[...]

    @pl.when(is_one_of(by_z))
    def _():
        value = weight_out[...] + total[s].astype(F32)
        for d in range(1, nsec):
            remote(total.at[0], third.at[d - 1], three_out.at[0], three_in.at[d - 1], sibling).wait_recv()
            value += third[d - 1].astype(F32)
        weight_out[...] = value

    @pl.when(is_one_of(by_near))
    def _():
        value = weight_out[...] + wide_sum(1)
        last_copy().wait_recv()
        weight_out[...] = value + last[...].astype(F32)
        last_copy().wait_send()

    for d in range(1, nsp):
        q = jnp.bitwise_xor(p, d)
        remote(back.at[q], returned.at[q], back_out.at[d - 1], back_in.at[q], sibling).wait_recv()
    own_back.wait()
    for copy in sends:
        copy.wait_send()
    for j in by_z:
        pl.when(s != j)(lambda j=j: third_copy(j).wait_send())
    for j in by_near:
        for k in range(2):
            pl.when(s != j)(lambda j=j, k=k: wide_copy(j, k).wait_send())


def finish_kernel(count, energy_in, returned, weight_in, table, energy, grad, weight, affine, wide, sems):
    copies = [
        pltpu.make_async_copy(energy_in, energy, sems.at[0]),
        pltpu.make_async_copy(weight_in, weight, sems.at[1]),
    ]
    for copy in copies:
        copy.start()
    for i in range(returned.shape[0]):
        wide[i] = returned[i].astype(F32)
        copies.append(pltpu.make_async_copy(wide.at[i], grad.at[i], sems.at[2 + i]))
        copies[-1].start()
    ch = table.shape[1]
    p = lax.axis_index("sp")
    start = 5 * p // 2
    block = table[pl.ds(start, 3)]
    odd = jnp.full((1, ch), p % 2, jnp.int32) == 1
    middle = ch // 2
    swapped = [jnp.concatenate([block[i : i + 1, middle:], block[i : i + 1, :middle]], 1) for i in range(3)]
    low = lax.broadcasted_iota(jnp.int32, (1, ch), 1) < middle
    later = [jnp.where(low, swapped[i], swapped[i + 1]) for i in range(2)]
    affine[pl.ds(0, ch)] = jnp.where(odd, later[0], block[0:1]).reshape(ch)
    affine[pl.ds(ch, ch)] = jnp.where(odd, later[1], block[1:2]).reshape(ch)
    affine[pl.ds(2 * ch, middle)] = jnp.where(odd, swapped[2], block[2:3])[:, :middle].reshape(middle)
    for copy in copies:
        copy.wait()


def whole_body(images, labels, chain_steps, conv_weights, class_affine, power_vectors, cotangent):
    nsec, nsp = lax.axis_size("section"), lax.axis_size("sp")
    nz = nsp // 2
    own, band, side, ch = images.shape
    half = side // 2
    rows = conv_weights.shape[0] // ch
    share = class_affine.shape[0]
    count = share * nsec * nsp // (2 * KERNELS * ch)
    anywhere = pl.BlockSpec(memory_space=pltpu.MemorySpace.HBM)
    vmem = pl.BlockSpec(memory_space=pltpu.VMEM)
    pixels = half * side
    dma = pltpu.SemaphoreType.DMA
    results = pl.pallas_call(
        partial(whole_kernel, nsec, nz, count, LANGEVIN_T, MODES),
        out_shape=[
            pltpu.VMEM((half, half, ch), F32),
            pltpu.VMEM((own, band // 2, 2, side, ch), BF16),
            pltpu.VMEM((rows, ch), F32),
            pltpu.VMEM((24, ch), F32),
        ],
        in_specs=[anywhere] * 7,
        out_specs=[vmem] * 4,
        scratch_shapes=[
            pltpu.VMEM(labels.shape[::-1], jnp.int32),
            pltpu.VMEM(chain_steps.shape, jnp.int32),
            pltpu.VMEM((rows, ch), F32),
            pltpu.VMEM((share,), F32),
            pltpu.VMEM(power_vectors.shape, F32),
            pltpu.VMEM((half, half, ch), BF16),
            pltpu.VMEM((nsec, nz, 2, rows, ch), BF16),
            pltpu.VMEM((nsec, nz, 2, TILE, ch), BF16),
            pltpu.VMEM((nsp, band, side, ch), BF16),
            pltpu.VMEM((KERNELS, half + 2, 2, side, 3 * ch), BF16),
            pltpu.VMEM((2, half + 2, 2, side, 3 * ch), BF16),
            pltpu.VMEM((KERNELS, 12 * ch, 2 * ch), BF16),
            pltpu.VMEM((KERNELS, pixels, 2 * ch), F32),
            pltpu.VMEM((KERNELS, pixels, 2 * ch), F32),
            pltpu.VMEM((pixels, ch), F32),
            pltpu.VMEM((pixels, ch), F32),
            pltpu.VMEM((TILE, ch), F32),
            pltpu.VMEM((KERNELS, nz, 2, rows, ch), BF16),
            pltpu.VMEM((KERNELS, nz, rows, ch), BF16),
            pltpu.VMEM((KERNELS, nz, rows, ch), BF16),
            pltpu.VMEM((KERNELS, nz - 1, rows, ch), BF16),
            pltpu.VMEM((KERNELS, rows, ch), BF16),
            pltpu.VMEM((nsec - 1, rows, ch), BF16),
            pltpu.VMEM((KERNELS, 2, rows, ch), BF16),
            pltpu.VMEM((KERNELS, 2, rows, ch), BF16),
            pltpu.VMEM((nsec - 1, 2, rows, ch), BF16),
            pltpu.VMEM((rows, ch), BF16),
            pltpu.VMEM((rows, ch), BF16),
            pltpu.VMEM((nsp, band // 2, 2, side, ch), BF16),
            pltpu.VMEM((nz, 2, 2, 8, ch), F32),
            pltpu.VMEM((nsec, 24, ch), F32),
            pltpu.VMEM((nsec - 1, 24, ch), F32),
            dma((8,)),
            dma((nsec, nz, 2)),
            dma((nz - 1,)),
            dma((nz, nsec - 1)),
            dma((nz,)),
            dma((nsec, nz)),
            dma((nsec + nz - 1,)),
            dma((nsec + nz - 1,)),
            dma((nsp - 1,)),
            dma((nsp,)),
            dma((KERNELS,)),
            dma((KERNELS,)),
            dma((KERNELS, nz - 1)),
            dma((KERNELS, nz - 1)),
            dma((KERNELS,)),
            dma((nsec - 1,)),
            dma((KERNELS, 2)),
            dma((KERNELS, 2)),
            dma((KERNELS, 2)),
            dma((nsec - 1, 2)),
            dma((2,)),
            dma((nsp - 1,)),
            dma((nsp,)),
            dma((2, nz)),
            dma((2, nz + 1)),
            dma((nsec - 1,)),
            dma((nsec - 1,)),
        ],
        compiler_params=pltpu.CompilerParams(
            collective_id=0, has_side_effects=True, vmem_limit_bytes=56 * 2**20
        ),
    )(
        images,
        labels.reshape(labels.shape[::-1]),
        chain_steps,
        conv_weights.reshape(rows, ch),
        class_affine,
        power_vectors,
        cotangent.reshape(half, half, ch),
    )
    energy, returned, weight_grad, affine_grad = pl.pallas_call(
        partial(finish_kernel, count),
        out_shape=[
            jax.ShapeDtypeStruct((half, half, ch), F32),
            jax.ShapeDtypeStruct((own, band // 2, 2, side, ch), F32),
            jax.ShapeDtypeStruct((rows, ch), F32),
            jax.ShapeDtypeStruct((share,), F32),
        ],
        in_specs=[vmem] * 4,
        out_specs=[anywhere] * 3 + [vmem],
        scratch_shapes=[pltpu.VMEM((own, band // 2, 2, side, ch), F32), dma((own + 2,))],
    )(*(pltpu.with_memory_space_constraint(r, pltpu.VMEM) for r in results))
    return (
        energy[None],
        returned.reshape(own, band, side, ch),
        weight_grad.reshape(-1),
        affine_grad,
    )


def body(images, labels, chain_steps, conv_weights, class_affine, power_vectors, cotangent):
    nsec, nsp = lax.axis_size("section"), lax.axis_size("sp")
    channels = images.shape[3]
    rows = conv_weights.shape[0] // channels
    fits = (
        nsec == KERNELS
        and nsp == 8
        and images.shape[0] == nsp
        and images.shape[1] * nsp == images.shape[2]
        and images.shape[1] % 2 == 0
        and chain_steps.shape == (1, 1)
        and rows % 16 == 0
        and class_affine.shape[0] * 2 == 5 * channels
    )
    chosen = whole_body if fits else general_body
    return chosen(
        images, labels, chain_steps, conv_weights, class_affine, power_vectors, cotangent
    )


def solution(mesh):
    in_specs = (
        P("section", "sp", None, None),
        P("section", None),
        P(("section", "sp"), None),
        P(("section", "sp")),
        P(("section", "sp")),
        P(),
        P(("section", "sp"), None, None, None),
    )
    out_specs = (
        P(("section", "sp"), None, None, None),
        P("section", "sp", None, None),
        P(("section", "sp")),
        P(("section", "sp")),
    )
    return jax.shard_map(body, mesh=mesh, in_specs=in_specs, out_specs=out_specs, check_vma=False)
```
